512 devices in a mesh: grp: 16 (over x, y_hi, core), ep: 32 (over y_lo, z).
Axes of the slice: x: 4, y: 4 (y_hi: 2, y_lo: 2; y = y_hi * 2 + y_lo), z: 16, core: 2. Of those that a mesh axis runs over, the one named last changes fastest.
Arguments:
- tokens: bfloat16 [4096, 3584], P('ep', 'grp'), may hold values from -6 to 6
- routes: int32 [4096, 1], P('ep'), may hold values from 0 to 31; in each aligned block of 128 rows (0 to 127, 128 to 255, ...) at most 8 rows name the same one
- route_weights: float32 [4096, 1], P('ep'), may hold values from 0.2 to 1
- hot_experts: int32 [16], replicated, may hold values from 0 to 15, as said below
- w_gate: bfloat16 [16, 3584, 2048], P(None, 'ep', 'grp'), may hold values from -0.09375 to 0.09375
- w_up: bfloat16 [16, 3584, 2048], P(None, 'ep', 'grp'), may hold values from -0.09375 to 0.09375
- w_down: bfloat16 [16, 2048, 3584], P(None, 'grp', 'ep'), may hold values from -0.125 to 0.125
- cotangent: bfloat16 [4096, 3584], P('ep', 'grp'), may hold values from -3 to 3
Outputs:
- layer_output: bfloat16 [4096, 3584], P('ep', 'grp')
- grad_tokens: bfloat16 [4096, 3584], P('ep', 'grp')
- grad_gate: bfloat16 [16, 3584, 2048], P(None, 'ep', 'grp')
- grad_up: bfloat16 [16, 3584, 2048], P(None, 'ep', 'grp')
- grad_down: bfloat16 [16, 2048, 3584], P(None, 'grp', 'ep')
The draws below stay inside these ranges and needn't reach their ends.
Inputs may be any that keep to these rules, and one draw needn't show every extreme that they name: `routes`: each row names one slot. Among the rows of one device (aligned blocks of 128 rows) no slot is named by more than 8 rows. `hot_experts`: entry j is the expert held by slot 16 + j; an expert may appear several times.
All inputs are finite; a program needn't handle non-finite values.
Results may differ from the reference program's by a relative error of at most 0.02.
Values may be sent and summed in bfloat16 or wider, within the bound.
A program may use at most 64 MiB of HBM per device.

```python
import math
import jax
import jax.numpy as jnp
import numpy as np
from jax import lax

D = 3584
FF = 2048
TOP = 1
TOK_DEV = 128
TOKENS = 4096
EXPERTS = 16
REPLICAS = 16
CAP = 8
HID = 128
N_GRP = 16
N_EP = 32


def draw_hot_experts(key, part):
    values = jax.random.randint(key, (REPLICAS,), 0, EXPERTS, dtype=jnp.int32)
    values = values.at[0].set(EXPERTS - 1).at[1].set(0)
    return jax.random.permutation(jax.random.fold_in(key, 7), values)


def shard_levels(stream_key, shape, shards, low, high):
    level = 1.0
    for axis_at, blocks in shards:
        draws = jax.random.uniform(jax.random.fold_in(jax.random.fold_in(stream_key, 6), axis_at), (blocks,), jnp.float32, low / len(shards), high / len(shards))
        level = level * jnp.repeat(jnp.exp(draws), shape[axis_at] // blocks).reshape((-1,) + (1,) * (len(shape) - 1 - axis_at))
    return level


def shared_out(own_key, own, number, rows, number_of, top, limit, lean):
    ranking = jax.random.permutation(own_key, number_of)
    heavy_load, common = shares(number_of, rows * top, limit, lean, True), shares(number_of, rows * top, limit, lean, False)
    places = jnp.arange(number_of)

    def named(sizes, turn):
        used = int((sizes > 0).sum())
        fixed = max(1, used // 4)
        shifted = fixed + (places - fixed + turn * (used - fixed)) % max(1, number_of - fixed)
        return jnp.zeros((number_of,), jnp.int32).at[ranking[jnp.where(places < fixed, places, shifted)]].set(jnp.asarray(sizes, jnp.int32))

    sizes = jnp.where(number % 4 == 0, named(heavy_load, number // 4), named(common, number - number // 4 - 1))
    mixed = jax.random.permutation(jax.random.fold_in(own, 3), number_of)
    giver, sink = mixed[0:number_of // 2 * 2:2], mixed[1:number_of // 2 * 2:2]
    margin = jnp.minimum(sizes[giver] - 1, limit - sizes[sink]) // 2
    margin = jnp.where((giver == ranking[0]) | (sink == ranking[0]) | (sizes[sink] == 0), 0, jnp.maximum(margin, 0))
    shifted = jax.random.randint(jax.random.fold_in(own, 4), (number_of // 2,), 0, 1 << 20) % (margin + 1)
    sizes = sizes.at[giver].add(-shifted).at[sink].add(shifted)
    items = jnp.searchsorted(jnp.cumsum(sizes), jnp.arange(rows * top), side="right").astype(jnp.int32)
    table = items.reshape(top, rows).T
    table = table[jax.random.permutation(jax.random.fold_in(own, 1), rows)]
    turn = jax.random.randint(jax.random.fold_in(own, 2), (rows, 1), 0, top)
    return jnp.take_along_axis(table, (jnp.arange(top)[None, :] + turn) % top, axis=1)


def shares(amount, total, most, skew, full):
    portions = [(1 << 20) // math.isqrt(rank ** skew) + 1 for rank in range(1, amount + 1)]
    largest = most if full else min(most, max(-(-total // amount), total * portions[0] // sum(portions)))
    least = 1 if total - largest >= amount - 1 else 0
    holding, surplus = [largest] + [least] * (amount - 1), total - largest - least * (amount - 1)
    while surplus > 0:
        movable = [i for i in range(1, amount) if holding[i] < largest] or [i for i in range(1, amount) if holding[i] < most]
        whole, left = sum([portions[i] for i in movable]), surplus
        for i in movable:
            extra = min(most - holding[i], max(1, left * portions[i] // whole), surplus)
            holding[i] = holding[i] + extra
            surplus = surplus - extra
    return np.array(holding)


def scatter_about(stream_key, dims, scale, limit, split=(), held_as=jnp.bfloat16):
    factor_of = shard_levels(stream_key, dims, split, -0.22, 0.18) if split else 1.0
    result = jax.random.normal(stream_key, dims, jnp.float32) * scale * factor_of
    return jnp.minimum(jnp.maximum(result, -limit), limit).astype(held_as)


def setup_inputs(seed: int = 0) -> dict:
    streams_of = jax.random.split(jax.random.key(seed), 9)
    tokens = scatter_about(streams_of[0], (TOKENS, D), 1.0, 6.0, ((0, 32), (1, 16)))
    routes_keys = jax.random.split(jax.random.fold_in(streams_of[1], 1), TOKENS // TOK_DEV)
    routes_turns = jax.random.permutation(jax.random.fold_in(streams_of[1], 3), TOKENS // TOK_DEV)
    routes = jax.vmap(lambda own, number: shared_out(jax.random.fold_in(streams_of[1], 2), own, number, TOK_DEV, N_EP, TOP, CAP, 2))(routes_keys, routes_turns).reshape((TOKENS, TOP))
    route_weights = jnp.clip(0.2 + 0.8 * jax.random.uniform(streams_of[2], (TOKENS, TOP), jnp.float32) ** shard_levels(streams_of[2], (TOKENS, TOP), ((0, 32),), -0.2, 0.2), 0.2, 1.0)
    hot_experts = draw_hot_experts(jax.random.fold_in(streams_of[8], 71), 0)
    w_gate = scatter_about(streams_of[4], (EXPERTS, D, FF), D ** -0.5, 0.09375, ((1, 32), (2, 16)))
    w_up = scatter_about(streams_of[5], (EXPERTS, D, FF), D ** -0.5, 0.09375, ((1, 32), (2, 16)))
    w_down = scatter_about(streams_of[6], (EXPERTS, FF, D), FF ** -0.5, 0.125, ((1, 16), (2, 32)))
    cotangent = scatter_about(streams_of[7], (TOKENS, D), 0.5, 3.0, ((0, 32), (1, 16)))
    return dict(tokens=tokens, routes=routes, route_weights=route_weights, hot_experts=hot_experts, w_gate=w_gate, w_up=w_up, w_down=w_down, cotangent=cotangent)


def place_routes(slots_dev):
    onehot = (slots_dev[:, None] == jnp.arange(N_EP, dtype=jnp.int32)[None, :]).astype(jnp.int32)
    before = jnp.cumsum(onehot, axis=0) - onehot
    position = jnp.sum(before * onehot, axis=1).astype(jnp.int32)
    return (slots_dev * CAP + position).astype(jnp.int32)


def reference(tokens, routes, route_weights, hot_experts, w_gate, w_up, w_down, cotangent):
    flat_count = TOK_DEV * TOP
    pad_rows = N_EP * CAP
    slot_host = jnp.concatenate([jnp.arange(EXPERTS, dtype=jnp.int32), hot_experts.astype(jnp.int32)])
    dest = jax.vmap(place_routes)(routes.reshape(N_EP, flat_count).astype(jnp.int32))

    def source_of(target):
        base = jnp.full((pad_rows,), flat_count, jnp.int32)
        return base.at[target].set(jnp.arange(flat_count, dtype=jnp.int32))

    source = jax.vmap(source_of)(dest)
    dev_base = (jnp.arange(N_EP, dtype=jnp.int32) * flat_count)[:, None]
    global_src = jnp.where(source < flat_count, source + dev_base, TOKENS * TOP).astype(jnp.int32)
    global_src = global_src.reshape(N_EP, N_EP, CAP).transpose(1, 0, 2).reshape(N_EP, pad_rows)
    token_idx = (global_src // TOP).astype(jnp.int32)
    weight_ext = jnp.concatenate([route_weights.reshape(-1), jnp.zeros((1,), jnp.float32)])
    slot_weights = weight_ext[global_src]
    tokens_ext = jnp.concatenate([tokens, jnp.zeros((1, D), tokens.dtype)], axis=0)
    cot_ext = jnp.concatenate([cotangent, jnp.zeros((1, D), cotangent.dtype)], axis=0)

    def per_slot(carry, inputs):
        acc_gate, acc_up, acc_down = carry
        idx, wts, expert = inputs
        x_rows = tokens_ext[idx]
        dz_rows = (cot_ext[idx].astype(jnp.float32) * wts[:, None]).astype(jnp.bfloat16)
        wg = w_gate[expert]
        wu = w_up[expert]
        wd = w_down[expert]
        gate_pre = jnp.dot(x_rows, wg, preferred_element_type=jnp.float32)
        up_pre = jnp.dot(x_rows, wu, preferred_element_type=jnp.float32)
        sg = jax.nn.sigmoid(gate_pre)
        act = (gate_pre * sg * up_pre).astype(jnp.bfloat16)
        parts = jnp.einsum('rgh,ghd->rgd', act.reshape(pad_rows, N_GRP, HID).astype(jnp.float32),
                           wd.reshape(N_GRP, HID, D).astype(jnp.float32)).astype(jnp.bfloat16)
        out_sum = jnp.sum(parts.astype(jnp.float32), axis=1)
        act_grad = jnp.dot(dz_rows, wd.T, preferred_element_type=jnp.float32)
        gate_grad = (act_grad * up_pre * sg * (1.0 + gate_pre * (1.0 - sg))).astype(jnp.bfloat16)
        up_grad = (act_grad * gate_pre * sg).astype(jnp.bfloat16)
        tok_parts = jnp.einsum('rgh,dgh->rgd', gate_grad.reshape(pad_rows, N_GRP, HID).astype(jnp.float32),
                               wg.reshape(D, N_GRP, HID).astype(jnp.float32))
        tok_parts = tok_parts + jnp.einsum('rgh,dgh->rgd', up_grad.reshape(pad_rows, N_GRP, HID).astype(jnp.float32),
                                           wu.reshape(D, N_GRP, HID).astype(jnp.float32))
        tok_sum = jnp.sum(tok_parts.astype(jnp.bfloat16).astype(jnp.float32), axis=1)
        slot_gate = jnp.dot(x_rows.T, gate_grad, preferred_element_type=jnp.float32).astype(jnp.bfloat16)
        slot_up = jnp.dot(x_rows.T, up_grad, preferred_element_type=jnp.float32).astype(jnp.bfloat16)
        slot_down = jnp.dot(act.T, dz_rows, preferred_element_type=jnp.float32).astype(jnp.bfloat16)
        acc_gate = acc_gate.at[expert].add(slot_gate.astype(jnp.float32))
        acc_up = acc_up.at[expert].add(slot_up.astype(jnp.float32))
        acc_down = acc_down.at[expert].add(slot_down.astype(jnp.float32))
        return (acc_gate, acc_up, acc_down), (out_sum, tok_sum)

    init = (jnp.zeros((EXPERTS, D, FF), jnp.float32), jnp.zeros((EXPERTS, D, FF), jnp.float32),
            jnp.zeros((EXPERTS, FF, D), jnp.float32))
    (acc_gate, acc_up, acc_down), (out_all, tok_all) = lax.scan(per_slot, init, (token_idx, slot_weights, slot_host))
    slot_of = dest // CAP
    pos_of = dest % CAP
    flat_row = (slot_of * pad_rows + jnp.arange(N_EP, dtype=jnp.int32)[:, None] * CAP + pos_of).reshape(-1)
    out_routes = out_all.reshape(N_EP * pad_rows, D)[flat_row].reshape(TOKENS, TOP, D)
    tok_routes = tok_all.reshape(N_EP * pad_rows, D)[flat_row].reshape(TOKENS, TOP, D)
    layer_output = jnp.sum(route_weights[:, :, None] * out_routes, axis=1).astype(jnp.bfloat16)
    grad_tokens = jnp.sum(tok_routes, axis=1).astype(jnp.bfloat16)
    return (layer_output, grad_tokens, acc_gate.astype(jnp.bfloat16), acc_up.astype(jnp.bfloat16),
            acc_down.astype(jnp.bfloat16))
```

```python
import functools

import jax
import jax.numpy as jnp
from jax import lax
from jax.experimental import pallas as pl
from jax.experimental.pallas import tpu as pltpu
from jax.sharding import PartitionSpec as P

MESH = pl.DeviceIdType.MESH
BF = jnp.bfloat16
F32 = jnp.float32
NX, NY, NZ, NEP, NGRP = 4, 2, 16, 32, 16
LAST = (((1,), (1,)), ((), ()))
FIRST = (((0,), (0,)), ((), ()))


def mm(a, b, dims=(((1,), (0,)), ((), ()))):
    return lax.dot_general(a, b, dims, preferred_element_type=F32)


def body(
    tok_ref, routes_ref, rw_ref, hot_ref, wg_ref, wu_ref, wd_ref, cot_ref,
    out_ref, gtok_ref, gg_ref, gu_ref, gd_ref,
    src, meta, a1r, xb, er, et, wall, xe, se, pa, pb, ya, ra, rb, yb,
    ha, hb, he, qq, rc, rfar, rx, ry, fin, b1r, b2r, tot, go,
    w_sem, o_sem, a1_s, a1_q, m_s, m_q, a2_s, a2_q, g3_s, g3_q,
    ya_s, ya_q, ra_s, ra_q, rb_s, rb_q, yb_s, yb_q,
    hy_s, hy_q, ga_s, ga_q, gb_s, gb_q, gy_s, gy_q,
    c5_s, c5_q, f5_s, f5_q, x5_s, x5_q, y5_s, y5_q, b1_s, b1_q, b2_s, b2_q,
):
    g = lax.axis_index("grp")
    p = lax.axis_index("ep")
    x, yh, c = g // 4, (g // 2) % 2, g % 2
    y, z = p // NZ, p % NZ
    zr, zl = y * NZ + (z + 1) % NZ, y * NZ + (z + NZ - 1) % NZ
    py = (1 - y) * NZ + z
    gi = lambda xx, hh, cc: xx * 4 + hh * 2 + cc
    xr, xl = (x + 1) % NX, (x + 3) % NX
    gr, gl = gi(xr, yh, c), gi(xl, yh, c)
    gy, gc = gi(x, 1 - yh, c), gi(x, yh, 1 - c)

    def put(s, d, ss, rs, **dev):
        return pltpu.make_async_remote_copy(
            src_ref=s, dst_ref=d, send_sem=ss, recv_sem=rs, device_id=dev, device_id_type=MESH
        )

    w_in = [
        pltpu.make_async_copy(r, wall.at[:, pl.ds(0, 112), pl.ds(128 * i, 128)], w_sem.at[i])
        for i, r in enumerate((wg_ref, wu_ref, wd_ref))
    ]
    for cp in w_in:
        cp.start()

    barrier = pltpu.get_barrier_semaphore()

    def hello_g(i, _):
        pl.semaphore_signal(barrier, inc=1, device_id={"grp": (g + i) % NGRP}, device_id_type=MESH)
        return 0

    def hello_e(i, _):
        pl.semaphore_signal(barrier, inc=1, device_id={"ep": (p + i) % NEP}, device_id_type=MESH)
        return 0

    lax.fori_loop(1, NGRP, hello_g, 0)
    lax.fori_loop(1, NEP, hello_e, 0)

    slot_row = routes_ref[...]
    rw_row = rw_ref[...]
    dz = (cot_ref[...].astype(F32) * rw_row).astype(BF)
    for h in range(2):
        src[0:7, h] = tok_ref[h * 112 : (h + 1) * 112, :].reshape(7, 16, 128)
        src[8:15, h] = dz[h * 112 : (h + 1) * 112, :].reshape(7, 16, 128)
    src[7] = jnp.zeros((2, 16, 128), BF)
    src[15] = jnp.zeros((2, 16, 128), BF)
    wall[:, 112:128, :] = jnp.zeros((16, 16, 384), BF)

    oh = jnp.where(lax.broadcasted_iota(jnp.int32, (NEP, 128), 0) == slot_row, 1.0, 0.0).astype(F32)
    upper = jnp.where(
        lax.broadcasted_iota(jnp.int32, (128, 128), 0) < lax.broadcasted_iota(jnp.int32, (128, 128), 1), 1.0, 0.0
    ).astype(BF)
    before = mm(oh.astype(BF), upper)
    pos_row = jnp.sum(oh * before, axis=0, keepdims=True)
    row_id = lax.broadcasted_iota(jnp.int32, (16, 128), 0)
    mrows = jnp.where(row_id == 0, slot_row.astype(F32), jnp.where(row_id == 1, pos_row, 0.0))
    meta[p] = mrows.astype(BF)

    pl.semaphore_wait(barrier, NGRP + NEP - 2)

    a1 = lambda i, t: put(src.at[t], a1r.at[g], a1_s.at[i], a1_q.at[i], grp=t)
    mt = lambda i, t: put(meta.at[p], meta.at[p], m_s.at[i], m_q.at[i], ep=t)
    a2 = lambda i, t: put(a1r.at[t // 2, t % 2], xb.at[g, p], a2_s.at[i], a2_q.at[i], ep=t)

    def loop(lo, hi, f):
        def step(i, _):
            f(i)
            return 0

        lax.fori_loop(lo, hi, step, 0)

    loop(1, NGRP, lambda i: a1(i, (g + i) % NGRP).start())
    loop(1, NEP, lambda i: mt(i, (p + i) % NEP).start())
    a1r[g] = src[g]

    def a1_wait(i):
        f = (g + NGRP - i) % NGRP
        put(src.at[f], a1r.at[f], a1_s.at[i], a1_q.at[i], grp=f).wait_recv()

    loop(1, NGRP, a1_wait)
    loop(1, NEP, lambda i: a2(i, (p + i) % NEP).start())
    xb[g, p] = a1r[p // 2, p % 2]

    def m_wait(i):
        f = (p + NEP - i) % NEP
        put(meta.at[p], meta.at[f], m_s.at[i], m_q.at[i], ep=f).wait_recv()

    loop(1, NEP, m_wait)

    def build(q):
        m0 = meta[2 * q].astype(F32)
        m1 = meta[2 * q + 1].astype(F32)
        d0 = m0[0:1, :] * 16.0 + m0[1:2, :]
        d1 = m1[0:1, :] * 16.0 + m1[1:2, :] + 8.0
        row = jnp.concatenate([d0, d1], axis=1)
        irow = row.astype(jnp.int32)
        er[q] = jnp.where(
            lax.broadcasted_iota(jnp.int32, (512, 256), 0) == irow, 1.0, 0.0
        ).astype(BF)
        col = jnp.transpose(jnp.broadcast_to(row, (128, 256))).astype(jnp.int32)
        for b in range(4):
            et[q, :, 128 * b : 128 * (b + 1)] = jnp.where(
                lax.broadcasted_iota(jnp.int32, (256, 128), 1) + 128 * b == col, 1.0, 0.0
            ).astype(BF)

    def a2_wait(i):
        f = (p + NEP - i) % NEP
        put(a1r.at[0, 0], xb.at[g, f], a2_s.at[i], a2_q.at[i], ep=f).wait_recv()

    loop(0, 4, build)
    loop(1, NEP, a2_wait)

    def g3(chunk, i, t):
        return put(xb.at[chunk], xb.at[chunk], g3_s.at[i], g3_q.at[i], grp=t)

    g3(g, 0, gy).start()
    g3(g, 1 + yh, gr).start()
    g3(g, 3 + yh, gl).start()
    g3(g, 7 + yh, gc).start()
    loop(4, 8, build)
    g3(gy, 0, gy).wait_recv()
    g3(gy, 1 + (1 - yh), gr).start()
    g3(gy, 3 + (1 - yh), gl).start()
    g3(gy, 7 + (1 - yh), gc).start()
    loop(8, 12, build)
    xf = (x + 2) % NX
    g3(gi(xl, 0, c), 1, gr).wait_recv()
    g3(gi(xl, 0, c), 5, gr).start()
    g3(gi(xl, 0, c), 7 + 6, gc).start()
    g3(gi(xr, 1, c), 4, gl).wait_recv()
    g3(gi(xr, 1, c), 6, gl).start()
    g3(gi(xr, 1, c), 7 + 3, gc).start()
    g3(gi(xl, 1, c), 2, gr).wait_recv()
    g3(gi(xl, 1, c), 7 + 7, gc).start()
    g3(gi(xr, 0, c), 3, gl).wait_recv()
    g3(gi(xr, 0, c), 7 + 2, gc).start()
    loop(12, 16, build)
    for h in range(2):
        g3(gi(xf, h, c), 5 + h, gr).wait_recv()
        g3(gi(xf, h, c), 7 + 4 + h, gc).start()
    for dx in range(4):
        for h in range(2):
            g3(gi((x + dx) % NX, h, 1 - c), 7 + 2 * dx + h, gc).wait_recv()

    for cp in w_in:
        cp.wait()

    def spread(q):
        t0 = xb[:, 2 * q].reshape(256, 128)
        t1 = xb[:, 2 * q + 1].reshape(256, 128)
        xe[q] = mm(er[q], jnp.concatenate([t0, t1], axis=1), LAST).astype(BF)

    loop(0, 16, spread)

    def host(s):
        return jnp.where(s < 16, s, hot_ref[jnp.maximum(s - 16, 0)])

    def first_dots(s):
        w = wall[host(s)]
        rows = pl.ds(pl.multiple_of(s * 16, 16), 16)
        xd = xe[:, rows, :].reshape(256, 256)
        se[:, rows, 0:256] = mm(xd[:, 0:128], w[:, 0:256]).astype(BF).reshape(16, 16, 256)
        se[:, rows, 256:384] = mm(xd[:, 128:256], w[:, 256:384]).astype(BF).reshape(16, 16, 128)

    loop(0, 32, first_dots)

    def squeeze(q):
        cc = mm(et[q], se[q]).astype(BF)
        zp = q % 8
        pa[pl.ds(2 * q, 2)] = cc[:, 0:256].reshape(2, 128, 256)
        for i in range(2):
            pb[2 * zp + i, q // 8] = cc[128 * i : 128 * (i + 1), 256:384]

    def ya_put(t):
        return put(pa.at[(1 - y) * NZ + t], ya.at[t], ya_s.at[t], ya_q.at[t], ep=py)

    def near(i):
        off = jnp.where(i % 2 == 1, 4 - (i + 1) // 2, 4 + i // 2)
        return (z // 2 + off) % 8

    def squeeze_far(i):
        zp = near(i)
        squeeze((1 - y) * 8 + zp)
        ya_put(2 * zp).start()
        ya_put(2 * zp + 1).start()

    loop(0, 8, squeeze_far)
    loop(0, 8, lambda i: squeeze(y * 8 + near(i)))

    def target(d, n, k):
        return (z + NZ + (n - k if d == 0 else k - n)) % NZ

    def a_step(d, n, k):
        t = target(d, n, k)
        ya_put(t).wait_recv()
        v = pa[y * NZ + t].astype(F32) + ya[t].astype(F32)
        if not (isinstance(k, int) and k == 0):
            put(pa.at[0], ra.at[d, k - 1], ra_s.at[d, k - 1], ra_q.at[d, k - 1], ep=zr).wait_recv()
            v = v + ra[d, k - 1].astype(F32)
        pa[y * NZ + t] = v.astype(BF)
        put(
            pa.at[y * NZ + t], ra.at[d, k], ra_s.at[d, k], ra_q.at[d, k], ep=zr if d == 0 else zl
        ).start()

    def b_step(d, n, k):
        t = target(d, n, k)
        if not (isinstance(k, int) and k == 0):
            put(pb.at[0], rb.at[d, k - 1], rb_s.at[d, k - 1], rb_q.at[d, k - 1], ep=zr).wait_recv()
            pb[t] = (pb[t].astype(F32) + rb[d, k - 1].astype(F32)).astype(BF)
        put(pb.at[t], rb.at[d, k], rb_s.at[d, k], rb_q.at[d, k], ep=zr if d == 0 else zl).start()

    def all_steps(k):
        b_step(0, 7, k)
        b_step(1, 8, k)
        a_step(0, 8, k)
        a_step(1, 7, k)

    all_steps(0)
    loop(1, 7, all_steps)
    b_step(1, 8, 7)
    a_step(0, 8, 7)
    put(pb.at[0], rb.at[0, 6], rb_s.at[0, 6], rb_q.at[0, 6], ep=zr).wait_recv()
    put(pb.at[0], rb.at[1, 7], rb_s.at[1, 7], rb_q.at[1, 7], ep=zr).wait_recv()
    ag_own = (
        pb[z, y].astype(F32) + rb[0, 6, y].astype(F32) + rb[1, 7, y].astype(F32)
    )
    pb[z, 1 - y] = (
        pb[z, 1 - y].astype(F32) + rb[0, 6, 1 - y].astype(F32) + rb[1, 7, 1 - y].astype(F32)
    ).astype(BF)
    yb_put = put(pb.at[z, 1 - y], yb, yb_s, yb_q, ep=py)
    yb_put.start()
    ya_put(z).wait_recv()
    put(pa.at[0], ra.at[1, 6], ra_s.at[1, 6], ra_q.at[1, 6], ep=zr).wait_recv()
    put(pa.at[0], ra.at[0, 7], ra_s.at[0, 7], ra_q.at[0, 7], ep=zr).wait_recv()
    pre = (
        pa[p].astype(F32) + ya[z].astype(F32) + ra[0, 7].astype(F32) + ra[1, 6].astype(F32)
    )
    gate, up = pre[:, 0:128], pre[:, 128:256]
    sg = jax.nn.sigmoid(gate)
    hb[z, y] = (gate * sg * up).astype(BF)
    hy_put = put(hb.at[z, y], hb.at[z, y], hy_s, hy_q, ep=py)
    hy_put.start()
    yb_put.wait_recv()
    ag = ag_own + yb[...].astype(F32)
    ha[p, :, 0:128] = (ag * up * sg * (1.0 + gate * (1.0 - sg))).astype(BF)
    ha[p, :, 128:256] = (ag * gate * sg).astype(BF)

    def origin(d, k):
        return (z + NZ + (-k if d == 0 else k)) % NZ

    def ga_put(d, k, o):
        return put(
            ha.at[y * NZ + o], ha.at[y * NZ + o], ga_s.at[d, k], ga_q.at[d, k], ep=zr if d == 0 else zl
        )

    def gb_put(d, k, o):
        return put(hb.at[o], hb.at[o], gb_s.at[d, k], gb_q.at[d, k], ep=zr if d == 0 else zl)

    def gy_put(yy, o):
        return put(ha.at[yy * NZ + o], ha.at[yy * NZ + o], gy_s.at[o], gy_q.at[o], ep=py)

    ga_put(0, 0, z).start()
    ga_put(1, 0, z).start()
    gy_put(y, z).start()
    put(hb.at[z, 1 - y], hb.at[z, 1 - y], hy_s, hy_q, ep=py).wait_recv()
    gb_put(0, 0, z).start()
    gb_put(1, 0, z).start()

    def ga_step(d, k, more=True):
        o = origin(d, k)
        ga_put(d, k - 1, o).wait_recv()
        if more:
            ga_put(d, k, o).start()
        gy_put(y, o).start()

    def gb_step(d, k, more=True):
        o = origin(d, k)
        gb_put(d, k - 1, o).wait_recv()
        if more:
            gb_put(d, k, o).start()

    def gather_steps(k):
        ga_step(0, k)
        ga_step(1, k)
        gb_step(0, k)
        gb_step(1, k)

    loop(1, 7, gather_steps)
    ga_step(0, 7)
    ga_step(1, 7, False)
    gb_step(0, 7, False)
    gb_step(1, 7)
    ga_step(0, 8, False)
    gb_step(1, 8, False)

    def spread_back(q):
        zp = q % 8
        hq = jnp.concatenate(
            [
                ha[pl.ds(2 * q, 2)].reshape(256, 256),
                jnp.concatenate([hb[2 * zp, q // 8], hb[2 * zp + 1, q // 8]], axis=0),
            ],
            axis=1,
        )
        he[q] = mm(er[q], hq).astype(BF)

    loop(0, 8, lambda i: spread_back(y * 8 + i))
    loop(0, 16, lambda o: gy_put(1 - y, o).wait_recv())
    loop(0, 8, lambda i: spread_back((1 - y) * 8 + i))

    def back_dots(s):
        w = wall[host(s)]
        rows = pl.ds(pl.multiple_of(s * 16, 16), 16)
        hs = he[:, rows, :].reshape(256, 384)
        se[:, rows, 0:128] = mm(hs[:, 256:384], w[:, 256:384], LAST).astype(BF).reshape(16, 16, 128)
        se[:, rows, 128:256] = mm(hs[:, 0:256], w[:, 0:256], LAST).astype(BF).reshape(16, 16, 128)

    loop(0, 32, back_dots)

    def squeeze_out(q):
        cc = mm(et[q], se[q, :, 0:256]).astype(BF)
        for i in range(2):
            for kind in range(2):
                qq[kind * 8 : (kind + 1) * 8, 2 * q + i] = cc[
                    128 * i : 128 * (i + 1), 128 * kind : 128 * (kind + 1)
                ].reshape(8, 16, 128)

    loop(0, 16, squeeze_out)

    def c5(dx, h):
        i = 2 * dx + h
        return put(qq.at[gi((x + dx) % NX, h, 1 - c)], rc.at[i], c5_s.at[i], c5_q.at[i], grp=gc)

    order = (2, 1, 3, 0)
    for dx in order:
        for h in range(2):
            c5(dx, h).start()

    def weight_dots(s):
        rows = pl.ds(pl.multiple_of(s * 16, 16), 16)
        xd = xe[:, rows, :].reshape(256, 256)
        hs = he[:, rows, :].reshape(256, 384)
        tot[s, :, 0:256] = mm(xd[:, 0:128], hs[:, 0:256], FIRST)[0:112].astype(BF).astype(F32)
        tot[s, :, 256:384] = mm(xd[:, 128:256], hs[:, 256:384], FIRST)[0:112].astype(BF).astype(F32)

    def addto(t, r):
        qq[t] = (qq[t].astype(F32) + r.astype(F32)).astype(BF)

    def with_core(dx, h):
        c5(dx, h).wait_recv()
        addto(gi((x + dx) % NX, h, c), rc[2 * dx + h])

    def f5(h):
        return put(qq.at[gi(xf, h, c)], rfar.at[h], f5_s.at[h], f5_q.at[h], grp=gr if h == 0 else gl)

    def x5(d, h):
        t = xr if d == 0 else xl
        return put(
            qq.at[gi(t, h, c)], rx.at[d, h], x5_s.at[d, h], x5_q.at[d, h], grp=gr if d == 0 else gl
        )

    loop(0, 4, weight_dots)
    for h in range(2):
        with_core(2, h)
        f5(h).start()
    with_core(1, 1)
    x5(0, 1).start()
    with_core(3, 0)
    x5(1, 0).start()
    with_core(1, 0)
    with_core(3, 1)
    f5(0).wait_recv()
    addto(gi(xr, 0, c), rfar[0])
    x5(0, 0).start()
    f5(1).wait_recv()
    addto(gi(xl, 1, c), rfar[1])
    x5(1, 1).start()
    loop(4, 12, weight_dots)
    for h in range(2):
        c5(0, h).wait_recv()
        for d in range(2):
            x5(d, h).wait_recv()

    def own_sum(h):
        return (
            qq[gi(x, h, c)].astype(F32)
            + rc[h].astype(F32)
            + rx[0, h].astype(F32)
            + rx[1, h].astype(F32)
        )

    qq[gy] = own_sum(1 - yh).astype(BF)
    y5 = put(qq.at[gy], ry, y5_s, y5_q, grp=gy)
    y5.start()
    loop(12, 20, weight_dots)
    mine = own_sum(yh)
    y5.wait_recv()
    fin[...] = (mine + ry[...].astype(F32)).astype(BF)

    b1 = lambda i, t: put(fin.at[t], b1r.at[p // 2, p % 2], b1_s.at[i], b1_q.at[i], ep=t)
    b2 = lambda i, t: put(b1r.at[t], b2r.at[g], b2_s.at[i], b2_q.at[i], grp=t)
    loop(1, NEP, lambda i: b1(i, (p + i) % NEP).start())
    b1r[p // 2, p % 2] = fin[p]
    loop(20, 32, weight_dots)

    def b1_wait(i):
        f = (p + NEP - i) % NEP
        put(fin.at[0], b1r.at[f // 2, f % 2], b1_s.at[i], b1_q.at[i], ep=f).wait_recv()

    loop(1, NEP, b1_wait)
    loop(1, NGRP, lambda i: b2(i, (g + i) % NGRP).start())
    b2r[g] = b1r[g]

    def chain(j):
        e = hot_ref[j]

        def look(i, prev):
            return jnp.where((i < j) & (hot_ref[i] == e), 16 + i, prev)

        prev = lax.fori_loop(0, 16, look, e)
        tot[16 + j] = tot[16 + j] + tot[prev]

    loop(0, 16, chain)

    def close(e):
        last = lax.fori_loop(0, 16, lambda i, v: jnp.where(hot_ref[i] == e, 16 + i, v), e)
        v = tot[last].astype(BF)
        for i in range(3):
            go[i, e] = v[:, 128 * i : 128 * (i + 1)]

    loop(0, 16, close)
    w_out = [
        pltpu.make_async_copy(go.at[i], r, o_sem.at[i]) for i, r in enumerate((gg_ref, gu_ref, gd_ref))
    ]
    for cp in w_out:
        cp.start()

    def b2_wait(i):
        f = (g + NGRP - i) % NGRP
        put(b1r.at[0], b2r.at[f], b2_s.at[i], b2_q.at[i], grp=f).wait_recv()

    loop(1, NGRP, b2_wait)
    for kind, ref in enumerate((out_ref, gtok_ref)):
        for h in range(2):
            rows = b2r[kind * 8 : (kind + 1) * 8, h].reshape(128, 128).astype(F32)
            v = jnp.transpose(rows)[0:112]
            if kind == 0:
                v = v * rw_row
            ref[h * 112 : (h + 1) * 112, :] = v.astype(BF)

    loop(1, NGRP, lambda i: a1(i, (g + i) % NGRP).wait_send())
    loop(1, NEP, lambda i: mt(i, (p + i) % NEP).wait_send())
    loop(1, NEP, lambda i: a2(i, (p + i) % NEP).wait_send())
    loop(0, 15, lambda i: g3(g, i, gy).wait_send())
    loop(0, 16, lambda t: ya_put(t).wait_send())
    for d in range(2):
        na, nb = (8, 7) if d == 0 else (7, 8)
        loop(0, na, lambda k: put(pa.at[0], ra.at[d, k], ra_s.at[d, k], ra_q.at[d, k], ep=zr).wait_send())
        loop(0, nb, lambda k: put(pb.at[0], rb.at[d, k], rb_s.at[d, k], rb_q.at[d, k], ep=zr).wait_send())
        loop(0, na, lambda k: ga_put(d, k, z).wait_send())
        loop(0, nb, lambda k: gb_put(d, k, z).wait_send())
    yb_put.wait_send()
    hy_put.wait_send()
    loop(0, 16, lambda o: gy_put(y, o).wait_send())
    for dx in range(4):
        for h in range(2):
            c5(dx, h).wait_send()
    for h in range(2):
        f5(h).wait_send()
        for d in range(2):
            x5(d, h).wait_send()
    y5.wait_send()
    loop(1, NEP, lambda i: b1(i, (p + i) % NEP).wait_send())
    loop(1, NGRP, lambda i: b2(i, (g + i) % NGRP).wait_send())
    for cp in w_out:
        cp.wait()


def layer(tokens, routes, route_weights, hot_experts, w_gate, w_up, w_down, cotangent):
    v = pltpu.VMEM
    dma = pltpu.SemaphoreType.DMA
    vm = pl.BlockSpec(memory_space=pltpu.VMEM)
    anym = pl.BlockSpec(memory_space=pl.ANY)
    sems = [
        (3,), (3,), (16,), (16,), (32,), (32,), (32,), (32,), (15,), (15,),
        (16,), (16,), (2, 8), (2, 8), (2, 8), (2, 8), None, None,
        None, None, (2, 8), (2, 8), (2, 8), (2, 8), (16,), (16,),
        (8,), (8,), (2,), (2,), (2, 2), (2, 2), None, None, (32,), (32,), (16,), (16,),
    ]
    out_t, gtok_t, gg, gu, gd = pl.pallas_call(
        body,
        out_shape=(
            jax.ShapeDtypeStruct((224, 128), BF),
            jax.ShapeDtypeStruct((224, 128), BF),
            jax.ShapeDtypeStruct((16, 112, 128), BF),
            jax.ShapeDtypeStruct((16, 112, 128), BF),
            jax.ShapeDtypeStruct((16, 112, 128), BF),
        ),
        in_specs=[vm, vm, vm, pl.BlockSpec(memory_space=pltpu.SMEM), anym, anym, anym, vm],
        out_specs=(vm, vm, anym, anym, anym),
        scratch_shapes=[
            v((16, 2, 16, 128), BF),
            v((32, 16, 128), BF),
            v((16, 2, 16, 128), BF),
            v((16, 32, 16, 128), BF),
            v((16, 512, 256), BF),
            v((16, 256, 512), BF),
            v((16, 128, 384), BF),
            v((16, 512, 256), BF),
            v((16, 512, 384), BF),
            v((32, 128, 256), BF),
            v((16, 2, 128, 128), BF),
            v((16, 128, 256), BF),
            v((2, 8, 128, 256), BF),
            v((2, 8, 2, 128, 128), BF),
            v((128, 128), BF),
            v((32, 128, 256), BF),
            v((16, 2, 128, 128), BF),
            v((16, 512, 384), BF),
            v((16, 32, 16, 128), BF),
            v((8, 32, 16, 128), BF),
            v((2, 32, 16, 128), BF),
            v((2, 2, 32, 16, 128), BF),
            v((32, 16, 128), BF),
            v((32, 16, 128), BF),
            v((16, 2, 16, 128), BF),
            v((16, 2, 16, 128), BF),
            v((32, 112, 384), F32),
            v((3, 16, 112, 128), BF),
        ]
        + [dma if s is None else dma(s) for s in sems],
        compiler_params=pltpu.CompilerParams(
            collective_id=0, has_side_effects=True, vmem_limit_bytes=60 * 1024 * 1024
        ),
        cost_estimate=pl.CostEstimate(flops=8 * 10**9, bytes_accessed=3 * 10**6, transcendentals=0),
    )(
        tokens.T,
        routes.reshape(1, 128),
        route_weights.reshape(1, 128),
        hot_experts,
        w_gate,
        w_up,
        jnp.swapaxes(w_down, 1, 2),
        cotangent.T,
    )
    return out_t.T, gtok_t.T, gg, gu, jnp.swapaxes(gd, 1, 2)


def solution(mesh):
    placed = (
        P("ep", "grp"),
        P("ep", None),
        P("ep", None),
        P(),
        P(None, "ep", "grp"),
        P(None, "ep", "grp"),
        P(None, "grp", "ep"),
        P("ep", "grp"),
    )
    return jax.shard_map(
        layer,
        mesh=mesh,
        in_specs=placed,
        out_specs=(
            P("ep", "grp"),
            P("ep", "grp"),
            P(None, "ep", "grp"),
            P(None, "ep", "grp"),
            P(None, "grp", "ep"),
        ),
        check_vma=False,
    )
```

```python
import functools

import jax
import jax.numpy as jnp
from jax import lax
from jax.experimental import pallas as pl
from jax.experimental.pallas import tpu as pltpu
from jax.sharding import PartitionSpec as P

MESH = pl.DeviceIdType.MESH
BF = jnp.bfloat16
F32 = jnp.float32
NX, NY, NZ, NEP, NGRP = 4, 2, 16, 32, 16
LAST = (((1,), (1,)), ((), ()))
FIRST = (((0,), (0,)), ((), ()))


def mm(a, b, dims=(((1,), (0,)), ((), ()))):
    return lax.dot_general(a, b, dims, preferred_element_type=F32)


def body(
    tok_ref, routes_ref, rw_ref, hot_ref, wg_ref, wu_ref, wd_ref, cot_ref,
    rows_ref, slots_ref,
    src, meta, a1r, xb, er, et, wall, xe, se, pa, pb, ya, ra, rb, yb,
    ha, hb, he, qq, rc, rfar, rx, ry, fin, b2r, tot,
    w_sem, o_sem, a1_s, a1_q, m_s, m_q, a2_s, a2_q, g3_s, g3_q,
    ya_s, ya_q, ra_s, ra_q, rb_s, rb_q, yb_s, yb_q,
    hy_s, hy_q, ga_s, ga_q, gb_s, gb_q, gy_s, gy_q,
    c5_s, c5_q, f5_s, f5_q, x5_s, x5_q, y5_s, y5_q, b1_s, b1_q,
):
    g = lax.axis_index("grp")
    p = lax.axis_index("ep")
    x, yh, c = g // 4, (g // 2) % 2, g % 2
    y, z = p // NZ, p % NZ
    zr, zl = y * NZ + (z + 1) % NZ, y * NZ + (z + NZ - 1) % NZ
    py = (1 - y) * NZ + z
    gi = lambda xx, hh, cc: xx * 4 + hh * 2 + cc
    xr, xl = (x + 1) % NX, (x + 3) % NX
    gr, gl = gi(xr, yh, c), gi(xl, yh, c)
    gy, gc = gi(x, 1 - yh, c), gi(x, yh, 1 - c)

    def put(s, d, ss, rs, **dev):
        return pltpu.make_async_remote_copy(
            src_ref=s, dst_ref=d, send_sem=ss, recv_sem=rs, device_id=dev, device_id_type=MESH
        )

    w_in = [
        pltpu.make_async_copy(r, wall.at[:, pl.ds(0, 112), pl.ds(128 * i, 128)], w_sem.at[i])
        for i, r in enumerate((wg_ref, wu_ref, wd_ref))
    ]
    for cp in w_in:
        cp.start()

    tail = []

    barrier = pltpu.get_barrier_semaphore()

    def hello_g(i, _):
        pl.semaphore_signal(barrier, inc=1, device_id={"grp": (g + i) % NGRP}, device_id_type=MESH)
        return 0

    def hello_e(i, _):
        pl.semaphore_signal(barrier, inc=1, device_id={"ep": (p + i) % NEP}, device_id_type=MESH)
        return 0

    lax.fori_loop(1, NGRP, hello_g, 0)
    lax.fori_loop(1, NEP, hello_e, 0)

    def hello_b(i, _):
        t, h = i // 2, i % 2

        @pl.when(jnp.logical_not((t == g) & (2 * g + h == p)))
        def _():
            pl.semaphore_signal(barrier, inc=1, device_id={"grp": t, "ep": 2 * g + h}, device_id_type=MESH)

        return 0

    lax.fori_loop(0, NEP, hello_b, 0)

    slot_row = routes_ref[...]
    dz = (cot_ref[...].astype(F32) * rw_ref[...]).astype(BF)
    for h in range(2):
        src[0:7, h] = tok_ref[h * 112 : (h + 1) * 112, :].reshape(7, 16, 128)
        src[8:15, h] = dz[h * 112 : (h + 1) * 112, :].reshape(7, 16, 128)
    src[7] = jnp.zeros((2, 16, 128), BF)
    src[15] = jnp.zeros((2, 16, 128), BF)
    wall[:, 112:128, :] = jnp.zeros((16, 16, 384), BF)

    oh = jnp.where(lax.broadcasted_iota(jnp.int32, (NEP, 128), 0) == slot_row, 1.0, 0.0).astype(F32)
    upper = jnp.where(
        lax.broadcasted_iota(jnp.int32, (128, 128), 0) < lax.broadcasted_iota(jnp.int32, (128, 128), 1), 1.0, 0.0
    ).astype(BF)
    before = mm(oh.astype(BF), upper)
    pos_row = jnp.sum(oh * before, axis=0, keepdims=True)
    row_id = lax.broadcasted_iota(jnp.int32, (16, 128), 0)
    mrows = jnp.where(row_id == 0, slot_row.astype(F32), jnp.where(row_id == 1, pos_row, 0.0))
    meta[p] = mrows.astype(BF)

    pl.semaphore_wait(barrier, NGRP + NEP - 2 + NEP - jnp.where(p // 2 == g, 1, 0))

    a1 = lambda i, t: put(src.at[t], a1r.at[g], a1_s.at[i], a1_q.at[i], grp=t)
    mt = lambda i, t: put(meta.at[p], meta.at[p], m_s.at[i], m_q.at[i], ep=t)
    a2 = lambda i, t: put(a1r.at[t // 2, t % 2], xb.at[g, p], a2_s.at[i], a2_q.at[i], ep=t)

    def loop(lo, hi, f):
        def step(i, _):
            f(i)
            return 0

        lax.fori_loop(lo, hi, step, 0)

    def dots(lo, hi, f, unroll=1):
        def step(i, _):
            f(i)
            return 0

        lax.fori_loop(lo, hi, step, 0, unroll=unroll)

    loop(1, NGRP, lambda i: a1(i, (g + i) % NGRP).start())
    loop(1, NEP, lambda i: mt(i, (p + i) % NEP).start())
    a1r[g] = src[g]

    def a1_wait(i):
        f = (g + NGRP - i) % NGRP
        put(src.at[f], a1r.at[f], a1_s.at[i], a1_q.at[i], grp=f).wait_recv()

    loop(1, NGRP, a1_wait)
    loop(1, NEP, lambda i: a2(i, (p + i) % NEP).start())
    tail.append(lambda: loop(1, NGRP, lambda i: a1(i, (g + i) % NGRP).wait_send()))
    tail.append(lambda: loop(1, NEP, lambda i: mt(i, (p + i) % NEP).wait_send()))
    tail.append(lambda: loop(1, NEP, lambda i: a2(i, (p + i) % NEP).wait_send()))
    xb[g, p] = a1r[p // 2, p % 2]

    def m_wait(i):
        f = (p + NEP - i) % NEP
        put(meta.at[p], meta.at[f], m_s.at[i], m_q.at[i], ep=f).wait_recv()

    loop(1, NEP, m_wait)

    def build(q):
        m0 = meta[2 * q].astype(F32)
        m1 = meta[2 * q + 1].astype(F32)
        d0 = m0[0:1, :] * 16.0 + m0[1:2, :]
        d1 = m1[0:1, :] * 16.0 + m1[1:2, :] + 8.0
        row = jnp.concatenate([d0, d1], axis=1)
        irow = row.astype(jnp.int32)
        er[q] = jnp.where(
            lax.broadcasted_iota(jnp.int32, (512, 256), 0) == irow, 1.0, 0.0
        ).astype(BF)
        col = jnp.transpose(jnp.broadcast_to(row, (128, 256))).astype(jnp.int32)
        for b in range(4):
            et[q, :, 128 * b : 128 * (b + 1)] = jnp.where(
                lax.broadcasted_iota(jnp.int32, (256, 128), 1) + 128 * b == col, 1.0, 0.0
            ).astype(BF)

    def a2_wait(i):
        f = (p + NEP - i) % NEP
        put(a1r.at[0, 0], xb.at[g, f], a2_s.at[i], a2_q.at[i], ep=f).wait_recv()

    dots(0, 4, build)
    loop(1, NEP, a2_wait)

    def g3(chunk, i, t):
        return put(xb.at[chunk], xb.at[chunk], g3_s.at[i], g3_q.at[i], grp=t)

    g3(g, 0, gy).start()
    g3(g, 1 + yh, gr).start()
    g3(g, 3 + yh, gl).start()
    g3(g, 7 + yh, gc).start()
    dots(4, 8, build)
    g3(gy, 0, gy).wait_recv()
    g3(gy, 1 + (1 - yh), gr).start()
    g3(gy, 3 + (1 - yh), gl).start()
    g3(gy, 7 + (1 - yh), gc).start()
    dots(8, 12, build)
    xf = (x + 2) % NX
    g3(gi(xl, 0, c), 1, gr).wait_recv()
    g3(gi(xl, 0, c), 5, gr).start()
    g3(gi(xl, 0, c), 7 + 6, gc).start()
    g3(gi(xr, 1, c), 4, gl).wait_recv()
    g3(gi(xr, 1, c), 6, gl).start()
    g3(gi(xr, 1, c), 7 + 3, gc).start()
    g3(gi(xl, 1, c), 2, gr).wait_recv()
    g3(gi(xl, 1, c), 7 + 7, gc).start()
    g3(gi(xr, 0, c), 3, gl).wait_recv()
    g3(gi(xr, 0, c), 7 + 2, gc).start()
    dots(12, 16, build)
    for h in range(2):
        g3(gi(xf, h, c), 5 + h, gr).wait_recv()
        g3(gi(xf, h, c), 7 + 4 + h, gc).start()
    for dx in range(4):
        for h in range(2):
            g3(gi((x + dx) % NX, h, 1 - c), 7 + 2 * dx + h, gc).wait_recv()

    tail.append(lambda: loop(0, 15, lambda i: g3(g, i, gy).wait_send()))
    for cp in w_in:
        cp.wait()

    def spread(q):
        t0 = xb[:, 2 * q].reshape(256, 128)
        t1 = xb[:, 2 * q + 1].reshape(256, 128)
        xe[q] = mm(er[q], jnp.concatenate([t0, t1], axis=1), LAST).astype(BF)

    dots(0, 16, spread)

    def host(s):
        return jnp.where(s < 16, s, hot_ref[jnp.maximum(s - 16, 0)])

    def first_dots(s):
        w = wall[host(s)]
        rows = pl.ds(pl.multiple_of(s * 16, 16), 16)
        xd = xe[:, rows, :].reshape(256, 256)
        se[:, rows, 0:256] = mm(xd[:, 0:128], w[:, 0:256]).astype(BF).reshape(16, 16, 256)
        se[:, rows, 256:384] = mm(xd[:, 128:256], w[:, 256:384]).astype(BF).reshape(16, 16, 128)

    dots(0, 32, first_dots, 1)

    def squeeze(q):
        cc = mm(et[q], se[q]).astype(BF)
        zp = q % 8
        pa[pl.ds(2 * q, 2)] = cc[:, 0:256].reshape(2, 128, 256)
        for i in range(2):
            pb[2 * zp + i, q // 8] = cc[128 * i : 128 * (i + 1), 256:384]

    def ya_put(t):
        return put(pa.at[(1 - y) * NZ + t], ya.at[t], ya_s.at[t], ya_q.at[t], ep=py)

    def near(i):
        off = jnp.where(i % 2 == 1, 4 - (i + 1) // 2, 4 + i // 2)
        return (z // 2 + off) % 8

    def squeeze_far(i):
        zp = near(i)
        squeeze((1 - y) * 8 + zp)
        ya_put(2 * zp).start()
        ya_put(2 * zp + 1).start()

    dots(0, 8, squeeze_far)
    dots(0, 8, lambda i: squeeze(y * 8 + near(i)))
    tail.append(lambda: loop(0, 16, lambda t: ya_put(t).wait_send()))

    def target(d, n, k):
        return (z + NZ + (n - k if d == 0 else k - n)) % NZ

    def a_put(d, k, t, j):
        r = pl.ds(64 * j, 64)
        return put(
            pa.at[y * NZ + t, r], ra.at[d, k, r], ra_s.at[d, k, j], ra_q.at[d, k, j], ep=zr if d == 0 else zl
        )

    def b_put(d, k, t, j):
        return put(
            pb.at[t, j], rb.at[d, k, j], rb_s.at[d, k, j], rb_q.at[d, k, j], ep=zr if d == 0 else zl
        )

    def a_step(d, n, k, j):
        t = target(d, n, k)
        r = pl.ds(64 * j, 64)
        if j == 0:
            ya_put(t).wait_recv()
        v = pa[y * NZ + t, r].astype(F32) + ya[t, r].astype(F32)
        if not (isinstance(k, int) and k == 0):
            a_put(d, k - 1, t, j).wait_recv()
            v = v + ra[d, k - 1, r].astype(F32)
        pa[y * NZ + t, r] = v.astype(BF)
        a_put(d, k, t, j).start()

    def b_step(d, n, k, j):
        t = target(d, n, k)
        if not (isinstance(k, int) and k == 0):
            b_put(d, k - 1, t, j).wait_recv()
            pb[t, j] = (pb[t, j].astype(F32) + rb[d, k - 1, j].astype(F32)).astype(BF)
        b_put(d, k, t, j).start()

    def all_steps(k):
        for j in range(2):
            b_step(0, 7, k, j)
            b_step(1, 8, k, j)
        for j in range(2):
            a_step(0, 8, k, j)
            a_step(1, 7, k, j)

    all_steps(0)
    loop(1, 7, all_steps)
    for j in range(2):
        b_step(1, 8, 7, j)
    for j in range(2):
        a_step(0, 8, 7, j)
    for j in range(2):
        b_put(0, 6, z, j).wait_recv()
        b_put(1, 7, z, j).wait_recv()
    ag_own = (
        pb[z, y].astype(F32) + rb[0, 6, y].astype(F32) + rb[1, 7, y].astype(F32)
    )
    pb[z, 1 - y] = (
        pb[z, 1 - y].astype(F32) + rb[0, 6, 1 - y].astype(F32) + rb[1, 7, 1 - y].astype(F32)
    ).astype(BF)
    yb_put = put(pb.at[z, 1 - y], yb, yb_s, yb_q, ep=py)
    yb_put.start()

    def ring_sends():
        for d in range(2):
            na, nb = (8, 7) if d == 0 else (7, 8)
            for j in range(2):
                loop(0, na, lambda k: a_put(d, k, z, j).wait_send())
                loop(0, nb, lambda k: b_put(d, k, z, j).wait_send())
        yb_put.wait_send()

    tail.append(ring_sends)
    ya_put(z).wait_recv()
    for j in range(2):
        a_put(1, 6, z, j).wait_recv()
        a_put(0, 7, z, j).wait_recv()
    pre = (
        pa[p].astype(F32) + ya[z].astype(F32) + ra[0, 7].astype(F32) + ra[1, 6].astype(F32)
    )
    gate, up = pre[:, 0:128], pre[:, 128:256]
    sg = jax.nn.sigmoid(gate)
    hb[z, y] = (gate * sg * up).astype(BF)
    hy_put = put(hb.at[z, y], hb.at[z, y], hy_s, hy_q, ep=py)
    hy_put.start()
    yb_put.wait_recv()
    ag = ag_own + yb[...].astype(F32)
    ha[p, :, 0:128] = (ag * up * sg * (1.0 + gate * (1.0 - sg))).astype(BF)
    ha[p, :, 128:256] = (ag * gate * sg).astype(BF)

    tail.append(hy_put.wait_send)
    def origin(d, k):
        return (z + NZ + (-k if d == 0 else k)) % NZ

    def ga_put(d, k, o):
        return put(
            ha.at[y * NZ + o], ha.at[y * NZ + o], ga_s.at[d, k], ga_q.at[d, k], ep=zr if d == 0 else zl
        )

    def gb_put(d, k, o):
        return put(hb.at[o], hb.at[o], gb_s.at[d, k], gb_q.at[d, k], ep=zr if d == 0 else zl)

    def gy_put(yy, o):
        return put(ha.at[yy * NZ + o], ha.at[yy * NZ + o], gy_s.at[o], gy_q.at[o], ep=py)

    ga_put(0, 0, z).start()
    ga_put(1, 0, z).start()
    gy_put(y, z).start()
    put(hb.at[z, 1 - y], hb.at[z, 1 - y], hy_s, hy_q, ep=py).wait_recv()
    gb_put(0, 0, z).start()
    gb_put(1, 0, z).start()

    def ga_step(d, k, more=True):
        o = origin(d, k)
        ga_put(d, k - 1, o).wait_recv()
        if more:
            ga_put(d, k, o).start()
        gy_put(y, o).start()

    def gb_step(d, k, more=True):
        o = origin(d, k)
        gb_put(d, k - 1, o).wait_recv()
        if more:
            gb_put(d, k, o).start()

    def gather_steps(k):
        ga_step(0, k)
        ga_step(1, k)
        gb_step(0, k)
        gb_step(1, k)

    loop(1, 7, gather_steps)
    ga_step(0, 7)
    ga_step(1, 7, False)
    gb_step(0, 7, False)
    gb_step(1, 7)
    ga_step(0, 8, False)
    gb_step(1, 8, False)

    def gather_sends():
        for d in range(2):
            na, nb = (8, 7) if d == 0 else (7, 8)
            loop(0, na, lambda k: ga_put(d, k, z).wait_send())
            loop(0, nb, lambda k: gb_put(d, k, z).wait_send())
        loop(0, 16, lambda o: gy_put(y, o).wait_send())

    tail.append(gather_sends)

    def spread_back(q):
        zp = q % 8
        hq = jnp.concatenate(
            [
                ha[pl.ds(2 * q, 2)].reshape(256, 256),
                jnp.concatenate([hb[2 * zp, q // 8], hb[2 * zp + 1, q // 8]], axis=0),
            ],
            axis=1,
        )
        he[q] = mm(er[q], hq).astype(BF)

    dots(0, 8, lambda i: spread_back(y * 8 + i))
    loop(0, 16, lambda o: gy_put(1 - y, o).wait_recv())
    dots(0, 8, lambda i: spread_back((1 - y) * 8 + i))

    def back_dots(s):
        w = wall[host(s)]
        rows = pl.ds(pl.multiple_of(s * 16, 16), 16)
        hs = he[:, rows, :].reshape(256, 384)
        se[:, rows, 0:128] = mm(hs[:, 256:384], w[:, 256:384], LAST).astype(BF).reshape(16, 16, 128)
        se[:, rows, 128:256] = mm(hs[:, 0:256], w[:, 0:256], LAST).astype(BF).reshape(16, 16, 128)

    dots(0, 32, back_dots, 1)

    def squeeze_out(q):
        cc = mm(et[q], se[q, :, 0:256]).astype(BF)
        for i in range(2):
            for kind in range(2):
                qq[kind * 8 : (kind + 1) * 8, 2 * q + i] = cc[
                    128 * i : 128 * (i + 1), 128 * kind : 128 * (kind + 1)
                ].reshape(8, 16, 128)

    dots(0, 16, squeeze_out)

    def c5(dx, h):
        i = 2 * dx + h
        return put(qq.at[gi((x + dx) % NX, h, 1 - c)], rc.at[i], c5_s.at[i], c5_q.at[i], grp=gc)

    order = (2, 1, 3, 0)
    for dx in order:
        for h in range(2):
            c5(dx, h).start()

    def weight_dots(s):
        rows = pl.ds(pl.multiple_of(s * 16, 16), 16)
        xd = xe[:, rows, :].reshape(256, 256)
        hs = he[:, rows, :].reshape(256, 384)
        tot[s, :, 0:256] = mm(xd[:, 0:128], hs[:, 0:256], FIRST)[0:112].astype(BF)
        tot[s, :, 256:384] = mm(xd[:, 128:256], hs[:, 256:384], FIRST)[0:112].astype(BF)

    w_out = []

    def weight_group(i):
        dots(8 * i, 8 * i + 8, weight_dots, 1)
        part = pl.ds(8 * i, 8)
        w_out.append(pltpu.make_async_copy(tot.at[part], slots_ref.at[part], o_sem.at[i]))
        w_out[-1].start()

    def addto(t, r):
        qq[t] = (qq[t].astype(F32) + r.astype(F32)).astype(BF)

    def with_core(dx, h):
        c5(dx, h).wait_recv()
        addto(gi((x + dx) % NX, h, c), rc[2 * dx + h])

    def f5(h):
        return put(qq.at[gi(xf, h, c)], rfar.at[h], f5_s.at[h], f5_q.at[h], grp=gr if h == 0 else gl)

    def x5(d, h):
        t = xr if d == 0 else xl
        return put(
            qq.at[gi(t, h, c)], rx.at[d, h], x5_s.at[d, h], x5_q.at[d, h], grp=gr if d == 0 else gl
        )

    for h in range(2):
        with_core(2, h)
        f5(h).start()
    with_core(1, 1)
    x5(0, 1).start()
    with_core(3, 0)
    x5(1, 0).start()
    with_core(1, 0)
    with_core(3, 1)
    f5(0).wait_recv()
    addto(gi(xr, 0, c), rfar[0])
    x5(0, 0).start()
    f5(1).wait_recv()
    addto(gi(xl, 1, c), rfar[1])
    x5(1, 1).start()
    weight_group(0)
    for h in range(2):
        c5(0, h).wait_recv()
        for d in range(2):
            x5(d, h).wait_recv()

    def own_sum(h):
        return (
            qq[gi(x, h, c)].astype(F32)
            + rc[h].astype(F32)
            + rx[0, h].astype(F32)
            + rx[1, h].astype(F32)
        )

    qq[gy] = own_sum(1 - yh).astype(BF)
    y5 = put(qq.at[gy], ry, y5_s, y5_q, grp=gy)
    y5.start()
    weight_group(1)
    mine = own_sum(yh)
    y5.wait_recv()
    fin[...] = (mine + ry[...].astype(F32)).astype(BF)

    def grp_sends():
        for h in range(2):
            for dx in range(4):
                c5(dx, h).wait_send()
            f5(h).wait_send()
            for d in range(2):
                x5(d, h).wait_send()
        y5.wait_send()

    tail.append(grp_sends)
    def b1(f):
        return put(fin.at[f], b2r.at[g, p % 2], b1_s.at[f], b1_q.at[2 * g + p % 2], grp=p // 2, ep=f)

    def b1_here(f):
        return (p // 2 == g) & (f == p)

    def b1_start(i):
        f = (p + i) % NEP

        @pl.when(jnp.logical_not(b1_here(f)))
        def _():
            b1(f).start()

    loop(0, NEP, b1_start)

    @pl.when(p // 2 == g)
    def _():
        b2r[g, p % 2] = fin[p]

    weight_group(2)
    weight_group(3)

    def b1_wait(i):
        t, h = i // 2, i % 2

        @pl.when(jnp.logical_not((t == g) & (2 * g + h == p)))
        def _():
            put(fin.at[0], b2r.at[t, h], b1_s.at[0], b1_q.at[i], grp=t, ep=2 * g + h).wait_recv()

    def b1_left(f):
        @pl.when(jnp.logical_not(b1_here(f)))
        def _():
            b1(f).wait_send()

    tail.append(lambda: loop(0, NEP, b1_left))
    loop(0, NEP, b1_wait)
    rows_out = pltpu.make_async_copy(b2r, rows_ref, o_sem.at[4])
    rows_out.start()
    tail.append(rows_out.wait)
    for grp4 in w_out:
        tail.append(grp4.wait)

    for wait in tail:
        wait()


def finish(rows_ref, slots_ref, rw_ref, hot_ref, out_ref, gtok_ref, gg_ref, gu_ref, gd_ref, acc):
    def base(e, _):
        acc[e] = slots_ref[e].astype(F32)
        return 0

    def more(j, _):
        e = hot_ref[j]
        acc[e] = acc[e] + slots_ref[16 + j].astype(F32)
        return 0

    def close(e, _):
        v = acc[e].astype(BF)
        gg_ref[e] = v[:, 0:128]
        gu_ref[e] = v[:, 128:256]
        gd_ref[e] = v[:, 256:384]
        return 0

    lax.fori_loop(0, 16, base, 0)
    lax.fori_loop(0, 16, more, 0)
    lax.fori_loop(0, 16, close, 0)
    for kind, ref in enumerate((out_ref, gtok_ref)):
        for h in range(2):
            part = rows_ref[kind * 8 : (kind + 1) * 8, h].reshape(128, 128).astype(F32)
            v = jnp.transpose(part)[0:112]
            if kind == 0:
                v = v * rw_ref[...]
            ref[h * 112 : (h + 1) * 112, :] = v.astype(BF)


def layer(tokens, routes, route_weights, hot_experts, w_gate, w_up, w_down, cotangent):
    v = pltpu.VMEM
    dma = pltpu.SemaphoreType.DMA
    vm = pl.BlockSpec(memory_space=pltpu.VMEM)
    anym = pl.BlockSpec(memory_space=pl.ANY)
    sems = [
        (3,), (5,), (16,), (16,), (32,), (32,), (32,), (32,), (15,), (15,),
        (16,), (16,), (2, 8, 2), (2, 8, 2), (2, 8, 2), (2, 8, 2), None, None,
        None, None, (2, 8), (2, 8), (2, 8), (2, 8), (16,), (16,),
        (8,), (8,), (2,), (2,), (2, 2), (2, 2), None, None, (32,), (32,),
    ]
    rw = route_weights.reshape(1, 128)
    rows, slots = pl.pallas_call(
        body,
        out_shape=(
            jax.ShapeDtypeStruct((16, 2, 16, 128), BF),
            jax.ShapeDtypeStruct((32, 112, 384), BF),
        ),
        in_specs=[vm, vm, vm, pl.BlockSpec(memory_space=pltpu.SMEM), anym, anym, anym, vm],
        out_specs=(anym, anym),
        scratch_shapes=[
            v((16, 2, 16, 128), BF),
            v((32, 16, 128), BF),
            v((16, 2, 16, 128), BF),
            v((16, 32, 16, 128), BF),
            v((16, 512, 256), BF),
            v((16, 256, 512), BF),
            v((16, 128, 384), BF),
            v((16, 512, 256), BF),
            v((16, 512, 384), BF),
            v((32, 128, 256), BF),
            v((16, 2, 128, 128), BF),
            v((16, 128, 256), BF),
            v((2, 8, 128, 256), BF),
            v((2, 8, 2, 128, 128), BF),
            v((128, 128), BF),
            v((32, 128, 256), BF),
            v((16, 2, 128, 128), BF),
            v((16, 512, 384), BF),
            v((16, 32, 16, 128), BF),
            v((8, 32, 16, 128), BF),
            v((2, 32, 16, 128), BF),
            v((2, 2, 32, 16, 128), BF),
            v((32, 16, 128), BF),
            v((32, 16, 128), BF),
            v((16, 2, 16, 128), BF),
            v((32, 112, 384), BF),
        ]
        + [dma if s is None else dma(s) for s in sems],
        compiler_params=pltpu.CompilerParams(
            collective_id=0, has_side_effects=True, vmem_limit_bytes=60 * 1024 * 1024
        ),
        cost_estimate=pl.CostEstimate(flops=8 * 10**9, bytes_accessed=3 * 10**6, transcendentals=0),
    )(
        tokens.T,
        routes.reshape(1, 128),
        rw,
        hot_experts,
        w_gate,
        w_up,
        jnp.swapaxes(w_down, 1, 2),
        cotangent.T,
    )
    grad = jax.ShapeDtypeStruct((16, 112, 128), BF)
    out_t, gtok_t, gg, gu, gd = pl.pallas_call(
        finish,
        out_shape=(
            jax.ShapeDtypeStruct((224, 128), BF),
            jax.ShapeDtypeStruct((224, 128), BF),
            grad,
            grad,
            grad,
        ),
        in_specs=[vm, vm, vm, pl.BlockSpec(memory_space=pltpu.SMEM)],
        out_specs=(vm, vm, vm, vm, vm),
        scratch_shapes=[v((16, 112, 384), F32)],
        compiler_params=pltpu.CompilerParams(vmem_limit_bytes=32 * 1024 * 1024),
    )(rows, slots, rw, hot_experts)
    return out_t.T, gtok_t.T, gg, gu, jnp.swapaxes(gd, 1, 2)


def solution(mesh):
    placed = (
        P("ep", "grp"),
        P("ep", None),
        P("ep", None),
        P(),
        P(None, "ep", "grp"),
        P(None, "ep", "grp"),
        P(None, "grp", "ep"),
        P("ep", "grp"),
    )
    return jax.shard_map(
        layer,
        mesh=mesh,
        in_specs=placed,
        out_specs=(
            P("ep", "grp"),
            P("ep", "grp"),
            P(None, "ep", "grp"),
            P(None, "ep", "grp"),
            P(None, "grp", "ep"),
        ),
        check_vma=False,
    )
```

```python
import functools

import jax
import jax.numpy as jnp
from jax import lax
from jax.experimental import pallas as pl
from jax.experimental.pallas import tpu as pltpu
from jax.sharding import PartitionSpec as P

MESH = pl.DeviceIdType.MESH
BF = jnp.bfloat16
F32 = jnp.float32
NX, NY, NZ, NEP, NGRP = 4, 2, 16, 32, 16
LAST = (((1,), (1,)), ((), ()))
FIRST = (((0,), (0,)), ((), ()))


def mm(a, b, dims=(((1,), (0,)), ((), ()))):
    return lax.dot_general(a, b, dims, preferred_element_type=F32)


def body(
    tok_ref, routes_ref, rw_ref, hot_ref, wg_ref, wu_ref, wd_ref, cot_ref,
    rows_ref, slots_ref,
    src, meta, a1r, xb, er, et, wall, xe, se, pa, pb, ya, ra, rb, yb,
    ha, hb, he, qq, rc, rfar, rx, ry, fin, b2r, tot,
    w_sem, o_sem, a1_s, a1_q, m_s, m_q, a2_s, a2_q, g3_s, g3_q,
    ya_s, ya_q, ra_s, ra_q, rb_s, rb_q, yb_s, yb_q,
    hy_s, hy_q, ga_s, ga_q, gb_s, gb_q, gy_s, gy_q,
    c5_s, c5_q, f5_s, f5_q, x5_s, x5_q, y5_s, y5_q, b1_s, b1_q,
):
    g = lax.axis_index("grp")
    p = lax.axis_index("ep")
    x, yh, c = g // 4, (g // 2) % 2, g % 2
    y, z = p // NZ, p % NZ
    zr, zl = y * NZ + (z + 1) % NZ, y * NZ + (z + NZ - 1) % NZ
    py = (1 - y) * NZ + z
    gi = lambda xx, hh, cc: xx * 4 + hh * 2 + cc
    xr, xl = (x + 1) % NX, (x + 3) % NX
    gr, gl = gi(xr, yh, c), gi(xl, yh, c)
    gy, gc = gi(x, 1 - yh, c), gi(x, yh, 1 - c)

    def put(s, d, ss, rs, **dev):
        return pltpu.make_async_remote_copy(
            src_ref=s, dst_ref=d, send_sem=ss, recv_sem=rs, device_id=dev, device_id_type=MESH
        )

    w_in = [
        pltpu.make_async_copy(r, wall.at[:, pl.ds(0, 112), pl.ds(128 * i, 128)], w_sem.at[i])
        for i, r in enumerate((wg_ref, wu_ref, wd_ref))
    ]
    for cp in w_in:
        cp.start()

    tail = []

    barrier = pltpu.get_barrier_semaphore()

    def hello_g(i, _):
        pl.semaphore_signal(barrier, inc=1, device_id={"grp": (g + i) % NGRP}, device_id_type=MESH)
        return 0

    def hello_e(i, _):
        pl.semaphore_signal(barrier, inc=1, device_id={"ep": (p + i) % NEP}, device_id_type=MESH)
        return 0

    lax.fori_loop(1, NGRP, hello_g, 0)
    lax.fori_loop(1, NEP, hello_e, 0)

    def hello_b(i, _):
        t, h = i // 2, i % 2

        @pl.when(jnp.logical_not((t == g) & (2 * g + h == p)))
        def _():
            pl.semaphore_signal(barrier, inc=1, device_id={"grp": t, "ep": 2 * g + h}, device_id_type=MESH)

        return 0

    lax.fori_loop(0, NEP, hello_b, 0)

    slot_row = routes_ref[...]
    dz = (cot_ref[...].astype(F32) * rw_ref[...]).astype(BF)
    for h in range(2):
        src[0:7, h] = tok_ref[h * 112 : (h + 1) * 112, :].reshape(7, 16, 128)
        src[8:15, h] = dz[h * 112 : (h + 1) * 112, :].reshape(7, 16, 128)
    src[7] = jnp.zeros((2, 16, 128), BF)
    src[15] = jnp.zeros((2, 16, 128), BF)
    wall[:, 112:128, :] = jnp.zeros((16, 16, 384), BF)

    oh = jnp.where(lax.broadcasted_iota(jnp.int32, (NEP, 128), 0) == slot_row, 1.0, 0.0).astype(F32)
    upper = jnp.where(
        lax.broadcasted_iota(jnp.int32, (128, 128), 0) < lax.broadcasted_iota(jnp.int32, (128, 128), 1), 1.0, 0.0
    ).astype(BF)
    before = mm(oh.astype(BF), upper)
    pos_row = jnp.sum(oh * before, axis=0, keepdims=True)
    row_id = lax.broadcasted_iota(jnp.int32, (16, 128), 0)
    mrows = jnp.where(row_id == 0, slot_row.astype(F32), jnp.where(row_id == 1, pos_row, 0.0))
    meta[p] = mrows.astype(BF)

    pl.semaphore_wait(barrier, NGRP + NEP - 2 + NEP - jnp.where(p // 2 == g, 1, 0))

    a1 = lambda i, t: put(src.at[t], a1r.at[g], a1_s.at[i], a1_q.at[i], grp=t)
    mt = lambda i, t: put(meta.at[p], meta.at[p], m_s.at[i], m_q.at[i], ep=t)
    a2 = lambda i, t: put(a1r.at[t // 2, t % 2], xb.at[g, p], a2_s.at[i], a2_q.at[i], ep=t)

    def loop(lo, hi, f):
        def step(i, _):
            f(i)
            return 0

        lax.fori_loop(lo, hi, step, 0)

    def dots(lo, hi, f, unroll=1):
        def step(i, _):
            f(i)
            return 0

        lax.fori_loop(lo, hi, step, 0, unroll=unroll)

    loop(1, NGRP, lambda i: a1(i, (g + i) % NGRP).start())
    loop(1, NEP, lambda i: mt(i, (p + i) % NEP).start())
    a1r[g] = src[g]

    def a1_wait(i):
        f = (g + NGRP - i) % NGRP
        put(src.at[f], a1r.at[f], a1_s.at[i], a1_q.at[i], grp=f).wait_recv()

    loop(1, NGRP, a1_wait)
    loop(1, NEP, lambda i: a2(i, (p + i) % NEP).start())
    tail.append(lambda: loop(1, NGRP, lambda i: a1(i, (g + i) % NGRP).wait_send()))
    tail.append(lambda: loop(1, NEP, lambda i: mt(i, (p + i) % NEP).wait_send()))
    tail.append(lambda: loop(1, NEP, lambda i: a2(i, (p + i) % NEP).wait_send()))
    xb[g, p] = a1r[p // 2, p % 2]

    def m_wait(i):
        f = (p + NEP - i) % NEP
        put(meta.at[p], meta.at[f], m_s.at[i], m_q.at[i], ep=f).wait_recv()

    loop(1, NEP, m_wait)

    def build(q):
        m0 = meta[2 * q].astype(F32)
        m1 = meta[2 * q + 1].astype(F32)
        d0 = m0[0:1, :] * 16.0 + m0[1:2, :]
        d1 = m1[0:1, :] * 16.0 + m1[1:2, :] + 8.0
        row = jnp.concatenate([d0, d1], axis=1)
        irow = row.astype(jnp.int32)
        er[q] = jnp.where(
            lax.broadcasted_iota(jnp.int32, (512, 256), 0) == irow, 1.0, 0.0
        ).astype(BF)
        col = jnp.transpose(jnp.broadcast_to(row, (128, 256))).astype(jnp.int32)
        for b in range(4):
            et[q, :, 128 * b : 128 * (b + 1)] = jnp.where(
                lax.broadcasted_iota(jnp.int32, (256, 128), 1) + 128 * b == col, 1.0, 0.0
            ).astype(BF)

    def a2_wait(i):
        f = (p + NEP - i) % NEP
        put(a1r.at[0, 0], xb.at[g, f], a2_s.at[i], a2_q.at[i], ep=f).wait_recv()

    dots(0, 4, build)
    loop(1, NEP, a2_wait)

    def g3(chunk, i, t):
        return put(xb.at[chunk], xb.at[chunk], g3_s.at[i], g3_q.at[i], grp=t)

    g3(g, 0, gy).start()
    g3(g, 1 + yh, gr).start()
    g3(g, 3 + yh, gl).start()
    g3(g, 7 + yh, gc).start()
    dots(4, 8, build)
    g3(gy, 0, gy).wait_recv()
    g3(gy, 1 + (1 - yh), gr).start()
    g3(gy, 3 + (1 - yh), gl).start()
    g3(gy, 7 + (1 - yh), gc).start()
    dots(8, 12, build)
    xf = (x + 2) % NX
    g3(gi(xl, 0, c), 1, gr).wait_recv()
    g3(gi(xl, 0, c), 5, gr).start()
    g3(gi(xl, 0, c), 7 + 6, gc).start()
    g3(gi(xr, 1, c), 4, gl).wait_recv()
    g3(gi(xr, 1, c), 6, gl).start()
    g3(gi(xr, 1, c), 7 + 3, gc).start()
    g3(gi(xl, 1, c), 2, gr).wait_recv()
    g3(gi(xl, 1, c), 7 + 7, gc).start()
    g3(gi(xr, 0, c), 3, gl).wait_recv()
    g3(gi(xr, 0, c), 7 + 2, gc).start()
    dots(12, 16, build)
    for h in range(2):
        g3(gi(xf, h, c), 5 + h, gr).wait_recv()
        g3(gi(xf, h, c), 7 + 4 + h, gc).start()
    for dx in range(4):
        for h in range(2):
            g3(gi((x + dx) % NX, h, 1 - c), 7 + 2 * dx + h, gc).wait_recv()

    tail.append(lambda: loop(0, 15, lambda i: g3(g, i, gy).wait_send()))
    for cp in w_in:
        cp.wait()

    def spread(i):
        e = er[pl.ds(2 * i, 2)]
        tb = xb[:, pl.ds(4 * i, 4)]
        rows = []
        for j in range(2):
            t0, t1 = tb[:, 2 * j].reshape(256, 128), tb[:, 2 * j + 1].reshape(256, 128)
            rows.append(mm(e[j], jnp.concatenate([t0, t1], axis=1), LAST).astype(BF))
        xe[pl.ds(2 * i, 2)] = jnp.stack(rows)

    dots(0, 8, spread)

    def host(s):
        return jnp.where(s < 16, s, hot_ref[jnp.maximum(s - 16, 0)])

    def first_dots(i):
        rows = pl.ds(pl.multiple_of(i * 64, 64), 64)
        xd = xe[:, rows, :]
        gu, dn = [], []
        for j in range(4):
            w = wall[host(4 * i + j)]
            xj = xd[:, 16 * j : 16 * j + 16].reshape(256, 256)
            gu.append(mm(xj[:, 0:128], w[:, 0:256]).astype(BF).reshape(16, 16, 256))
            dn.append(mm(xj[:, 128:256], w[:, 256:384]).astype(BF).reshape(16, 16, 128))
        se[:, rows, 0:256] = jnp.concatenate(gu, axis=1)
        se[:, rows, 256:384] = jnp.concatenate(dn, axis=1)

    dots(0, 8, first_dots, 1)

    def squeeze(qs):
        both = [mm(et[q], se[q]).astype(BF) for q in qs]
        for q, cc in zip(qs, both):
            pa[pl.ds(2 * q, 2)] = cc[:, 0:256].reshape(2, 128, 256)
            pb[pl.ds(2 * (q % 8), 2), q // 8] = cc[:, 256:384].reshape(2, 128, 128)

    def ya_put(t):
        return put(pa.at[(1 - y) * NZ + t], ya.at[t], ya_s.at[t], ya_q.at[t], ep=py)

    def near(i):
        off = jnp.where(i % 2 == 1, 4 - (i + 1) // 2, 4 + i // 2)
        return (z // 2 + off) % 8

    def squeeze_far(i):
        zs = [near(2 * i + j) for j in range(2)]
        squeeze([(1 - y) * 8 + zp for zp in zs])
        for zp in zs:
            ya_put(2 * zp).start()
            ya_put(2 * zp + 1).start()

    dots(0, 4, squeeze_far)
    dots(0, 4, lambda i: squeeze([y * 8 + near(2 * i + j) for j in range(2)]))
    tail.append(lambda: loop(0, 16, lambda t: ya_put(t).wait_send()))

    def target(d, n, k):
        return (z + NZ + (n - k if d == 0 else k - n)) % NZ

    def a_put(d, k, t, j):
        r = pl.ds(64 * j, 64)
        return put(
            pa.at[y * NZ + t, r], ra.at[d, k, r], ra_s.at[d, k, j], ra_q.at[d, k, j], ep=zr if d == 0 else zl
        )

    def b_put(d, k, t, j):
        return put(
            pb.at[t, j], rb.at[d, k, j], rb_s.at[d, k, j], rb_q.at[d, k, j], ep=zr if d == 0 else zl
        )

    def a_step(d, n, k, j):
        t = target(d, n, k)
        r = pl.ds(64 * j, 64)
        if j == 0:
            ya_put(t).wait_recv()
        v = pa[y * NZ + t, r].astype(F32) + ya[t, r].astype(F32)
        if not (isinstance(k, int) and k == 0):
            a_put(d, k - 1, t, j).wait_recv()
            v = v + ra[d, k - 1, r].astype(F32)
        pa[y * NZ + t, r] = v.astype(BF)
        a_put(d, k, t, j).start()

    def b_step(d, n, k, j):
        t = target(d, n, k)
        if not (isinstance(k, int) and k == 0):
            b_put(d, k - 1, t, j).wait_recv()
            pb[t, j] = (pb[t, j].astype(F32) + rb[d, k - 1, j].astype(F32)).astype(BF)
        b_put(d, k, t, j).start()

    def all_steps(k):
        for j in range(2):
            b_step(0, 7, k, j)
            b_step(1, 8, k, j)
        for j in range(2):
            a_step(0, 8, k, j)
            a_step(1, 7, k, j)

    all_steps(0)
    loop(1, 7, all_steps)
    for j in range(2):
        b_step(1, 8, 7, j)
    for j in range(2):
        a_step(0, 8, 7, j)
    for j in range(2):
        b_put(0, 6, z, j).wait_recv()
        b_put(1, 7, z, j).wait_recv()
    ag_own = (
        pb[z, y].astype(F32) + rb[0, 6, y].astype(F32) + rb[1, 7, y].astype(F32)
    )
    pb[z, 1 - y] = (
        pb[z, 1 - y].astype(F32) + rb[0, 6, 1 - y].astype(F32) + rb[1, 7, 1 - y].astype(F32)
    ).astype(BF)
    yb_put = put(pb.at[z, 1 - y], yb, yb_s, yb_q, ep=py)
    yb_put.start()

    def ring_sends():
        for d in range(2):
            na, nb = (8, 7) if d == 0 else (7, 8)
            for j in range(2):
                loop(0, na, lambda k: a_put(d, k, z, j).wait_send())
                loop(0, nb, lambda k: b_put(d, k, z, j).wait_send())
        yb_put.wait_send()

    tail.append(ring_sends)
    ya_put(z).wait_recv()
    for j in range(2):
        a_put(1, 6, z, j).wait_recv()
        a_put(0, 7, z, j).wait_recv()
    pre = (
        pa[p].astype(F32) + ya[z].astype(F32) + ra[0, 7].astype(F32) + ra[1, 6].astype(F32)
    )
    gate, up = pre[:, 0:128], pre[:, 128:256]
    sg = jax.nn.sigmoid(gate)
    hb[z, y] = (gate * sg * up).astype(BF)
    hy_put = put(hb.at[z, y], hb.at[z, y], hy_s, hy_q, ep=py)
    hy_put.start()
    yb_put.wait_recv()
    ag = ag_own + yb[...].astype(F32)
    ha[p, :, 0:128] = (ag * up * sg * (1.0 + gate * (1.0 - sg))).astype(BF)
    ha[p, :, 128:256] = (ag * gate * sg).astype(BF)

    tail.append(hy_put.wait_send)
    def origin(d, k):
        return (z + NZ + (-k if d == 0 else k)) % NZ

    def ga_put(d, k, o):
        return put(
            ha.at[y * NZ + o], ha.at[y * NZ + o], ga_s.at[d, k], ga_q.at[d, k], ep=zr if d == 0 else zl
        )

    def gb_put(d, k, o):
        return put(hb.at[o], hb.at[o], gb_s.at[d, k], gb_q.at[d, k], ep=zr if d == 0 else zl)

    def gy_put(yy, o):
        return put(ha.at[yy * NZ + o], ha.at[yy * NZ + o], gy_s.at[o], gy_q.at[o], ep=py)

    ga_put(0, 0, z).start()
    ga_put(1, 0, z).start()
    gy_put(y, z).start()
    put(hb.at[z, 1 - y], hb.at[z, 1 - y], hy_s, hy_q, ep=py).wait_recv()
    gb_put(0, 0, z).start()
    gb_put(1, 0, z).start()

    def ga_step(d, k, more=True):
        o = origin(d, k)
        ga_put(d, k - 1, o).wait_recv()
        if more:
            ga_put(d, k, o).start()
        gy_put(y, o).start()

    def gb_step(d, k, more=True):
        o = origin(d, k)
        gb_put(d, k - 1, o).wait_recv()
        if more:
            gb_put(d, k, o).start()

    def gather_steps(k):
        ga_step(0, k)
        ga_step(1, k)
        gb_step(0, k)
        gb_step(1, k)

    loop(1, 7, gather_steps)
    ga_step(0, 7)
    ga_step(1, 7, False)
    gb_step(0, 7, False)
    gb_step(1, 7)
    ga_step(0, 8, False)
    gb_step(1, 8, False)

    def gather_sends():
        for d in range(2):
            na, nb = (8, 7) if d == 0 else (7, 8)
            loop(0, na, lambda k: ga_put(d, k, z).wait_send())
            loop(0, nb, lambda k: gb_put(d, k, z).wait_send())
        loop(0, 16, lambda o: gy_put(y, o).wait_send())

    tail.append(gather_sends)

    def spread_back(i):
        e = er[pl.ds(2 * i, 2)]
        hs = ha[pl.ds(4 * i, 4)]
        zp = (2 * i) % 8
        hd = hb[pl.ds(2 * zp, 4), (2 * i) // 8]
        rows = []
        for j in range(2):
            hq = jnp.concatenate(
                [hs[2 * j : 2 * j + 2].reshape(256, 256), hd[2 * j : 2 * j + 2].reshape(256, 128)], axis=1
            )
            rows.append(mm(e[j], hq).astype(BF))
        he[pl.ds(2 * i, 2)] = jnp.stack(rows)

    dots(0, 4, lambda i: spread_back(y * 4 + i))
    loop(0, 16, lambda o: gy_put(1 - y, o).wait_recv())
    dots(0, 4, lambda i: spread_back((1 - y) * 4 + i))

    def back_dots(i):
        rows = pl.ds(pl.multiple_of(i * 64, 64), 64)
        hs = he[:, rows, :]
        dn, gu = [], []
        for j in range(4):
            w = wall[host(4 * i + j)]
            hj = hs[:, 16 * j : 16 * j + 16].reshape(256, 384)
            dn.append(mm(hj[:, 256:384], w[:, 256:384], LAST).astype(BF).reshape(16, 16, 128))
            gu.append(mm(hj[:, 0:256], w[:, 0:256], LAST).astype(BF).reshape(16, 16, 128))
        se[:, rows, 0:128] = jnp.concatenate(dn, axis=1)
        se[:, rows, 128:256] = jnp.concatenate(gu, axis=1)

    dots(0, 8, back_dots, 1)

    def squeeze_out(i):
        t = et[pl.ds(2 * i, 2)]
        parts = se[pl.ds(2 * i, 2), :, 0:256]
        sums = jnp.stack([mm(t[j], parts[j]).astype(BF) for j in range(2)])
        sums = sums.reshape(4, 8, 16, 256)
        for b in range(8):
            qq[b, pl.ds(4 * i, 4)] = sums[:, b, :, 0:128]
            qq[8 + b, pl.ds(4 * i, 4)] = sums[:, b, :, 128:256]

    dots(0, 8, squeeze_out)

    def c5(dx, h):
        i = 2 * dx + h
        return put(qq.at[gi((x + dx) % NX, h, 1 - c)], rc.at[i], c5_s.at[i], c5_q.at[i], grp=gc)

    order = (2, 1, 3, 0)
    for dx in order:
        for h in range(2):
            c5(dx, h).start()

    def weight_dots(i):
        rows = pl.ds(pl.multiple_of(i * 64, 64), 64)
        xd = xe[:, rows, :]
        hs = he[:, rows, :]
        for j in range(4):
            xj = xd[:, 16 * j : 16 * j + 16].reshape(256, 256)
            hj = hs[:, 16 * j : 16 * j + 16].reshape(256, 384)
            tot[4 * i + j, :, 0:256] = mm(xj[:, 0:128], hj[:, 0:256], FIRST)[0:112].astype(BF)
            tot[4 * i + j, :, 256:384] = mm(xj[:, 128:256], hj[:, 256:384], FIRST)[0:112].astype(BF)

    w_out = []

    def weight_group(i):
        dots(2 * i, 2 * i + 2, weight_dots, 1)
        part = pl.ds(8 * i, 8)
        w_out.append(pltpu.make_async_copy(tot.at[part], slots_ref.at[part], o_sem.at[i]))
        w_out[-1].start()

    def addto(t, r):
        qq[t] = (qq[t].astype(F32) + r.astype(F32)).astype(BF)

    def with_core(dx, h):
        c5(dx, h).wait_recv()
        addto(gi((x + dx) % NX, h, c), rc[2 * dx + h])

    def f5(h):
        return put(qq.at[gi(xf, h, c)], rfar.at[h], f5_s.at[h], f5_q.at[h], grp=gr if h == 0 else gl)

    def x5(d, h):
        t = xr if d == 0 else xl
        return put(
            qq.at[gi(t, h, c)], rx.at[d, h], x5_s.at[d, h], x5_q.at[d, h], grp=gr if d == 0 else gl
        )

    for h in range(2):
        with_core(2, h)
        f5(h).start()
    with_core(1, 1)
    x5(0, 1).start()
    with_core(3, 0)
    x5(1, 0).start()
    with_core(1, 0)
    with_core(3, 1)
    f5(0).wait_recv()
    addto(gi(xr, 0, c), rfar[0])
    x5(0, 0).start()
    f5(1).wait_recv()
    addto(gi(xl, 1, c), rfar[1])
    x5(1, 1).start()
    weight_group(0)
    for h in range(2):
        c5(0, h).wait_recv()
        for d in range(2):
            x5(d, h).wait_recv()

    def own_sum(h):
        return (
            qq[gi(x, h, c)].astype(F32)
            + rc[h].astype(F32)
            + rx[0, h].astype(F32)
            + rx[1, h].astype(F32)
        )

    qq[gy] = own_sum(1 - yh).astype(BF)
    y5 = put(qq.at[gy], ry, y5_s, y5_q, grp=gy)
    y5.start()
    weight_group(1)
    mine = own_sum(yh)
    y5.wait_recv()
    fin[...] = (mine + ry[...].astype(F32)).astype(BF)

    def grp_sends():
        for h in range(2):
            for dx in range(4):
                c5(dx, h).wait_send()
            f5(h).wait_send()
            for d in range(2):
                x5(d, h).wait_send()
        y5.wait_send()

    tail.append(grp_sends)
    def b1(f):
        return put(fin.at[f], b2r.at[g, p % 2], b1_s.at[f], b1_q.at[2 * g + p % 2], grp=p // 2, ep=f)

    def b1_here(f):
        return (p // 2 == g) & (f == p)

    def b1_start(i):
        f = (p + i) % NEP

        @pl.when(jnp.logical_not(b1_here(f)))
        def _():
            b1(f).start()

    loop(0, NEP, b1_start)

    @pl.when(p // 2 == g)
    def _():
        b2r[g, p % 2] = fin[p]

    weight_group(2)
    weight_group(3)

    def b1_wait(i):
        t, h = i // 2, i % 2

        @pl.when(jnp.logical_not((t == g) & (2 * g + h == p)))
        def _():
            put(fin.at[0], b2r.at[t, h], b1_s.at[0], b1_q.at[i], grp=t, ep=2 * g + h).wait_recv()

    def b1_left(f):
        @pl.when(jnp.logical_not(b1_here(f)))
        def _():
            b1(f).wait_send()

    tail.append(lambda: loop(0, NEP, b1_left))
    loop(0, NEP, b1_wait)
    rows_out = pltpu.make_async_copy(b2r, rows_ref, o_sem.at[4])
    rows_out.start()
    tail.append(rows_out.wait)
    for grp4 in w_out:
        tail.append(grp4.wait)

    for wait in tail:
        wait()


def finish(rows_ref, slots_ref, rw_ref, hot_ref, out_ref, gtok_ref, gg_ref, gu_ref, gd_ref, acc):
    def base(e, _):
        acc[e] = slots_ref[e].astype(F32)
        return 0

    def more(j, _):
        e = hot_ref[j]
        acc[e] = acc[e] + slots_ref[16 + j].astype(F32)
        return 0

    def close(e, _):
        v = acc[e].astype(BF)
        gg_ref[e] = v[:, 0:128]
        gu_ref[e] = v[:, 128:256]
        gd_ref[e] = v[:, 256:384]
        return 0

    lax.fori_loop(0, 16, base, 0)
    lax.fori_loop(0, 16, more, 0)
    lax.fori_loop(0, 16, close, 0)
    for kind, ref in enumerate((out_ref, gtok_ref)):
        for h in range(2):
            part = rows_ref[kind * 8 : (kind + 1) * 8, h].reshape(128, 128).astype(F32)
            v = jnp.transpose(part)[0:112]
            if kind == 0:
                v = v * rw_ref[...]
            ref[h * 112 : (h + 1) * 112, :] = v.astype(BF)


def layer(tokens, routes, route_weights, hot_experts, w_gate, w_up, w_down, cotangent):
    v = pltpu.VMEM
    dma = pltpu.SemaphoreType.DMA
    vm = pl.BlockSpec(memory_space=pltpu.VMEM)
    anym = pl.BlockSpec(memory_space=pl.ANY)
    sems = [
        (3,), (5,), (16,), (16,), (32,), (32,), (32,), (32,), (15,), (15,),
        (16,), (16,), (2, 8, 2), (2, 8, 2), (2, 8, 2), (2, 8, 2), None, None,
        None, None, (2, 8), (2, 8), (2, 8), (2, 8), (16,), (16,),
        (8,), (8,), (2,), (2,), (2, 2), (2, 2), None, None, (32,), (32,),
    ]
    rw = route_weights.reshape(1, 128)
    rows, slots = pl.pallas_call(
        body,
        out_shape=(
            jax.ShapeDtypeStruct((16, 2, 16, 128), BF),
            jax.ShapeDtypeStruct((32, 112, 384), BF),
        ),
        in_specs=[vm, vm, vm, pl.BlockSpec(memory_space=pltpu.SMEM), anym, anym, anym, vm],
        out_specs=(anym, anym),
        scratch_shapes=[
            v((16, 2, 16, 128), BF),
            v((32, 16, 128), BF),
            v((16, 2, 16, 128), BF),
            v((16, 32, 16, 128), BF),
            v((16, 512, 256), BF),
            v((16, 256, 512), BF),
            v((16, 128, 384), BF),
            v((16, 512, 256), BF),
            v((16, 512, 384), BF),
            v((32, 128, 256), BF),
            v((16, 2, 128, 128), BF),
            v((16, 128, 256), BF),
            v((2, 8, 128, 256), BF),
            v((2, 8, 2, 128, 128), BF),
            v((128, 128), BF),
            v((32, 128, 256), BF),
            v((16, 2, 128, 128), BF),
            v((16, 512, 384), BF),
            v((16, 32, 16, 128), BF),
            v((8, 32, 16, 128), BF),
            v((2, 32, 16, 128), BF),
            v((2, 2, 32, 16, 128), BF),
            v((32, 16, 128), BF),
            v((32, 16, 128), BF),
            v((16, 2, 16, 128), BF),
            v((32, 112, 384), BF),
        ]
        + [dma if s is None else dma(s) for s in sems],
        compiler_params=pltpu.CompilerParams(
            collective_id=0, has_side_effects=True, vmem_limit_bytes=60 * 1024 * 1024
        ),
        cost_estimate=pl.CostEstimate(flops=8 * 10**9, bytes_accessed=3 * 10**6, transcendentals=0),
    )(
        tokens.T,
        routes.reshape(1, 128),
        rw,
        hot_experts,
        w_gate,
        w_up,
        jnp.swapaxes(w_down, 1, 2),
        cotangent.T,
    )
    grad = jax.ShapeDtypeStruct((16, 112, 128), BF)
    out_t, gtok_t, gg, gu, gd = pl.pallas_call(
        finish,
        out_shape=(
            jax.ShapeDtypeStruct((224, 128), BF),
            jax.ShapeDtypeStruct((224, 128), BF),
            grad,
            grad,
            grad,
        ),
        in_specs=[vm, vm, vm, pl.BlockSpec(memory_space=pltpu.SMEM)],
        out_specs=(vm, vm, vm, vm, vm),
        scratch_shapes=[v((16, 112, 384), F32)],
        compiler_params=pltpu.CompilerParams(vmem_limit_bytes=32 * 1024 * 1024),
    )(rows, slots, rw, hot_experts)
    return out_t.T, gtok_t.T, gg, gu, jnp.swapaxes(gd, 1, 2)


def solution(mesh):
    placed = (
        P("ep", "grp"),
        P("ep", None),
        P("ep", None),
        P(),
        P(None, "ep", "grp"),
        P(None, "ep", "grp"),
        P(None, "grp", "ep"),
        P("ep", "grp"),
    )
    return jax.shard_map(
        layer,
        mesh=mesh,
        in_specs=placed,
        out_specs=(
            P("ep", "grp"),
            P("ep", "grp"),
            P(None, "ep", "grp"),
            P(None, "ep", "grp"),
            P(None, "grp", "ep"),
        ),
        check_vma=False,
    )
```

```python
import functools

import jax
import jax.numpy as jnp
from jax import lax
from jax.experimental import pallas as pl
from jax.experimental.pallas import tpu as pltpu
from jax.sharding import PartitionSpec as P

MESH = pl.DeviceIdType.MESH
BF = jnp.bfloat16
F32 = jnp.float32
NX, NY, NZ, NEP, NGRP = 4, 2, 16, 32, 16
LAST = (((1,), (1,)), ((), ()))
FIRST = (((0,), (0,)), ((), ()))


def mm(a, b, dims=(((1,), (0,)), ((), ()))):
    return lax.dot_general(a, b, dims, preferred_element_type=F32)


def body(
    tok_ref, routes_ref, rw_ref, hot_ref, wg_ref, wu_ref, wd_ref, cot_ref,
    rows_ref, slots_ref,
    src, meta, a1r, xb, er, et, wall, xe, se, pa, pb, ya, ra, rb, yb,
    ha, hb, he, qq, rc, rfar, rx, ry, fin, b2r, tot,
    w_sem, o_sem, a1_s, a1_q, m_s, m_q, a2_s, a2_q, g3_s, g3_q,
    ya_s, ya_q, ra_s, ra_q, rb_s, rb_q, yb_s, yb_q,
    hy_s, hy_q, ga_s, ga_q, gb_s, gb_q, gy_s, gy_q,
    c5_s, c5_q, f5_s, f5_q, x5_s, x5_q, y5_s, y5_q, b1_s, b1_q,
):
    g = lax.axis_index("grp")
    p = lax.axis_index("ep")
    x, yh, c = g // 4, (g // 2) % 2, g % 2
    y, z = p // NZ, p % NZ
    zr, zl = y * NZ + (z + 1) % NZ, y * NZ + (z + NZ - 1) % NZ
    py = (1 - y) * NZ + z
    gi = lambda xx, hh, cc: xx * 4 + hh * 2 + cc
    xr, xl = (x + 1) % NX, (x + 3) % NX
    gr, gl = gi(xr, yh, c), gi(xl, yh, c)
    gy, gc = gi(x, 1 - yh, c), gi(x, yh, 1 - c)

    def put(s, d, ss, rs, **dev):
        return pltpu.make_async_remote_copy(
            src_ref=s, dst_ref=d, send_sem=ss, recv_sem=rs, device_id=dev, device_id_type=MESH
        )

    w_in = [
        pltpu.make_async_copy(r, wall.at[:, pl.ds(0, 112), pl.ds(128 * i, 128)], w_sem.at[i])
        for i, r in enumerate((wg_ref, wu_ref, wd_ref))
    ]
    for cp in w_in:
        cp.start()

    tail = []

    barrier = pltpu.get_barrier_semaphore()

    def hello_g(i, _):
        pl.semaphore_signal(barrier, inc=1, device_id={"grp": (g + i) % NGRP}, device_id_type=MESH)
        return 0

    def hello_e(i, _):
        pl.semaphore_signal(barrier, inc=1, device_id={"ep": (p + i) % NEP}, device_id_type=MESH)
        return 0

    lax.fori_loop(1, NGRP, hello_g, 0)
    lax.fori_loop(1, NEP, hello_e, 0)

    def hello_b(i, _):
        t, h = i // 2, i % 2

        @pl.when(jnp.logical_not((t == g) & (2 * g + h == p)))
        def _():
            pl.semaphore_signal(barrier, inc=1, device_id={"grp": t, "ep": 2 * g + h}, device_id_type=MESH)

        return 0

    lax.fori_loop(0, NEP, hello_b, 0)

    slot_row = routes_ref[...]
    dz = (cot_ref[...].astype(F32) * rw_ref[...]).astype(BF)
    for h in range(2):
        src[0:7, h] = tok_ref[h * 112 : (h + 1) * 112, :].reshape(7, 16, 128)
        src[8:15, h] = dz[h * 112 : (h + 1) * 112, :].reshape(7, 16, 128)
    src[7] = jnp.zeros((2, 16, 128), BF)
    src[15] = jnp.zeros((2, 16, 128), BF)
    wall[:, 112:128, :] = jnp.zeros((16, 16, 384), BF)

    oh = jnp.where(lax.broadcasted_iota(jnp.int32, (NEP, 128), 0) == slot_row, 1.0, 0.0).astype(F32)
    upper = jnp.where(
        lax.broadcasted_iota(jnp.int32, (128, 128), 0) < lax.broadcasted_iota(jnp.int32, (128, 128), 1), 1.0, 0.0
    ).astype(BF)
    before = mm(oh.astype(BF), upper)
    pos_row = jnp.sum(oh * before, axis=0, keepdims=True)
    row_id = lax.broadcasted_iota(jnp.int32, (16, 128), 0)
    mrows = jnp.where(row_id == 0, slot_row.astype(F32), jnp.where(row_id == 1, pos_row, 0.0))
    meta[p] = mrows.astype(BF)

    pl.semaphore_wait(barrier, NGRP + NEP - 2 + NEP - jnp.where(p // 2 == g, 1, 0))

    a1 = lambda i, t: put(src.at[t], a1r.at[g], a1_s.at[i], a1_q.at[i], grp=t)
    mt = lambda i, t: put(meta.at[p], meta.at[p], m_s.at[i], m_q.at[i], ep=t)

    def place(at, yy, zz):
        r = (zz + 2 * NZ - 2 * (at // 2 + 3)) % NZ
        return r // 8, yy, r % 8

    def a2(i, t):
        return put(
            a1r.at[t // 2, t % 2], xb.at[(g,) + place(t % NZ, y, z)], a2_s.at[i], a2_q.at[i], ep=t
        )

    def zpair(half, j):
        return (z // 2 + 3 + 4 * half + j) % 8

    def pair_block(q):
        return ((q // 4) % 2) * NZ + 2 * zpair(q // 8, q % 4)

    def loop(lo, hi, f):
        def step(i, _):
            f(i)
            return 0

        lax.fori_loop(lo, hi, step, 0)

    def dots(lo, hi, f, unroll=1):
        def step(i, _):
            f(i)
            return 0

        lax.fori_loop(lo, hi, step, 0, unroll=unroll)

    loop(1, NGRP, lambda i: a1(i, (g + i) % NGRP).start())
    loop(1, NEP, lambda i: mt(i, (p + i) % NEP).start())
    a1r[g] = src[g]

    def a1_wait(i):
        f = (g + NGRP - i) % NGRP
        put(src.at[f], a1r.at[f], a1_s.at[i], a1_q.at[i], grp=f).wait_recv()

    loop(1, NGRP, a1_wait)
    loop(1, NEP, lambda i: a2(i, (p + i) % NEP).start())
    tail.append(lambda: loop(1, NGRP, lambda i: a1(i, (g + i) % NGRP).wait_send()))
    tail.append(lambda: loop(1, NEP, lambda i: mt(i, (p + i) % NEP).wait_send()))
    tail.append(lambda: loop(1, NEP, lambda i: a2(i, (p + i) % NEP).wait_send()))
    xb[(g,) + place(z, y, z)] = a1r[p // 2, p % 2]

    def m_wait(i):
        f = (p + NEP - i) % NEP
        put(meta.at[p], meta.at[f], m_s.at[i], m_q.at[i], ep=f).wait_recv()

    loop(1, NEP, m_wait)

    def build(q):
        m0 = meta[pair_block(q)].astype(F32)
        m1 = meta[pair_block(q) + 1].astype(F32)
        d0 = m0[0:1, :] * 16.0 + m0[1:2, :]
        d1 = m1[0:1, :] * 16.0 + m1[1:2, :] + 8.0
        row = jnp.concatenate([d0, d1], axis=1)
        irow = row.astype(jnp.int32)
        er[q] = jnp.where(
            lax.broadcasted_iota(jnp.int32, (512, 256), 0) == irow, 1.0, 0.0
        ).astype(BF)
        col = jnp.transpose(jnp.broadcast_to(row, (128, 256))).astype(jnp.int32)
        for b in range(4):
            et[q, :, 128 * b : 128 * (b + 1)] = jnp.where(
                lax.broadcasted_iota(jnp.int32, (256, 128), 1) + 128 * b == col, 1.0, 0.0
            ).astype(BF)

    def a2_wait(i):
        f = (p + NEP - i) % NEP
        put(a1r.at[0, 0], xb.at[(g,) + place(z, f // NZ, f % NZ)], a2_s.at[i], a2_q.at[i], ep=f).wait_recv()

    dots(0, 4, build)
    loop(1, NEP, a2_wait)

    def g3(chunk, i, t, k):
        return put(xb.at[chunk, k], xb.at[chunk, k], g3_s.at[k, i], g3_q.at[k, i], grp=t)

    xf = (x + 2) % NX

    def g_own(k):
        g3(g, 1 + yh, gr, k).start()
        g3(g, 3 + yh, gl, k).start()
        g3(g, 7 + yh, gc, k).start()

    def g_pair(k):
        g3(gy, 0, gy, k).wait_recv()
        g3(gy, 1 + (1 - yh), gr, k).start()
        g3(gy, 3 + (1 - yh), gl, k).start()
        g3(gy, 7 + (1 - yh), gc, k).start()

    def g_relay(k):
        g3(gi(xl, 0, c), 1, gr, k).wait_recv()
        g3(gi(xl, 0, c), 5, gr, k).start()
        g3(gi(xl, 0, c), 7 + 6, gc, k).start()
        g3(gi(xr, 1, c), 4, gl, k).wait_recv()
        g3(gi(xr, 1, c), 6, gl, k).start()
        g3(gi(xr, 1, c), 7 + 3, gc, k).start()
        g3(gi(xl, 1, c), 2, gr, k).wait_recv()
        g3(gi(xl, 1, c), 7 + 7, gc, k).start()
        g3(gi(xr, 0, c), 3, gl, k).wait_recv()
        g3(gi(xr, 0, c), 7 + 2, gc, k).start()

    def g_far(k):
        for h in range(2):
            g3(gi(xf, h, c), 5 + h, gr, k).wait_recv()
            g3(gi(xf, h, c), 7 + 4 + h, gc, k).start()

    def g_core(k):
        for dx in range(4):
            for h in range(2):
                g3(gi((x + dx) % NX, h, 1 - c), 7 + 2 * dx + h, gc, k).wait_recv()

    def spread(i):
        e = er[pl.ds(2 * i, 2)]
        k, yy, m = i // 4, (i // 2) % 2, i % 2
        tb = xb[:, k, yy, pl.ds(4 * m, 4)]
        rows = []
        for j in range(2):
            t0, t1 = tb[:, 2 * j].reshape(256, 128), tb[:, 2 * j + 1].reshape(256, 128)
            rows.append(mm(e[j], jnp.concatenate([t0, t1], axis=1), LAST).astype(BF))
        xe[pl.ds(2 * i, 2)] = jnp.stack(rows)

    def host(s):
        return jnp.where(s < 16, s, hot_ref[jnp.maximum(s - 16, 0)])

    def first_dots(k):
        part = pl.ds(8 * k, 8)

        def four(i):
            rows = pl.ds(pl.multiple_of(i * 64, 64), 64)
            xd = xe[part, rows, :]
            gu, dn = [], []
            for j in range(4):
                w = wall[host(4 * i + j)]
                xj = xd[:, 16 * j : 16 * j + 16].reshape(128, 256)
                gu.append(mm(xj[:, 0:128], w[:, 0:256]).astype(BF).reshape(8, 16, 256))
                dn.append(mm(xj[:, 128:256], w[:, 256:384]).astype(BF).reshape(8, 16, 128))
            se[part, rows, 0:256] = jnp.concatenate(gu, axis=1)
            se[part, rows, 256:384] = jnp.concatenate(dn, axis=1)

        dots(0, 8, four, 1)

    def squeeze(k, yy, i):
        js = (1 - i, 2 + i) if k == 0 else (3 - i, i)
        both = [mm(et[8 * k + 4 * yy + j], se[8 * k + 4 * yy + j]).astype(BF) for j in js]
        for j, cc in zip(js, both):
            zp = zpair(k, j)
            pa[pl.ds(yy * NZ + 2 * zp, 2)] = cc[:, 0:256].reshape(2, 128, 256)
            pb[pl.ds(2 * zp, 2), yy] = cc[:, 256:384].reshape(2, 128, 128)
        return js

    def squeezes(k):
        def far(i):
            for j in squeeze(k, 1 - y, i):
                ya_put(2 * zpair(k, j)).start()
                ya_put(2 * zpair(k, j) + 1).start()

        loop(0, 2, far)
        loop(0, 2, lambda i: squeeze(k, y, i))

    def ya_put(t):
        return put(pa.at[(1 - y) * NZ + t], ya.at[t], ya_s.at[t], ya_q.at[t], ep=py)

    tail.append(lambda: loop(0, 16, lambda t: ya_put(t).wait_send()))

    def target(d, n, k):
        return (z + NZ + (n - k if d == 0 else k - n)) % NZ

    def a_put(d, k, t, j):
        r = pl.ds(64 * j, 64)
        return put(
            pa.at[y * NZ + t, r], ra.at[d, k, r], ra_s.at[d, k, j], ra_q.at[d, k, j], ep=zr if d == 0 else zl
        )

    def b_put(d, k, t, j):
        return put(
            pb.at[t, j], rb.at[d, k, j], rb_s.at[d, k, j], rb_q.at[d, k, j], ep=zr if d == 0 else zl
        )

    def a_step(d, n, k, j):
        t = target(d, n, k)
        r = pl.ds(64 * j, 64)
        if j == 0:
            ya_put(t).wait_recv()
        v = pa[y * NZ + t, r].astype(F32) + ya[t, r].astype(F32)
        if not (isinstance(k, int) and k == 0):
            a_put(d, k - 1, t, j).wait_recv()
            v = v + ra[d, k - 1, r].astype(F32)
        pa[y * NZ + t, r] = v.astype(BF)
        a_put(d, k, t, j).start()

    def b_step(d, n, k, j):
        t = target(d, n, k)
        if not (isinstance(k, int) and k == 0):
            b_put(d, k - 1, t, j).wait_recv()
            pb[t, j] = (pb[t, j].astype(F32) + rb[d, k - 1, j].astype(F32)).astype(BF)
        b_put(d, k, t, j).start()

    def all_steps(k):
        for j in range(2):
            b_step(0, 7, k, j)
            b_step(1, 8, k, j)
        for j in range(2):
            a_step(0, 8, k, j)
            a_step(1, 7, k, j)

    g3(g, 0, gy, 0).start()
    g3(g, 0, gy, 1).start()
    g_own(0)
    dots(4, 10, build)
    g_pair(0)
    g_own(1)
    dots(10, 16, build)
    g_relay(0)
    for cp in w_in:
        cp.wait()
    g_pair(1)
    g_far(0)
    for k in range(2):
        tail.append(lambda k=k: loop(0, 15, lambda i: g3(g, i, gy, k).wait_send()))
    g_core(0)
    dots(0, 4, spread)
    g_relay(1)
    first_dots(0)
    g_far(1)
    squeezes(0)
    all_steps(0)
    g_core(1)
    dots(4, 8, spread)
    first_dots(1)

    def ring_and_rest(k):
        all_steps(k)

        @pl.when(k == 1)
        def _():
            squeezes(1)

    loop(1, 7, ring_and_rest)
    for j in range(2):
        b_step(1, 8, 7, j)
    for j in range(2):
        a_step(0, 8, 7, j)
    for j in range(2):
        b_put(0, 6, z, j).wait_recv()
        b_put(1, 7, z, j).wait_recv()
    ag_own = (
        pb[z, y].astype(F32) + rb[0, 6, y].astype(F32) + rb[1, 7, y].astype(F32)
    )
    pb[z, 1 - y] = (
        pb[z, 1 - y].astype(F32) + rb[0, 6, 1 - y].astype(F32) + rb[1, 7, 1 - y].astype(F32)
    ).astype(BF)
    yb_put = put(pb.at[z, 1 - y], yb, yb_s, yb_q, ep=py)
    yb_put.start()

    def ring_sends():
        for d in range(2):
            na, nb = (8, 7) if d == 0 else (7, 8)
            for j in range(2):
                loop(0, na, lambda k: a_put(d, k, z, j).wait_send())
                loop(0, nb, lambda k: b_put(d, k, z, j).wait_send())
        yb_put.wait_send()

    tail.append(ring_sends)
    ya_put(z).wait_recv()
    for j in range(2):
        a_put(1, 6, z, j).wait_recv()
        a_put(0, 7, z, j).wait_recv()
    pre = (
        pa[p].astype(F32) + ya[z].astype(F32) + ra[0, 7].astype(F32) + ra[1, 6].astype(F32)
    )
    gate, up = pre[:, 0:128], pre[:, 128:256]
    sg = jax.nn.sigmoid(gate)
    hb[z, y] = (gate * sg * up).astype(BF)
    hy_put = put(hb.at[z, y], hb.at[z, y], hy_s, hy_q, ep=py)
    hy_put.start()
    yb_put.wait_recv()
    ag = ag_own + yb[...].astype(F32)
    ha[p, :, 0:128] = (ag * up * sg * (1.0 + gate * (1.0 - sg))).astype(BF)
    ha[p, :, 128:256] = (ag * gate * sg).astype(BF)

    tail.append(hy_put.wait_send)
    def origin(d, k):
        return (z + NZ + (-k if d == 0 else k)) % NZ

    def ga_put(d, k, o):
        return put(
            ha.at[y * NZ + o], ha.at[y * NZ + o], ga_s.at[d, k], ga_q.at[d, k], ep=zr if d == 0 else zl
        )

    def gb_put(d, k, o):
        return put(hb.at[o], hb.at[o], gb_s.at[d, k], gb_q.at[d, k], ep=zr if d == 0 else zl)

    def gy_put(yy, o):
        return put(ha.at[yy * NZ + o], ha.at[yy * NZ + o], gy_s.at[o], gy_q.at[o], ep=py)

    ga_put(0, 0, z).start()
    ga_put(1, 0, z).start()
    gy_put(y, z).start()
    put(hb.at[z, 1 - y], hb.at[z, 1 - y], hy_s, hy_q, ep=py).wait_recv()
    gb_put(0, 0, z).start()
    gb_put(1, 0, z).start()

    def ga_step(d, k, more=True):
        o = origin(d, k)
        ga_put(d, k - 1, o).wait_recv()
        if more:
            ga_put(d, k, o).start()
        gy_put(y, o).start()

    def gb_step(d, k, more=True):
        o = origin(d, k)
        gb_put(d, k - 1, o).wait_recv()
        if more:
            gb_put(d, k, o).start()

    def gather_steps(k):
        ga_step(0, k)
        ga_step(1, k)
        gb_step(0, k)
        gb_step(1, k)

    def gather_sends():
        for d in range(2):
            na, nb = (8, 7) if d == 0 else (7, 8)
            loop(0, na, lambda k: ga_put(d, k, z).wait_send())
            loop(0, nb, lambda k: gb_put(d, k, z).wait_send())
        loop(0, 16, lambda o: gy_put(y, o).wait_send())

    tail.append(gather_sends)

    def spread_back(k):
        def two(n):
            yy, m = n // 2, n % 2
            i = 8 * k + 2 * n
            e = er[pl.ds(i, 2)]
            rows = []
            for j in range(2):
                zp = zpair(k, 2 * m + j)
                hq = jnp.concatenate(
                    [
                        ha[pl.ds(yy * NZ + 2 * zp, 2)].reshape(256, 256),
                        hb[pl.ds(2 * zp, 2), yy].reshape(256, 128),
                    ],
                    axis=1,
                )
                rows.append(mm(e[j], hq).astype(BF))
            he[pl.ds(i, 2)] = jnp.stack(rows)

        loop(0, 4, two)

    def gy_wait(k):
        for j in range(4):
            gy_put(1 - y, 2 * zpair(k, j)).wait_recv()
            gy_put(1 - y, 2 * zpair(k, j) + 1).wait_recv()

    def back_dots(k):
        part = pl.ds(8 * k, 8)

        def four(i):
            rows = pl.ds(pl.multiple_of(i * 64, 64), 64)
            hs = he[part, rows, :]
            dn, gu = [], []
            for j in range(4):
                w = wall[host(4 * i + j)]
                hj = hs[:, 16 * j : 16 * j + 16].reshape(128, 384)
                dn.append(mm(hj[:, 256:384], w[:, 256:384], LAST).astype(BF).reshape(8, 16, 128))
                gu.append(mm(hj[:, 0:256], w[:, 0:256], LAST).astype(BF).reshape(8, 16, 128))
            se[part, rows, 0:128] = jnp.concatenate(dn, axis=1)
            se[part, rows, 128:256] = jnp.concatenate(gu, axis=1)

        dots(0, 8, four, 1)

    def squeeze_out(k):
        def two(i):
            r = 8 * k + 2 * i
            t = et[pl.ds(r, 2)]
            parts = se[pl.ds(r, 2), :, 0:256]
            sums = jnp.stack([mm(t[j], parts[j]).astype(BF) for j in range(2)])
            sums = sums.reshape(4, 8, 16, 256)
            m = pl.ds(4 * (i % 2), 4)
            for b in range(8):
                qq[b, k, i // 2, m] = sums[:, b, :, 0:128]
                qq[8 + b, k, i // 2, m] = sums[:, b, :, 128:256]

        dots(0, 4, two, 1)

    def c5(dx, h, k):
        i = 2 * dx + h
        return put(
            qq.at[gi((x + dx) % NX, h, 1 - c), k], rc.at[k, i], c5_s.at[k, i], c5_q.at[k, i], grp=gc
        )

    def core_sends(k):
        for dx in (2, 1, 3, 0):
            for h in range(2):
                c5(dx, h, k).start()

    def weight_dots(i):
        rows = pl.ds(pl.multiple_of(i * 64, 64), 64)
        xd = xe[:, rows, :]
        hs = he[:, rows, :]
        for j in range(4):
            xj = xd[:, 16 * j : 16 * j + 16].reshape(256, 256)
            hj = hs[:, 16 * j : 16 * j + 16].reshape(256, 384)
            tot[4 * i + j, :, 0:256] = mm(xj[:, 0:128], hj[:, 0:256], FIRST)[0:112].astype(BF)
            tot[4 * i + j, :, 256:384] = mm(xj[:, 128:256], hj[:, 256:384], FIRST)[0:112].astype(BF)

    w_out = []

    def weight_group(i):
        dots(2 * i, 2 * i + 2, weight_dots, 1)
        part = pl.ds(8 * i, 8)
        w_out.append(pltpu.make_async_copy(tot.at[part], slots_ref.at[part], o_sem.at[i]))
        w_out[-1].start()

    def addto(t, k, r):
        qq[t, k] = (qq[t, k].astype(F32) + r.astype(F32)).astype(BF)

    def with_core(dx, h, k):
        c5(dx, h, k).wait_recv()
        addto(gi((x + dx) % NX, h, c), k, rc[k, 2 * dx + h])

    def f5(h, k):
        return put(
            qq.at[gi(xf, h, c), k], rfar.at[k, h], f5_s.at[k, h], f5_q.at[k, h], grp=gr if h == 0 else gl
        )

    def x5(d, h, k):
        t = xr if d == 0 else xl
        return put(
            qq.at[gi(t, h, c), k],
            rx.at[k, d, h],
            x5_s.at[k, d, h],
            x5_q.at[k, d, h],
            grp=gr if d == 0 else gl,
        )

    def x_first(k):
        for h in range(2):
            with_core(2, h, k)
            f5(h, k).start()
        with_core(1, 1, k)
        x5(0, 1, k).start()
        with_core(3, 0, k)
        x5(1, 0, k).start()
        with_core(1, 0, k)
        with_core(3, 1, k)

    def x_second(k):
        f5(0, k).wait_recv()
        addto(gi(xr, 0, c), k, rfar[k, 0])
        x5(0, 0, k).start()
        f5(1, k).wait_recv()
        addto(gi(xl, 1, c), k, rfar[k, 1])
        x5(1, 1, k).start()

    def own_sum(h, k):
        return (
            qq[gi(x, h, c), k].astype(F32)
            + rc[k, h].astype(F32)
            + rx[k, 0, h].astype(F32)
            + rx[k, 1, h].astype(F32)
        )

    def y5(k):
        return put(qq.at[gy, k], ry.at[k], y5_s.at[k], y5_q.at[k], grp=gy)

    def y_sends(k):
        for h in range(2):
            c5(0, h, k).wait_recv()
            for d in range(2):
                x5(d, h, k).wait_recv()
        qq[gy, k] = own_sum(1 - yh, k).astype(BF)
        y5(k).start()

    def y_close(k):
        y5(k).wait_recv()
        fin[k] = (own_sum(yh, k) + ry[k].astype(F32)).astype(BF)

    def grp_sends():
        for k in range(2):
            for h in range(2):
                for dx in range(4):
                    c5(dx, h, k).wait_send()
                f5(h, k).wait_send()
                for d in range(2):
                    x5(d, h, k).wait_send()
            y5(k).wait_send()

    tail.append(grp_sends)

    def b1(f):
        return put(
            fin.at[place(z, f // NZ, f % NZ)],
            b2r.at[g, p % 2],
            b1_s.at[f],
            b1_q.at[2 * g + p % 2],
            grp=p // 2,
            ep=f,
        )

    def b1_here(f):
        return (p // 2 == g) & (f == p)

    def b1_start(i):
        f = ((i // 8) % 2) * NZ + (2 * zpair(i // 16, 0) + i % 8) % NZ

        @pl.when(jnp.logical_not(b1_here(f)))
        def _():
            b1(f).start()

    loop(1, 6, gather_steps)
    gy_wait(1)
    spread_back(1)
    gather_steps(6)
    back_dots(1)
    ga_step(0, 7)
    ga_step(1, 7, False)
    gb_step(0, 7, False)
    gb_step(1, 7)
    squeeze_out(1)
    core_sends(1)
    ga_step(0, 8, False)
    gb_step(1, 8, False)
    x_first(1)
    gy_wait(0)
    spread_back(0)
    x_second(1)
    back_dots(0)
    squeeze_out(0)
    core_sends(0)
    y_sends(1)
    weight_group(0)
    x_first(0)
    y_close(1)
    loop(16, 32, b1_start)

    @pl.when(p // 2 == g)
    def _():
        b2r[g, p % 2] = fin[place(z, y, z)]

    weight_group(1)
    x_second(0)
    weight_group(2)
    y_sends(0)
    weight_group(3)
    y_close(0)
    loop(0, 16, b1_start)

    def b1_wait(i):
        t, h = i // 2, i % 2

        @pl.when(jnp.logical_not((t == g) & (2 * g + h == p)))
        def _():
            put(fin.at[0, 0, 0], b2r.at[t, h], b1_s.at[0], b1_q.at[i], grp=t, ep=2 * g + h).wait_recv()

    def b1_left(f):
        @pl.when(jnp.logical_not(b1_here(f)))
        def _():
            b1(f).wait_send()

    tail.append(lambda: loop(0, NEP, b1_left))
    loop(0, NEP, b1_wait)
    rows_out = pltpu.make_async_copy(b2r, rows_ref, o_sem.at[4])
    rows_out.start()
    tail.append(rows_out.wait)
    for grp4 in w_out:
        tail.append(grp4.wait)

    for wait in tail:
        wait()


def finish(rows_ref, slots_ref, rw_ref, hot_ref, out_ref, gtok_ref, gg_ref, gu_ref, gd_ref, acc):
    def base(e, _):
        acc[e] = slots_ref[e].astype(F32)
        return 0

    def more(j, _):
        e = hot_ref[j]
        acc[e] = acc[e] + slots_ref[16 + j].astype(F32)
        return 0

    def close(e, _):
        v = acc[e].astype(BF)
        gg_ref[e] = v[:, 0:128]
        gu_ref[e] = v[:, 128:256]
        gd_ref[e] = v[:, 256:384]
        return 0

    lax.fori_loop(0, 16, base, 0)
    lax.fori_loop(0, 16, more, 0)
    lax.fori_loop(0, 16, close, 0)
    for kind, ref in enumerate((out_ref, gtok_ref)):
        for h in range(2):
            part = rows_ref[kind * 8 : (kind + 1) * 8, h].reshape(128, 128).astype(F32)
            v = jnp.transpose(part)[0:112]
            if kind == 0:
                v = v * rw_ref[...]
            ref[h * 112 : (h + 1) * 112, :] = v.astype(BF)


def layer(tokens, routes, route_weights, hot_experts, w_gate, w_up, w_down, cotangent):
    v = pltpu.VMEM
    dma = pltpu.SemaphoreType.DMA
    vm = pl.BlockSpec(memory_space=pltpu.VMEM)
    anym = pl.BlockSpec(memory_space=pl.ANY)
    sems = [
        (3,), (5,), (16,), (16,), (32,), (32,), (32,), (32,), (2, 15), (2, 15),
        (16,), (16,), (2, 8, 2), (2, 8, 2), (2, 8, 2), (2, 8, 2), None, None,
        None, None, (2, 8), (2, 8), (2, 8), (2, 8), (16,), (16,),
        (2, 8), (2, 8), (2, 2), (2, 2), (2, 2, 2), (2, 2, 2), (2,), (2,), (32,), (32,),
    ]
    rw = route_weights.reshape(1, 128)
    rows, slots = pl.pallas_call(
        body,
        out_shape=(
            jax.ShapeDtypeStruct((16, 2, 16, 128), BF),
            jax.ShapeDtypeStruct((32, 112, 384), BF),
        ),
        in_specs=[vm, vm, vm, pl.BlockSpec(memory_space=pltpu.SMEM), anym, anym, anym, vm],
        out_specs=(anym, anym),
        scratch_shapes=[
            v((16, 2, 16, 128), BF),
            v((32, 16, 128), BF),
            v((16, 2, 16, 128), BF),
            v((16, 2, 2, 8, 16, 128), BF),
            v((16, 512, 256), BF),
            v((16, 256, 512), BF),
            v((16, 128, 384), BF),
            v((16, 512, 256), BF),
            v((16, 512, 384), BF),
            v((32, 128, 256), BF),
            v((16, 2, 128, 128), BF),
            v((16, 128, 256), BF),
            v((2, 8, 128, 256), BF),
            v((2, 8, 2, 128, 128), BF),
            v((128, 128), BF),
            v((32, 128, 256), BF),
            v((16, 2, 128, 128), BF),
            v((16, 512, 384), BF),
            v((16, 2, 2, 8, 16, 128), BF),
            v((2, 8, 2, 8, 16, 128), BF),
            v((2, 2, 2, 8, 16, 128), BF),
            v((2, 2, 2, 2, 8, 16, 128), BF),
            v((2, 2, 8, 16, 128), BF),
            v((2, 2, 8, 16, 128), BF),
            v((16, 2, 16, 128), BF),
            v((32, 112, 384), BF),
        ]
        + [dma if s is None else dma(s) for s in sems],
        compiler_params=pltpu.CompilerParams(
            collective_id=0, has_side_effects=True, vmem_limit_bytes=60 * 1024 * 1024
        ),
        cost_estimate=pl.CostEstimate(flops=8 * 10**9, bytes_accessed=3 * 10**6, transcendentals=0),
    )(
        tokens.T,
        routes.reshape(1, 128),
        rw,
        hot_experts,
        w_gate,
        w_up,
        jnp.swapaxes(w_down, 1, 2),
        cotangent.T,
    )
    grad = jax.ShapeDtypeStruct((16, 112, 128), BF)
    out_t, gtok_t, gg, gu, gd = pl.pallas_call(
        finish,
        out_shape=(
            jax.ShapeDtypeStruct((224, 128), BF),
            jax.ShapeDtypeStruct((224, 128), BF),
            grad,
            grad,
            grad,
        ),
        in_specs=[vm, vm, vm, pl.BlockSpec(memory_space=pltpu.SMEM)],
        out_specs=(vm, vm, vm, vm, vm),
        scratch_shapes=[v((16, 112, 384), F32)],
        compiler_params=pltpu.CompilerParams(vmem_limit_bytes=32 * 1024 * 1024),
    )(rows, slots, rw, hot_experts)
    return out_t.T, gtok_t.T, gg, gu, jnp.swapaxes(gd, 1, 2)


def solution(mesh):
    placed = (
        P("ep", "grp"),
        P("ep", None),
        P("ep", None),
        P(),
        P(None, "ep", "grp"),
        P(None, "ep", "grp"),
        P(None, "grp", "ep"),
        P("ep", "grp"),
    )
    return jax.shard_map(
        layer,
        mesh=mesh,
        in_specs=placed,
        out_specs=(
            P("ep", "grp"),
            P("ep", "grp"),
            P(None, "ep", "grp"),
            P(None, "ep", "grp"),
            P(None, "grp", "ep"),
        ),
        check_vma=False,
    )
```

```python
import functools

import jax
import jax.numpy as jnp
from jax import lax
from jax.experimental import pallas as pl
from jax.experimental.pallas import tpu as pltpu
from jax.sharding import PartitionSpec as P

MESH = pl.DeviceIdType.MESH
BF = jnp.bfloat16
F32 = jnp.float32
NX, NY, NZ, NEP, NGRP = 4, 2, 16, 32, 16
LAST = (((1,), (1,)), ((), ()))
FIRST = (((0,), (0,)), ((), ()))


def mm(a, b, dims=(((1,), (0,)), ((), ()))):
    return lax.dot_general(a, b, dims, preferred_element_type=F32)


def body(
    tok_ref, routes_ref, rw_ref, hot_ref, wg_ref, wu_ref, wd_ref, cot_ref,
    rows_ref, slots_ref,
    src, meta, a1r, xb, er, et, wall, xe, se, pa, pb, ya, ra, rb, yb,
    ha, hb, he, qq, rc, rfar, rx, ry, fin, b2r, tot,
    w_sem, o_sem, a1_s, a1_q, m_s, m_q, a2_s, a2_q, g3_s, g3_q,
    ya_s, ya_q, ra_s, ra_q, rb_s, rb_q, yb_s, yb_q,
    hy_s, hy_q, ga_s, ga_q, gb_s, gb_q, gy_s, gy_q,
    c5_s, c5_q, f5_s, f5_q, x5_s, x5_q, y5_s, y5_q, b1_s, b1_q,
):
    g = lax.axis_index("grp")
    p = lax.axis_index("ep")
    x, yh, c = g // 4, (g // 2) % 2, g % 2
    y, z = p // NZ, p % NZ
    zr, zl = y * NZ + (z + 1) % NZ, y * NZ + (z + NZ - 1) % NZ
    py = (1 - y) * NZ + z
    gi = lambda xx, hh, cc: xx * 4 + hh * 2 + cc
    xr, xl = (x + 1) % NX, (x + 3) % NX
    gr, gl = gi(xr, yh, c), gi(xl, yh, c)
    gy, gc = gi(x, 1 - yh, c), gi(x, yh, 1 - c)

    def put(s, d, ss, rs, **dev):
        return pltpu.make_async_remote_copy(
            src_ref=s, dst_ref=d, send_sem=ss, recv_sem=rs, device_id=dev, device_id_type=MESH
        )

    w_in = [
        pltpu.make_async_copy(r, wall.at[:, pl.ds(0, 112), pl.ds(128 * i, 128)], w_sem.at[i])
        for i, r in enumerate((wg_ref, wu_ref, wd_ref))
    ]
    for cp in w_in:
        cp.start()

    tail = []

    barrier = pltpu.get_barrier_semaphore()

    def hello_g(i, _):
        pl.semaphore_signal(barrier, inc=1, device_id={"grp": (g + i) % NGRP}, device_id_type=MESH)
        return 0

    def hello_e(i, _):
        pl.semaphore_signal(barrier, inc=1, device_id={"ep": (p + i) % NEP}, device_id_type=MESH)
        return 0

    lax.fori_loop(1, NGRP, hello_g, 0)
    lax.fori_loop(1, NEP, hello_e, 0)

    def hello_b(i, _):
        t, h = i // 2, i % 2

        @pl.when(jnp.logical_not((t == g) & (2 * g + h == p)))
        def _():
            pl.semaphore_signal(barrier, inc=1, device_id={"grp": t, "ep": 2 * g + h}, device_id_type=MESH)

        return 0

    lax.fori_loop(0, NEP, hello_b, 0)

    slot_row = routes_ref[...]
    dz = (cot_ref[...].astype(F32) * rw_ref[...]).astype(BF)
    for h in range(2):
        src[0:7, h] = tok_ref[h * 112 : (h + 1) * 112, :].reshape(7, 16, 128)
        src[8:15, h] = dz[h * 112 : (h + 1) * 112, :].reshape(7, 16, 128)
    src[7] = jnp.zeros((2, 16, 128), BF)
    src[15] = jnp.zeros((2, 16, 128), BF)
    wall[:, 112:128, :] = jnp.zeros((16, 16, 384), BF)

    oh = jnp.where(lax.broadcasted_iota(jnp.int32, (NEP, 128), 0) == slot_row, 1.0, 0.0).astype(F32)
    upper = jnp.where(
        lax.broadcasted_iota(jnp.int32, (128, 128), 0) < lax.broadcasted_iota(jnp.int32, (128, 128), 1), 1.0, 0.0
    ).astype(BF)
    before = mm(oh.astype(BF), upper)
    pos_row = jnp.sum(oh * before, axis=0, keepdims=True)
    row_id = lax.broadcasted_iota(jnp.int32, (16, 128), 0)
    mrows = jnp.where(row_id == 0, slot_row.astype(F32), jnp.where(row_id == 1, pos_row, 0.0))
    meta[p] = mrows.astype(BF)

    pl.semaphore_wait(barrier, NGRP + NEP - 2 + NEP - jnp.where(p // 2 == g, 1, 0))

    a1 = lambda i, t: put(src.at[t], a1r.at[g], a1_s.at[i], a1_q.at[i], grp=t)
    mt = lambda i, t: put(meta.at[p], meta.at[p], m_s.at[i], m_q.at[i], ep=t)

    def place(at, yy, zz):
        r = (zz + 2 * NZ - 2 * (at // 2 + 3)) % NZ
        return r // 8, yy, r % 8

    def a2(i, t):
        return put(
            a1r.at[t // 2, t % 2], xb.at[(g,) + place(t % NZ, y, z)], a2_s.at[i], a2_q.at[i], ep=t
        )

    def zpair(half, j):
        return (z // 2 + 3 + 4 * half + j) % 8

    def pair_block(q):
        return ((q // 4) % 2) * NZ + 2 * zpair(q // 8, q % 4)

    def loop(lo, hi, f):
        def step(i, _):
            f(i)
            return 0

        lax.fori_loop(lo, hi, step, 0)

    def dots(lo, hi, f, unroll=1):
        def step(i, _):
            f(i)
            return 0

        lax.fori_loop(lo, hi, step, 0, unroll=unroll)

    loop(1, NGRP, lambda i: a1(i, (g + i) % NGRP).start())
    loop(1, NEP, lambda i: mt(i, (p + i) % NEP).start())
    a1r[g] = src[g]

    def a1_wait(i):
        f = (g + NGRP - i) % NGRP
        put(src.at[f], a1r.at[f], a1_s.at[i], a1_q.at[i], grp=f).wait_recv()

    loop(1, NGRP, a1_wait)
    loop(1, NEP, lambda i: a2(i, (p + i) % NEP).start())
    tail.append(lambda: loop(1, NGRP, lambda i: a1(i, (g + i) % NGRP).wait_send()))
    tail.append(lambda: loop(1, NEP, lambda i: mt(i, (p + i) % NEP).wait_send()))
    tail.append(lambda: loop(1, NEP, lambda i: a2(i, (p + i) % NEP).wait_send()))
    xb[(g,) + place(z, y, z)] = a1r[p // 2, p % 2]

    def m_wait(i):
        f = (p + NEP - i) % NEP
        put(meta.at[p], meta.at[f], m_s.at[i], m_q.at[i], ep=f).wait_recv()

    loop(1, NEP, m_wait)

    def build(q):
        m0 = meta[pair_block(q)].astype(F32)
        m1 = meta[pair_block(q) + 1].astype(F32)
        d0 = m0[0:1, :] * 16.0 + m0[1:2, :]
        d1 = m1[0:1, :] * 16.0 + m1[1:2, :] + 8.0
        row = jnp.concatenate([d0, d1], axis=1)
        irow = row.astype(jnp.int32)
        er[q] = jnp.where(
            lax.broadcasted_iota(jnp.int32, (512, 256), 0) == irow, 1.0, 0.0
        ).astype(BF)
        col = jnp.transpose(jnp.broadcast_to(row, (128, 256))).astype(jnp.int32)
        for b in range(4):
            et[q, :, 128 * b : 128 * (b + 1)] = jnp.where(
                lax.broadcasted_iota(jnp.int32, (256, 128), 1) + 128 * b == col, 1.0, 0.0
            ).astype(BF)

    def a2_wait(i):
        f = (p + NEP - i) % NEP
        put(a1r.at[0, 0], xb.at[(g,) + place(z, f // NZ, f % NZ)], a2_s.at[i], a2_q.at[i], ep=f).wait_recv()

    dots(0, 4, build)
    loop(1, NEP, a2_wait)

    def g3(chunk, i, t, k):
        return put(xb.at[chunk, k], xb.at[chunk, k], g3_s.at[k, i], g3_q.at[k, i], grp=t)

    xf = (x + 2) % NX

    def g_own(k):
        g3(g, 1 + yh, gr, k).start()
        g3(g, 3 + yh, gl, k).start()
        g3(g, 7 + yh, gc, k).start()

    def g_pair(k):
        g3(gy, 0, gy, k).wait_recv()
        g3(gy, 1 + (1 - yh), gr, k).start()
        g3(gy, 3 + (1 - yh), gl, k).start()
        g3(gy, 7 + (1 - yh), gc, k).start()

    def g_relay(k):
        g3(gi(xl, 0, c), 1, gr, k).wait_recv()
        g3(gi(xl, 0, c), 5, gr, k).start()
        g3(gi(xl, 0, c), 7 + 6, gc, k).start()
        g3(gi(xr, 1, c), 4, gl, k).wait_recv()
        g3(gi(xr, 1, c), 6, gl, k).start()
        g3(gi(xr, 1, c), 7 + 3, gc, k).start()
        g3(gi(xl, 1, c), 2, gr, k).wait_recv()
        g3(gi(xl, 1, c), 7 + 7, gc, k).start()
        g3(gi(xr, 0, c), 3, gl, k).wait_recv()
        g3(gi(xr, 0, c), 7 + 2, gc, k).start()

    def g_far(k):
        for h in range(2):
            g3(gi(xf, h, c), 5 + h, gr, k).wait_recv()
            g3(gi(xf, h, c), 7 + 4 + h, gc, k).start()

    def g_core(k):
        for dx in range(4):
            for h in range(2):
                g3(gi((x + dx) % NX, h, 1 - c), 7 + 2 * dx + h, gc, k).wait_recv()

    def spread(i):
        e = er[pl.ds(2 * i, 2)]
        k, yy, m = i // 4, (i // 2) % 2, i % 2
        tb = xb[:, k, yy, pl.ds(4 * m, 4)]
        rows = []
        for j in range(2):
            t0, t1 = tb[:, 2 * j].reshape(256, 128), tb[:, 2 * j + 1].reshape(256, 128)
            rows.append(mm(e[j], jnp.concatenate([t0, t1], axis=1), LAST).astype(BF))
        xe[pl.ds(2 * i, 2)] = jnp.stack(rows)

    def host(s):
        return jnp.where(s < 16, s, hot_ref[jnp.maximum(s - 16, 0)])

    def first_dots(k):
        part = pl.ds(8 * k, 8)

        def four(i):
            rows = pl.ds(pl.multiple_of(i * 64, 64), 64)
            xd = xe[part, rows, :]
            gu, dn = [], []
            for j in range(4):
                w = wall[host(4 * i + j)]
                xj = xd[:, 16 * j : 16 * j + 16].reshape(128, 256)
                gu.append(mm(xj[:, 0:128], w[:, 0:256]).astype(BF).reshape(8, 16, 256))
                dn.append(mm(xj[:, 128:256], w[:, 256:384]).astype(BF).reshape(8, 16, 128))
            se[part, rows, 0:256] = jnp.concatenate(gu, axis=1)
            se[part, rows, 256:384] = jnp.concatenate(dn, axis=1)

        dots(0, 8, four, 1)

    def squeeze(k, yy, i):
        js = (1 - i, 2 + i) if k == 0 else (3 - i, i)
        both = [mm(et[8 * k + 4 * yy + j], se[8 * k + 4 * yy + j]).astype(BF) for j in js]
        for j, cc in zip(js, both):
            zp = zpair(k, j)
            pa[pl.ds(yy * NZ + 2 * zp, 2)] = cc[:, 0:256].reshape(2, 128, 256)
            pb[pl.ds(2 * zp, 2), yy] = cc[:, 256:384].reshape(2, 128, 128)
        return js

    def squeezes(k):
        def far(i):
            for j in squeeze(k, 1 - y, i):
                ya_put(2 * zpair(k, j)).start()
                ya_put(2 * zpair(k, j) + 1).start()

        loop(0, 2, far)
        loop(0, 2, lambda i: squeeze(k, y, i))

    def ya_put(t):
        return put(pa.at[(1 - y) * NZ + t], ya.at[t], ya_s.at[t], ya_q.at[t], ep=py)

    tail.append(lambda: loop(0, 16, lambda t: ya_put(t).wait_send()))

    def target(d, n, k):
        return (z + NZ + (n - k if d == 0 else k - n)) % NZ

    def a_put(d, k, t, j):
        r = pl.ds(64 * j, 64)
        return put(
            pa.at[y * NZ + t, r], ra.at[d, k, r], ra_s.at[d, k, j], ra_q.at[d, k, j], ep=zr if d == 0 else zl
        )

    def b_put(d, k, t, j):
        return put(
            pb.at[t, j], rb.at[d, k, j], rb_s.at[d, k, j], rb_q.at[d, k, j], ep=zr if d == 0 else zl
        )

    def a_step(d, n, k, j):
        t = target(d, n, k)
        r = pl.ds(64 * j, 64)
        if j == 0:
            ya_put(t).wait_recv()
        v = pa[y * NZ + t, r].astype(F32) + ya[t, r].astype(F32)
        if not (isinstance(k, int) and k == 0):
            a_put(d, k - 1, t, j).wait_recv()
            v = v + ra[d, k - 1, r].astype(F32)
        pa[y * NZ + t, r] = v.astype(BF)
        a_put(d, k, t, j).start()

    def b_step(d, n, k, j):
        t = target(d, n, k)
        if not (isinstance(k, int) and k == 0):
            b_put(d, k - 1, t, j).wait_recv()
            pb[t, j] = (pb[t, j].astype(F32) + rb[d, k - 1, j].astype(F32)).astype(BF)
        b_put(d, k, t, j).start()

    def all_steps(k):
        for j in range(2):
            b_step(0, 7, k, j)
            b_step(1, 8, k, j)
        for j in range(2):
            a_step(0, 8, k, j)
            a_step(1, 7, k, j)

    g3(g, 0, gy, 0).start()
    g3(g, 0, gy, 1).start()
    g_own(0)
    dots(4, 10, build)
    g_pair(0)
    g_own(1)
    dots(10, 16, build)
    g_relay(0)
    for cp in w_in:
        cp.wait()
    g_pair(1)
    g_far(0)
    for k in range(2):
        tail.append(lambda k=k: loop(0, 15, lambda i: g3(g, i, gy, k).wait_send()))
    g_core(0)
    dots(0, 4, spread)
    g_relay(1)
    first_dots(0)
    squeezes(0)
    all_steps(0)
    g_far(1)
    g_core(1)
    dots(4, 8, spread)
    first_dots(1)

    def ring_and_rest(k):
        all_steps(k)

        @pl.when(k == 1)
        def _():
            squeezes(1)

        for at, waits in ((3, tail[0:3]), (4, tail[3:])):

            @pl.when(k == at)
            def _(waits=waits):
                for wait in waits:
                    wait()

    loop(1, 7, ring_and_rest)
    tail.clear()
    for j in range(2):
        b_step(1, 8, 7, j)
    for j in range(2):
        a_step(0, 8, 7, j)
    for j in range(2):
        b_put(0, 6, z, j).wait_recv()
        b_put(1, 7, z, j).wait_recv()
    ag_own = (
        pb[z, y].astype(F32) + rb[0, 6, y].astype(F32) + rb[1, 7, y].astype(F32)
    )
    pb[z, 1 - y] = (
        pb[z, 1 - y].astype(F32) + rb[0, 6, 1 - y].astype(F32) + rb[1, 7, 1 - y].astype(F32)
    ).astype(BF)
    yb_put = put(pb.at[z, 1 - y], yb, yb_s, yb_q, ep=py)
    yb_put.start()

    def ring_sends():
        for d in range(2):
            na, nb = (8, 7) if d == 0 else (7, 8)
            for j in range(2):
                loop(0, na, lambda k: a_put(d, k, z, j).wait_send())
                loop(0, nb, lambda k: b_put(d, k, z, j).wait_send())
        yb_put.wait_send()

    tail.append(ring_sends)
    ya_put(z).wait_recv()
    for j in range(2):
        a_put(1, 6, z, j).wait_recv()
        a_put(0, 7, z, j).wait_recv()
    pre = (
        pa[p].astype(F32) + ya[z].astype(F32) + ra[0, 7].astype(F32) + ra[1, 6].astype(F32)
    )
    gate, up = pre[:, 0:128], pre[:, 128:256]
    sg = jax.nn.sigmoid(gate)
    hb[z, y] = (gate * sg * up).astype(BF)
    hy_put = put(hb.at[z, y], hb.at[z, y], hy_s, hy_q, ep=py)
    hy_put.start()
    yb_put.wait_recv()
    ag = ag_own + yb[...].astype(F32)
    ha[p, :, 0:128] = (ag * up * sg * (1.0 + gate * (1.0 - sg))).astype(BF)
    ha[p, :, 128:256] = (ag * gate * sg).astype(BF)

    tail.append(hy_put.wait_send)
    def origin(d, k):
        return (z + NZ + (-k if d == 0 else k)) % NZ

    def ga_put(d, k, o):
        return put(
            ha.at[y * NZ + o], ha.at[y * NZ + o], ga_s.at[d, k], ga_q.at[d, k], ep=zr if d == 0 else zl
        )

    def gb_put(d, k, o):
        return put(hb.at[o], hb.at[o], gb_s.at[d, k], gb_q.at[d, k], ep=zr if d == 0 else zl)

    def gy_put(yy, o):
        return put(ha.at[yy * NZ + o], ha.at[yy * NZ + o], gy_s.at[o], gy_q.at[o], ep=py)

    ga_put(0, 0, z).start()
    ga_put(1, 0, z).start()
    gy_put(y, z).start()
    put(hb.at[z, 1 - y], hb.at[z, 1 - y], hy_s, hy_q, ep=py).wait_recv()
    gb_put(0, 0, z).start()
    gb_put(1, 0, z).start()

    def ga_step(d, k, more=True):
        o = origin(d, k)
        ga_put(d, k - 1, o).wait_recv()
        if more:
            ga_put(d, k, o).start()
        gy_put(y, o).start()

    def gb_step(d, k, more=True):
        o = origin(d, k)
        gb_put(d, k - 1, o).wait_recv()
        if more:
            gb_put(d, k, o).start()

    def gather_steps(k):
        ga_step(0, k)
        ga_step(1, k)
        gb_step(0, k)
        gb_step(1, k)

    def gather_sends():
        for d in range(2):
            na, nb = (8, 7) if d == 0 else (7, 8)
            loop(0, na, lambda k: ga_put(d, k, z).wait_send())
            loop(0, nb, lambda k: gb_put(d, k, z).wait_send())
        loop(0, 16, lambda o: gy_put(y, o).wait_send())

    def spread_back(k):
        def two(n):
            yy, m = n // 2, n % 2
            i = 8 * k + 2 * n
            e = er[pl.ds(i, 2)]
            rows = []
            for j in range(2):
                zp = zpair(k, 2 * m + j)
                hq = jnp.concatenate(
                    [
                        ha[pl.ds(yy * NZ + 2 * zp, 2)].reshape(256, 256),
                        hb[pl.ds(2 * zp, 2), yy].reshape(256, 128),
                    ],
                    axis=1,
                )
                rows.append(mm(e[j], hq).astype(BF))
            he[pl.ds(i, 2)] = jnp.stack(rows)

        loop(0, 4, two)

    def gy_wait(k):
        for j in range(4):
            gy_put(1 - y, 2 * zpair(k, j)).wait_recv()
            gy_put(1 - y, 2 * zpair(k, j) + 1).wait_recv()

    def back_dots(k):
        part = pl.ds(8 * k, 8)

        def four(i):
            rows = pl.ds(pl.multiple_of(i * 64, 64), 64)
            hs = he[part, rows, :]
            dn, gu = [], []
            for j in range(4):
                w = wall[host(4 * i + j)]
                hj = hs[:, 16 * j : 16 * j + 16].reshape(128, 384)
                dn.append(mm(hj[:, 256:384], w[:, 256:384], LAST).astype(BF).reshape(8, 16, 128))
                gu.append(mm(hj[:, 0:256], w[:, 0:256], LAST).astype(BF).reshape(8, 16, 128))
            se[part, rows, 0:128] = jnp.concatenate(dn, axis=1)
            se[part, rows, 128:256] = jnp.concatenate(gu, axis=1)

        dots(0, 8, four, 1)

    def squeeze_out(k):
        def two(i):
            r = 8 * k + 2 * i
            t = et[pl.ds(r, 2)]
            parts = se[pl.ds(r, 2), :, 0:256]
            sums = jnp.stack([mm(t[j], parts[j]).astype(BF) for j in range(2)])
            sums = sums.reshape(4, 8, 16, 256)
            m = pl.ds(4 * (i % 2), 4)
            for b in range(8):
                qq[b, k, i // 2, m] = sums[:, b, :, 0:128]
                qq[8 + b, k, i // 2, m] = sums[:, b, :, 128:256]

        dots(0, 4, two, 1)

    def c5(dx, h, k):
        i = 2 * dx + h
        return put(
            qq.at[gi((x + dx) % NX, h, 1 - c), k], rc.at[k, i], c5_s.at[k, i], c5_q.at[k, i], grp=gc
        )

    def core_sends(k):
        for dx in (2, 1, 3, 0):
            for h in range(2):
                c5(dx, h, k).start()

    def weight_dots(i):
        rows = pl.ds(pl.multiple_of(i * 64, 64), 64)
        xd = xe[:, rows, :]
        hs = he[:, rows, :]
        for j in range(4):
            xj = xd[:, 16 * j : 16 * j + 16].reshape(256, 256)
            hj = hs[:, 16 * j : 16 * j + 16].reshape(256, 384)
            tot[4 * i + j, :, 0:256] = mm(xj[:, 0:128], hj[:, 0:256], FIRST)[0:112].astype(BF)
            tot[4 * i + j, :, 256:384] = mm(xj[:, 128:256], hj[:, 256:384], FIRST)[0:112].astype(BF)

    w_out = []

    def weight_group(i):
        dots(2 * i, 2 * i + 2, weight_dots, 1)
        part = pl.ds(8 * i, 8)
        w_out.append(pltpu.make_async_copy(tot.at[part], slots_ref.at[part], o_sem.at[i]))
        w_out[-1].start()

    def addto(t, k, r):
        qq[t, k] = (qq[t, k].astype(F32) + r.astype(F32)).astype(BF)

    def with_core(dx, h, k):
        c5(dx, h, k).wait_recv()
        addto(gi((x + dx) % NX, h, c), k, rc[k, 2 * dx + h])

    def f5(h, k):
        return put(
            qq.at[gi(xf, h, c), k], rfar.at[k, h], f5_s.at[k, h], f5_q.at[k, h], grp=gr if h == 0 else gl
        )

    def x5(d, h, k):
        t = xr if d == 0 else xl
        return put(
            qq.at[gi(t, h, c), k],
            rx.at[k, d, h],
            x5_s.at[k, d, h],
            x5_q.at[k, d, h],
            grp=gr if d == 0 else gl,
        )

    def x_first(k):
        for h in range(2):
            with_core(2, h, k)
            f5(h, k).start()
        with_core(1, 1, k)
        x5(0, 1, k).start()
        with_core(3, 0, k)
        x5(1, 0, k).start()
        with_core(1, 0, k)
        with_core(3, 1, k)

    def x_second(k):
        f5(0, k).wait_recv()
        addto(gi(xr, 0, c), k, rfar[k, 0])
        x5(0, 0, k).start()
        f5(1, k).wait_recv()
        addto(gi(xl, 1, c), k, rfar[k, 1])
        x5(1, 1, k).start()

    def own_sum(h, k):
        return (
            qq[gi(x, h, c), k].astype(F32)
            + rc[k, h].astype(F32)
            + rx[k, 0, h].astype(F32)
            + rx[k, 1, h].astype(F32)
        )

    def y5(k):
        return put(qq.at[gy, k], ry.at[k], y5_s.at[k], y5_q.at[k], grp=gy)

    def y_sends(k):
        for h in range(2):
            c5(0, h, k).wait_recv()
            for d in range(2):
                x5(d, h, k).wait_recv()
        qq[gy, k] = own_sum(1 - yh, k).astype(BF)
        y5(k).start()

    def y_close(k):
        y5(k).wait_recv()
        fin[k] = (own_sum(yh, k) + ry[k].astype(F32)).astype(BF)

    def grp_sends():
        for k in range(2):
            for h in range(2):
                for dx in range(4):
                    c5(dx, h, k).wait_send()
                f5(h, k).wait_send()
                for d in range(2):
                    x5(d, h, k).wait_send()
            y5(k).wait_send()

    def b1(f):
        return put(
            fin.at[place(z, f // NZ, f % NZ)],
            b2r.at[g, p % 2],
            b1_s.at[f],
            b1_q.at[2 * g + p % 2],
            grp=p // 2,
            ep=f,
        )

    def b1_here(f):
        return (p // 2 == g) & (f == p)

    def b1_start(i):
        f = ((i // 8) % 2) * NZ + (2 * zpair(i // 16, 0) + i % 8) % NZ

        @pl.when(jnp.logical_not(b1_here(f)))
        def _():
            b1(f).start()

    early, tail[:] = tail[:], []

    def gather_and_rest(k):
        gather_steps(k)

        @pl.when(k == 2)
        def _():
            for wait in early:
                wait()

    loop(1, 6, gather_and_rest)
    gy_wait(1)
    spread_back(1)
    gather_steps(6)
    back_dots(1)
    ga_step(0, 7)
    ga_step(1, 7, False)
    gb_step(0, 7, False)
    gb_step(1, 7)
    squeeze_out(1)
    core_sends(1)
    ga_step(0, 8, False)
    gb_step(1, 8, False)
    x_first(1)
    gy_wait(0)
    spread_back(0)
    x_second(1)
    back_dots(0)
    squeeze_out(0)
    core_sends(0)
    gather_sends()
    y_sends(1)
    weight_group(0)
    x_first(0)
    y_close(1)
    loop(16, 32, b1_start)

    @pl.when(p // 2 == g)
    def _():
        b2r[g, p % 2] = fin[place(z, y, z)]

    weight_group(1)
    x_second(0)
    weight_group(2)
    y_sends(0)
    weight_group(3)
    y_close(0)
    loop(0, 16, b1_start)

    def b1_wait(i):
        t, h = i // 2, i % 2

        @pl.when(jnp.logical_not((t == g) & (2 * g + h == p)))
        def _():
            put(fin.at[0, 0, 0], b2r.at[t, h], b1_s.at[0], b1_q.at[i], grp=t, ep=2 * g + h).wait_recv()

    def b1_left(f):
        @pl.when(jnp.logical_not(b1_here(f)))
        def _():
            b1(f).wait_send()

    grp_sends()
    loop(0, NEP, b1_left)
    loop(0, NEP, b1_wait)
    rows_out = pltpu.make_async_copy(b2r, rows_ref, o_sem.at[4])
    rows_out.start()
    tail.append(rows_out.wait)
    for grp4 in w_out:
        tail.append(grp4.wait)

    for wait in tail:
        wait()


def finish(
    rows_ref, slots_ref, rw_ref, hot_ref, out_ref, gtok_ref, gg_ref, gu_ref, gd_ref, rows_v, slots_v, acc, sem
):
    rows_in = pltpu.make_async_copy(rows_ref, rows_v, sem.at[0])
    low = pltpu.make_async_copy(slots_ref.at[pl.ds(0, 16)], slots_v.at[pl.ds(0, 16)], sem.at[1])
    high = pltpu.make_async_copy(slots_ref.at[pl.ds(16, 16)], slots_v.at[pl.ds(16, 16)], sem.at[2])
    rows_in.start()
    low.start()
    high.start()

    def base(e, _):
        acc[e] = slots_v[e].astype(F32)
        return 0

    def more(j, _):
        e = hot_ref[j]
        acc[e] = acc[e] + slots_v[16 + j].astype(F32)
        return 0

    def close(e, _):
        v = acc[e].astype(BF)
        gg_ref[e] = v[:, 0:128]
        gu_ref[e] = v[:, 128:256]
        gd_ref[e] = v[:, 256:384]
        return 0

    rows_in.wait()
    for kind, ref in enumerate((out_ref, gtok_ref)):
        for h in range(2):
            part = rows_v[kind * 8 : (kind + 1) * 8, h].reshape(128, 128).astype(F32)
            v = jnp.transpose(part)[0:112]
            if kind == 0:
                v = v * rw_ref[...]
            ref[h * 112 : (h + 1) * 112, :] = v.astype(BF)
    low.wait()
    lax.fori_loop(0, 16, base, 0)
    high.wait()
    lax.fori_loop(0, 16, more, 0)
    lax.fori_loop(0, 16, close, 0)


def layer(tokens, routes, route_weights, hot_experts, w_gate, w_up, w_down, cotangent):
    v = pltpu.VMEM
    dma = pltpu.SemaphoreType.DMA
    vm = pl.BlockSpec(memory_space=pltpu.VMEM)
    anym = pl.BlockSpec(memory_space=pl.ANY)
    sems = [
        (3,), (5,), (16,), (16,), (32,), (32,), (32,), (32,), (2, 15), (2, 15),
        (16,), (16,), (2, 8, 2), (2, 8, 2), (2, 8, 2), (2, 8, 2), None, None,
        None, None, (2, 8), (2, 8), (2, 8), (2, 8), (16,), (16,),
        (2, 8), (2, 8), (2, 2), (2, 2), (2, 2, 2), (2, 2, 2), (2,), (2,), (32,), (32,),
    ]
    rw = route_weights.reshape(1, 128)
    rows, slots = pl.pallas_call(
        body,
        out_shape=(
            jax.ShapeDtypeStruct((16, 2, 16, 128), BF),
            jax.ShapeDtypeStruct((32, 112, 384), BF),
        ),
        in_specs=[vm, vm, vm, pl.BlockSpec(memory_space=pltpu.SMEM), anym, anym, anym, vm],
        out_specs=(anym, anym),
        scratch_shapes=[
            v((16, 2, 16, 128), BF),
            v((32, 16, 128), BF),
            v((16, 2, 16, 128), BF),
            v((16, 2, 2, 8, 16, 128), BF),
            v((16, 512, 256), BF),
            v((16, 256, 512), BF),
            v((16, 128, 384), BF),
            v((16, 512, 256), BF),
            v((16, 512, 384), BF),
            v((32, 128, 256), BF),
            v((16, 2, 128, 128), BF),
            v((16, 128, 256), BF),
            v((2, 8, 128, 256), BF),
            v((2, 8, 2, 128, 128), BF),
            v((128, 128), BF),
            v((32, 128, 256), BF),
            v((16, 2, 128, 128), BF),
            v((16, 512, 384), BF),
            v((16, 2, 2, 8, 16, 128), BF),
            v((2, 8, 2, 8, 16, 128), BF),
            v((2, 2, 2, 8, 16, 128), BF),
            v((2, 2, 2, 2, 8, 16, 128), BF),
            v((2, 2, 8, 16, 128), BF),
            v((2, 2, 8, 16, 128), BF),
            v((16, 2, 16, 128), BF),
            v((32, 112, 384), BF),
        ]
        + [dma if s is None else dma(s) for s in sems],
        compiler_params=pltpu.CompilerParams(
            collective_id=0, has_side_effects=True, vmem_limit_bytes=60 * 1024 * 1024
        ),
        cost_estimate=pl.CostEstimate(flops=8 * 10**9, bytes_accessed=3 * 10**6, transcendentals=0),
    )(
        tokens.T,
        routes.reshape(1, 128),
        rw,
        hot_experts,
        w_gate,
        w_up,
        jnp.swapaxes(w_down, 1, 2),
        cotangent.T,
    )
    grad = jax.ShapeDtypeStruct((16, 112, 128), BF)
    out_t, gtok_t, gg, gu, gd = pl.pallas_call(
        finish,
        out_shape=(
            jax.ShapeDtypeStruct((224, 128), BF),
            jax.ShapeDtypeStruct((224, 128), BF),
            grad,
            grad,
            grad,
        ),
        in_specs=[anym, anym, vm, pl.BlockSpec(memory_space=pltpu.SMEM)],
        out_specs=(vm, vm, vm, vm, vm),
        scratch_shapes=[
            v((16, 2, 16, 128), BF),
            v((32, 112, 384), BF),
            v((16, 112, 384), F32),
            dma((3,)),
        ],
        compiler_params=pltpu.CompilerParams(vmem_limit_bytes=60 * 1024 * 1024),
    )(rows, slots, rw, hot_experts)
    return out_t.T, gtok_t.T, gg, gu, jnp.swapaxes(gd, 1, 2)


def solution(mesh):
    placed = (
        P("ep", "grp"),
        P("ep", None),
        P("ep", None),
        P(),
        P(None, "ep", "grp"),
        P(None, "ep", "grp"),
        P(None, "grp", "ep"),
        P("ep", "grp"),
    )
    return jax.shard_map(
        layer,
        mesh=mesh,
        in_specs=placed,
        out_specs=(
            P("ep", "grp"),
            P("ep", "grp"),
            P(None, "ep", "grp"),
            P(None, "ep", "grp"),
            P(None, "grp", "ep"),
        ),
        check_vma=False,
    )
```

```python
import functools

import jax
import jax.numpy as jnp
from jax import lax
from jax.experimental import pallas as pl
from jax.experimental.pallas import tpu as pltpu
from jax.sharding import PartitionSpec as P

MESH = pl.DeviceIdType.MESH
BF = jnp.bfloat16
F32 = jnp.float32
NX, NY, NZ, NEP, NGRP = 4, 2, 16, 32, 16
LAST = (((1,), (1,)), ((), ()))
FIRST = (((0,), (0,)), ((), ()))


def mm(a, b, dims=(((1,), (0,)), ((), ()))):
    return lax.dot_general(a, b, dims, preferred_element_type=F32)


def body(
    tok_ref, routes_ref, rw_ref, hot_ref, wg_ref, wu_ref, wd_ref, cot_ref,
    rows_ref, slots_ref,
    src, meta, a1r, xb, er, et, wall, xe, se, pa, pb, ya, ra, rb, yb,
    ha, hb, he, qq, rc, rfar, rx, ry, fin, b2r, tot,
    w_sem, o_sem, a1_s, a1_q, m_s, m_q, a2_s, a2_q, g3_s, g3_q,
    ya_s, ya_q, ra_s, ra_q, rb_s, rb_q, yb_s, yb_q,
    hy_s, hy_q, ga_s, ga_q, gb_s, gb_q, gy_s, gy_q,
    c5_s, c5_q, f5_s, f5_q, x5_s, x5_q, y5_s, y5_q, b1_s, b1_q,
):
    g = lax.axis_index("grp")
    p = lax.axis_index("ep")
    x, yh, c = g // 4, (g // 2) % 2, g % 2
    y, z = p // NZ, p % NZ
    zr, zl = y * NZ + (z + 1) % NZ, y * NZ + (z + NZ - 1) % NZ
    py = (1 - y) * NZ + z
    gi = lambda xx, hh, cc: xx * 4 + hh * 2 + cc
    xr, xl = (x + 1) % NX, (x + 3) % NX
    gr, gl = gi(xr, yh, c), gi(xl, yh, c)
    gy, gc = gi(x, 1 - yh, c), gi(x, yh, 1 - c)

    def put(s, d, ss, rs, **dev):
        return pltpu.make_async_remote_copy(
            src_ref=s, dst_ref=d, send_sem=ss, recv_sem=rs, device_id=dev, device_id_type=MESH
        )

    w_in = [
        pltpu.make_async_copy(r, wall.at[:, pl.ds(0, 112), pl.ds(128 * i, 128)], w_sem.at[i])
        for i, r in enumerate((wg_ref, wu_ref, wd_ref))
    ]
    for cp in w_in:
        cp.start()

    tail = []

    barrier = pltpu.get_barrier_semaphore()

    def hello_g(i, _):
        pl.semaphore_signal(barrier, inc=1, device_id={"grp": (g + i) % NGRP}, device_id_type=MESH)
        return 0

    def hello_e(i, _):
        pl.semaphore_signal(barrier, inc=1, device_id={"ep": (p + i) % NEP}, device_id_type=MESH)
        return 0

    lax.fori_loop(1, NGRP, hello_g, 0)
    lax.fori_loop(1, NEP, hello_e, 0)

    def hello_b(i, _):
        t, h = i // 2, i % 2

        @pl.when(jnp.logical_not((t == g) & (2 * g + h == p)))
        def _():
            pl.semaphore_signal(barrier, inc=1, device_id={"grp": t, "ep": 2 * g + h}, device_id_type=MESH)

        return 0

    lax.fori_loop(0, NEP, hello_b, 0)

    slot_row = routes_ref[...]
    dz = (cot_ref[...].astype(F32) * rw_ref[...]).astype(BF)
    for h in range(2):
        src[0:7, h] = tok_ref[h * 112 : (h + 1) * 112, :].reshape(7, 16, 128)
        src[8:15, h] = dz[h * 112 : (h + 1) * 112, :].reshape(7, 16, 128)
    src[7] = jnp.zeros((2, 16, 128), BF)
    src[15] = jnp.zeros((2, 16, 128), BF)
    wall[:, 112:128, :] = jnp.zeros((16, 16, 384), BF)

    oh = jnp.where(lax.broadcasted_iota(jnp.int32, (NEP, 128), 0) == slot_row, 1.0, 0.0).astype(F32)
    upper = jnp.where(
        lax.broadcasted_iota(jnp.int32, (128, 128), 0) < lax.broadcasted_iota(jnp.int32, (128, 128), 1), 1.0, 0.0
    ).astype(BF)
    before = mm(oh.astype(BF), upper)
    pos_row = jnp.sum(oh * before, axis=0, keepdims=True)
    row_id = lax.broadcasted_iota(jnp.int32, (16, 128), 0)
    mrows = jnp.where(row_id == 0, slot_row.astype(F32), jnp.where(row_id == 1, pos_row, 0.0))
    meta[p] = mrows.astype(BF)

    pl.semaphore_wait(barrier, NGRP + NEP - 2 + NEP - jnp.where(p // 2 == g, 1, 0))

    a1 = lambda i, t: put(src.at[t], a1r.at[g], a1_s.at[i], a1_q.at[i], grp=t)
    mt = lambda i, t: put(meta.at[p], meta.at[p], m_s.at[i], m_q.at[i], ep=t)

    def place(at, yy, zz):
        r = (zz + 2 * NZ - 2 * (at // 2 + 3)) % NZ
        return r // 8, yy, r % 8

    def a2(t):
        return put(
            a1r.at[t // 2, t % 2], xb.at[(g,) + place(t % NZ, y, z)], a2_s.at[t], a2_q.at[p], ep=t
        )

    def a2_start(n):
        m = n // 2
        off = jnp.where(m % 2 == 0, 8 - m // 2, 8 + (m + 1) // 2)
        a2(((y + n) % 2) * NZ + (z + off) % NZ).start()

    def zpair(half, j):
        return (z // 2 + 3 + 4 * half + j) % 8

    def pair_block(q):
        return ((q // 4) % 2) * NZ + 2 * zpair(q // 8, q % 4)

    def loop(lo, hi, f):
        def step(i, _):
            f(i)
            return 0

        lax.fori_loop(lo, hi, step, 0)

    def dots(lo, hi, f, unroll=1):
        def step(i, _):
            f(i)
            return 0

        lax.fori_loop(lo, hi, step, 0, unroll=unroll)

    loop(1, NGRP, lambda i: a1(i, (g + i) % NGRP).start())
    loop(1, NEP, lambda i: mt(i, (p + i) % NEP).start())
    a1r[g] = src[g]

    def a1_wait(i):
        f = (g + NGRP - i) % NGRP
        put(src.at[f], a1r.at[f], a1_s.at[i], a1_q.at[i], grp=f).wait_recv()

    loop(1, NGRP, a1_wait)
    loop(0, 30, a2_start)
    a2(py).start()
    tail.append(lambda: loop(1, NGRP, lambda i: a1(i, (g + i) % NGRP).wait_send()))
    tail.append(lambda: loop(1, NEP, lambda i: mt(i, (p + i) % NEP).wait_send()))
    tail.append(lambda: loop(1, NEP, lambda i: a2((p + i) % NEP).wait_send()))
    xb[(g,) + place(z, y, z)] = a1r[p // 2, p % 2]

    def m_wait(i):
        f = (p + NEP - i) % NEP
        put(meta.at[p], meta.at[f], m_s.at[i], m_q.at[i], ep=f).wait_recv()

    loop(1, NEP, m_wait)

    def build(q):
        m0 = meta[pair_block(q)].astype(F32)
        m1 = meta[pair_block(q) + 1].astype(F32)
        d0 = m0[0:1, :] * 16.0 + m0[1:2, :]
        d1 = m1[0:1, :] * 16.0 + m1[1:2, :] + 8.0
        row = jnp.concatenate([d0, d1], axis=1)
        irow = row.astype(jnp.int32)
        er[q] = jnp.where(
            lax.broadcasted_iota(jnp.int32, (512, 256), 0) == irow, 1.0, 0.0
        ).astype(BF)
        col = jnp.transpose(jnp.broadcast_to(row, (128, 256))).astype(jnp.int32)
        for b in range(4):
            et[q, :, 128 * b : 128 * (b + 1)] = jnp.where(
                lax.broadcasted_iota(jnp.int32, (256, 128), 1) + 128 * b == col, 1.0, 0.0
            ).astype(BF)

    def a2_wait(i):
        f = (p + NEP - i) % NEP
        put(a1r.at[0, 0], xb.at[(g,) + place(z, f // NZ, f % NZ)], a2_s.at[f], a2_q.at[f], ep=f).wait_recv()

    dots(0, 4, build)
    loop(1, NEP, a2_wait)

    def g3(chunk, i, t, k):
        return put(xb.at[chunk, k], xb.at[chunk, k], g3_s.at[k, i], g3_q.at[k, i], grp=t)

    xf = (x + 2) % NX

    def g_own(k):
        g3(g, 1 + yh, gr, k).start()
        g3(g, 3 + yh, gl, k).start()
        g3(g, 7 + yh, gc, k).start()

    def g_pair(k):
        g3(gy, 0, gy, k).wait_recv()
        g3(gy, 1 + (1 - yh), gr, k).start()
        g3(gy, 3 + (1 - yh), gl, k).start()
        g3(gy, 7 + (1 - yh), gc, k).start()

    def g_relay(k):
        g3(gi(xl, 0, c), 1, gr, k).wait_recv()
        g3(gi(xl, 0, c), 5, gr, k).start()
        g3(gi(xl, 0, c), 7 + 6, gc, k).start()
        g3(gi(xr, 1, c), 4, gl, k).wait_recv()
        g3(gi(xr, 1, c), 6, gl, k).start()
        g3(gi(xr, 1, c), 7 + 3, gc, k).start()
        g3(gi(xl, 1, c), 2, gr, k).wait_recv()
        g3(gi(xl, 1, c), 7 + 7, gc, k).start()
        g3(gi(xr, 0, c), 3, gl, k).wait_recv()
        g3(gi(xr, 0, c), 7 + 2, gc, k).start()

    def g_far(k):
        for h in range(2):
            g3(gi(xf, h, c), 5 + h, gr, k).wait_recv()
            g3(gi(xf, h, c), 7 + 4 + h, gc, k).start()

    def g_core(k):
        for dx in range(4):
            for h in range(2):
                g3(gi((x + dx) % NX, h, 1 - c), 7 + 2 * dx + h, gc, k).wait_recv()

    def spread(i):
        e = er[pl.ds(2 * i, 2)]
        k, yy, m = i // 4, (i // 2) % 2, i % 2
        tb = xb[:, k, yy, pl.ds(4 * m, 4)]
        rows = []
        for j in range(2):
            t0, t1 = tb[:, 2 * j].reshape(256, 128), tb[:, 2 * j + 1].reshape(256, 128)
            rows.append(mm(e[j], jnp.concatenate([t0, t1], axis=1), LAST).astype(BF))
        xe[pl.ds(2 * i, 2)] = jnp.stack(rows)

    def host(s):
        return jnp.where(s < 16, s, hot_ref[jnp.maximum(s - 16, 0)])

    def first_dots(k):
        part = pl.ds(8 * k, 8)

        def four(i):
            rows = pl.ds(pl.multiple_of(i * 64, 64), 64)
            xd = xe[part, rows, :]
            gu, dn = [], []
            for j in range(4):
                w = wall[host(4 * i + j)]
                xj = xd[:, 16 * j : 16 * j + 16].reshape(128, 256)
                gu.append(mm(xj[:, 0:128], w[:, 0:256]).astype(BF).reshape(8, 16, 256))
                dn.append(mm(xj[:, 128:256], w[:, 256:384]).astype(BF).reshape(8, 16, 128))
            se[part, rows, 0:256] = jnp.concatenate(gu, axis=1)
            se[part, rows, 256:384] = jnp.concatenate(dn, axis=1)

        dots(0, 8, four, 1)

    def squeeze(k, yy, i):
        js = (1 - i, 2 + i) if k == 0 else (3 - i, i)
        both = [mm(et[8 * k + 4 * yy + j], se[8 * k + 4 * yy + j]).astype(BF) for j in js]
        for j, cc in zip(js, both):
            zp = zpair(k, j)
            pa[pl.ds(yy * NZ + 2 * zp, 2)] = cc[:, 0:256].reshape(2, 128, 256)
            pb[pl.ds(2 * zp, 2), yy] = cc[:, 256:384].reshape(2, 128, 128)
        return js

    def squeezes(k):
        def far(i):
            for j in squeeze(k, 1 - y, i):
                ya_put(2 * zpair(k, j)).start()
                ya_put(2 * zpair(k, j) + 1).start()

        loop(0, 2, far)
        loop(0, 2, lambda i: squeeze(k, y, i))

    def ya_put(t):
        return put(pa.at[(1 - y) * NZ + t], ya.at[t], ya_s.at[t], ya_q.at[t], ep=py)

    tail.append(lambda: loop(0, 16, lambda t: ya_put(t).wait_send()))

    def target(d, n, k):
        return (z + NZ + (n - k if d == 0 else k - n)) % NZ

    def a_put(d, k, t, j):
        r = pl.ds(64 * j, 64)
        return put(
            pa.at[y * NZ + t, r], ra.at[d, k, r], ra_s.at[d, k, j], ra_q.at[d, k, j], ep=zr if d == 0 else zl
        )

    def b_put(d, k, t, j):
        return put(
            pb.at[t, j], rb.at[d, k, j], rb_s.at[d, k, j], rb_q.at[d, k, j], ep=zr if d == 0 else zl
        )

    def a_step(d, n, k, j):
        t = target(d, n, k)
        r = pl.ds(64 * j, 64)
        if j == 0:
            ya_put(t).wait_recv()
        v = pa[y * NZ + t, r].astype(F32) + ya[t, r].astype(F32)
        if not (isinstance(k, int) and k == 0):
            a_put(d, k - 1, t, j).wait_recv()
            v = v + ra[d, k - 1, r].astype(F32)
        pa[y * NZ + t, r] = v.astype(BF)
        a_put(d, k, t, j).start()

    def b_step(d, n, k, j):
        t = target(d, n, k)
        if not (isinstance(k, int) and k == 0):
            b_put(d, k - 1, t, j).wait_recv()
            pb[t, j] = (pb[t, j].astype(F32) + rb[d, k - 1, j].astype(F32)).astype(BF)
        b_put(d, k, t, j).start()

    def all_steps(k):
        for j in range(2):
            b_step(0, 7, k, j)
            b_step(1, 8, k, j)
        for j in range(2):
            a_step(0, 8, k, j)
            a_step(1, 7, k, j)

    g3(g, 0, gy, 0).start()
    g3(g, 0, gy, 1).start()
    g_own(0)
    dots(4, 10, build)
    g_pair(0)
    g_own(1)
    dots(10, 16, build)
    g_relay(0)
    for cp in w_in:
        cp.wait()
    g_pair(1)
    g_far(0)
    for k in range(2):
        tail.append(lambda k=k: loop(0, 15, lambda i: g3(g, i, gy, k).wait_send()))
    g_core(0)
    dots(0, 4, spread)
    g_relay(1)
    first_dots(0)
    squeezes(0)
    all_steps(0)
    g_far(1)
    g_core(1)
    dots(4, 8, spread)

    def ring_and_rest(k):
        all_steps(k)

        @pl.when(k == 1)
        def _():
            first_dots(1)
            squeezes(1)

        for at, waits in ((3, tail[0:3]), (4, tail[3:])):

            @pl.when(k == at)
            def _(waits=waits):
                for wait in waits:
                    wait()

    loop(1, 7, ring_and_rest)
    tail.clear()
    for j in range(2):
        b_step(1, 8, 7, j)
    for j in range(2):
        a_step(0, 8, 7, j)
    for j in range(2):
        b_put(0, 6, z, j).wait_recv()
        b_put(1, 7, z, j).wait_recv()
    ag_own = (
        pb[z, y].astype(F32) + rb[0, 6, y].astype(F32) + rb[1, 7, y].astype(F32)
    )
    pb[z, 1 - y] = (
        pb[z, 1 - y].astype(F32) + rb[0, 6, 1 - y].astype(F32) + rb[1, 7, 1 - y].astype(F32)
    ).astype(BF)
    yb_put = put(pb.at[z, 1 - y], yb, yb_s, yb_q, ep=py)
    yb_put.start()

    def ring_sends():
        for d in range(2):
            na, nb = (8, 7) if d == 0 else (7, 8)
            for j in range(2):
                loop(0, na, lambda k: a_put(d, k, z, j).wait_send())
                loop(0, nb, lambda k: b_put(d, k, z, j).wait_send())
        yb_put.wait_send()

    tail.append(ring_sends)
    ya_put(z).wait_recv()
    for j in range(2):
        a_put(1, 6, z, j).wait_recv()
        a_put(0, 7, z, j).wait_recv()
    pre = (
        pa[p].astype(F32) + ya[z].astype(F32) + ra[0, 7].astype(F32) + ra[1, 6].astype(F32)
    )
    gate, up = pre[:, 0:128], pre[:, 128:256]
    sg = jax.nn.sigmoid(gate)
    hb[z, y] = (gate * sg * up).astype(BF)
    hy_put = put(hb.at[z, y], hb.at[z, y], hy_s, hy_q, ep=py)
    hy_put.start()
    yb_put.wait_recv()
    ag = ag_own + yb[...].astype(F32)
    ha[p, :, 0:128] = (ag * up * sg * (1.0 + gate * (1.0 - sg))).astype(BF)
    ha[p, :, 128:256] = (ag * gate * sg).astype(BF)

    tail.append(hy_put.wait_send)
    def origin(d, k):
        return (z + NZ + (-k if d == 0 else k)) % NZ

    def ga_put(d, k, o):
        return put(
            ha.at[y * NZ + o], ha.at[y * NZ + o], ga_s.at[d, k], ga_q.at[d, k], ep=zr if d == 0 else zl
        )

    def gb_put(d, k, o):
        return put(hb.at[o], hb.at[o], gb_s.at[d, k], gb_q.at[d, k], ep=zr if d == 0 else zl)

    def gy_put(yy, o):
        return put(ha.at[yy * NZ + o], ha.at[yy * NZ + o], gy_s.at[o], gy_q.at[o], ep=py)

    ga_put(0, 0, z).start()
    ga_put(1, 0, z).start()
    gy_put(y, z).start()
    put(hb.at[z, 1 - y], hb.at[z, 1 - y], hy_s, hy_q, ep=py).wait_recv()
    gb_put(0, 0, z).start()
    gb_put(1, 0, z).start()

    def ga_step(d, k, more=True):
        o = origin(d, k)
        ga_put(d, k - 1, o).wait_recv()
        if more:
            ga_put(d, k, o).start()
        gy_put(y, o).start()

    def gb_step(d, k, more=True):
        o = origin(d, k)
        gb_put(d, k - 1, o).wait_recv()
        if more:
            gb_put(d, k, o).start()

    def gather_steps(k):
        ga_step(0, k)
        ga_step(1, k)
        gb_step(0, k)
        gb_step(1, k)

    def gather_sends():
        for d in range(2):
            na, nb = (8, 7) if d == 0 else (7, 8)
            loop(0, na, lambda k: ga_put(d, k, z).wait_send())
            loop(0, nb, lambda k: gb_put(d, k, z).wait_send())
        loop(0, 16, lambda o: gy_put(y, o).wait_send())

    def spread_back(k):
        def two(n):
            yy, m = n // 2, n % 2
            i = 8 * k + 2 * n
            e = er[pl.ds(i, 2)]
            rows = []
            for j in range(2):
                zp = zpair(k, 2 * m + j)
                hq = jnp.concatenate(
                    [
                        ha[pl.ds(yy * NZ + 2 * zp, 2)].reshape(256, 256),
                        hb[pl.ds(2 * zp, 2), yy].reshape(256, 128),
                    ],
                    axis=1,
                )
                rows.append(mm(e[j], hq).astype(BF))
            he[pl.ds(i, 2)] = jnp.stack(rows)

        loop(0, 4, two)

    def gy_wait(k):
        for j in range(4):
            gy_put(1 - y, 2 * zpair(k, j)).wait_recv()
            gy_put(1 - y, 2 * zpair(k, j) + 1).wait_recv()

    def back_dots(k):
        part = pl.ds(8 * k, 8)

        def four(i):
            rows = pl.ds(pl.multiple_of(i * 64, 64), 64)
            hs = he[part, rows, :]
            dn, gu = [], []
            for j in range(4):
                w = wall[host(4 * i + j)]
                hj = hs[:, 16 * j : 16 * j + 16].reshape(128, 384)
                dn.append(mm(hj[:, 256:384], w[:, 256:384], LAST).astype(BF).reshape(8, 16, 128))
                gu.append(mm(hj[:, 0:256], w[:, 0:256], LAST).astype(BF).reshape(8, 16, 128))
            se[part, rows, 0:128] = jnp.concatenate(dn, axis=1)
            se[part, rows, 128:256] = jnp.concatenate(gu, axis=1)

        dots(0, 8, four, 1)

    def squeeze_out(k):
        def two(i):
            r = 8 * k + 2 * i
            t = et[pl.ds(r, 2)]
            parts = se[pl.ds(r, 2), :, 0:256]
            sums = jnp.stack([mm(t[j], parts[j]).astype(BF) for j in range(2)])
            sums = sums.reshape(4, 8, 16, 256)
            m = pl.ds(4 * (i % 2), 4)
            for b in range(8):
                qq[b, k, i // 2, m] = sums[:, b, :, 0:128]
                qq[8 + b, k, i // 2, m] = sums[:, b, :, 128:256]

        dots(0, 4, two, 1)

    def c5(dx, h, k):
        i = 2 * dx + h
        return put(
            qq.at[gi((x + dx) % NX, h, 1 - c), k], rc.at[k, i], c5_s.at[k, i], c5_q.at[k, i], grp=gc
        )

    def core_sends(k):
        for dx in (2, 1, 3, 0):
            for h in range(2):
                c5(dx, h, k).start()

    def weight_dots(i):
        rows = pl.ds(pl.multiple_of(i * 64, 64), 64)
        xd = xe[:, rows, :]
        hs = he[:, rows, :]
        for j in range(4):
            xj = xd[:, 16 * j : 16 * j + 16].reshape(256, 256)
            hj = hs[:, 16 * j : 16 * j + 16].reshape(256, 384)
            tot[4 * i + j, :, 0:256] = mm(xj[:, 0:128], hj[:, 0:256], FIRST)[0:112].astype(BF)
            tot[4 * i + j, :, 256:384] = mm(xj[:, 128:256], hj[:, 256:384], FIRST)[0:112].astype(BF)

    w_out = []

    def weight_group(i):
        dots(2 * i, 2 * i + 2, weight_dots, 1)
        part = pl.ds(8 * i, 8)
        w_out.append(pltpu.make_async_copy(tot.at[part], slots_ref.at[part], o_sem.at[i]))
        w_out[-1].start()

    def addto(t, k, r):
        qq[t, k] = (qq[t, k].astype(F32) + r.astype(F32)).astype(BF)

    def with_core(dx, h, k):
        c5(dx, h, k).wait_recv()
        addto(gi((x + dx) % NX, h, c), k, rc[k, 2 * dx + h])

    def f5(h, k):
        return put(
            qq.at[gi(xf, h, c), k], rfar.at[k, h], f5_s.at[k, h], f5_q.at[k, h], grp=gr if h == 0 else gl
        )

    def x5(d, h, k):
        t = xr if d == 0 else xl
        return put(
            qq.at[gi(t, h, c), k],
            rx.at[k, d, h],
            x5_s.at[k, d, h],
            x5_q.at[k, d, h],
            grp=gr if d == 0 else gl,
        )

    def x_first(k):
        for h in range(2):
            with_core(2, h, k)
            f5(h, k).start()
        with_core(1, 1, k)
        x5(0, 1, k).start()
        with_core(3, 0, k)
        x5(1, 0, k).start()
        with_core(1, 0, k)
        with_core(3, 1, k)

    def x_second(k):
        f5(0, k).wait_recv()
        addto(gi(xr, 0, c), k, rfar[k, 0])
        x5(0, 0, k).start()
        f5(1, k).wait_recv()
        addto(gi(xl, 1, c), k, rfar[k, 1])
        x5(1, 1, k).start()

    def own_sum(h, k):
        return (
            qq[gi(x, h, c), k].astype(F32)
            + rc[k, h].astype(F32)
            + rx[k, 0, h].astype(F32)
            + rx[k, 1, h].astype(F32)
        )

    def y5(k):
        return put(qq.at[gy, k], ry.at[k], y5_s.at[k], y5_q.at[k], grp=gy)

    def y_sends(k):
        for h in range(2):
            c5(0, h, k).wait_recv()
            for d in range(2):
                x5(d, h, k).wait_recv()
        qq[gy, k] = own_sum(1 - yh, k).astype(BF)
        y5(k).start()

    def y_close(k):
        y5(k).wait_recv()
        fin[k] = (own_sum(yh, k) + ry[k].astype(F32)).astype(BF)

    def grp_sends():
        for k in range(2):
            for h in range(2):
                for dx in range(4):
                    c5(dx, h, k).wait_send()
                f5(h, k).wait_send()
                for d in range(2):
                    x5(d, h, k).wait_send()
            y5(k).wait_send()

    def b1(f):
        return put(
            fin.at[place(z, f // NZ, f % NZ)],
            b2r.at[g, p % 2],
            b1_s.at[f],
            b1_q.at[2 * g + p % 2],
            grp=p // 2,
            ep=f,
        )

    def b1_here(f):
        return (p // 2 == g) & (f == p)

    def b1_start(i):
        f = ((i // 8) % 2) * NZ + (2 * zpair(i // 16, 0) + i % 8) % NZ

        @pl.when(jnp.logical_not(b1_here(f)))
        def _():
            b1(f).start()

    early, tail[:] = tail[:], []

    def gather_and_rest(k):
        gather_steps(k)

        @pl.when(k == 2)
        def _():
            for wait in early:
                wait()

    loop(1, 6, gather_and_rest)
    gy_wait(1)
    spread_back(1)
    gather_steps(6)
    back_dots(1)
    ga_step(0, 7)
    ga_step(1, 7, False)
    gb_step(0, 7, False)
    gb_step(1, 7)
    squeeze_out(1)
    core_sends(1)
    ga_step(0, 8, False)
    gb_step(1, 8, False)
    x_first(1)
    gy_wait(0)
    spread_back(0)
    x_second(1)
    back_dots(0)
    squeeze_out(0)
    core_sends(0)
    gather_sends()
    y_sends(1)
    weight_group(0)
    x_first(0)
    y_close(1)
    loop(16, 32, b1_start)

    @pl.when(p // 2 == g)
    def _():
        b2r[g, p % 2] = fin[place(z, y, z)]

    weight_group(1)
    x_second(0)
    weight_group(2)
    y_sends(0)
    weight_group(3)
    y_close(0)
    loop(0, 16, b1_start)

    def b1_wait(i):
        t, h = i // 2, i % 2

        @pl.when(jnp.logical_not((t == g) & (2 * g + h == p)))
        def _():
            put(fin.at[0, 0, 0], b2r.at[t, h], b1_s.at[0], b1_q.at[i], grp=t, ep=2 * g + h).wait_recv()

    def b1_left(f):
        @pl.when(jnp.logical_not(b1_here(f)))
        def _():
            b1(f).wait_send()

    grp_sends()
    loop(0, NEP, b1_left)
    loop(0, NEP, b1_wait)
    rows_out = pltpu.make_async_copy(b2r, rows_ref, o_sem.at[4])
    rows_out.start()
    tail.append(rows_out.wait)
    for grp4 in w_out:
        tail.append(grp4.wait)

    for wait in tail:
        wait()


def finish(
    rows_ref, slots_ref, rw_ref, hot_ref, out_ref, gtok_ref, gg_ref, gu_ref, gd_ref, rows_v, slots_v, acc, sem
):
    rows_in = pltpu.make_async_copy(rows_ref, rows_v, sem.at[0])
    low = pltpu.make_async_copy(slots_ref.at[pl.ds(0, 16)], slots_v.at[pl.ds(0, 16)], sem.at[1])
    high = pltpu.make_async_copy(slots_ref.at[pl.ds(16, 16)], slots_v.at[pl.ds(16, 16)], sem.at[2])
    rows_in.start()
    low.start()
    high.start()

    def base(e, _):
        acc[e] = slots_v[e].astype(F32)
        return 0

    def more(j, _):
        e = hot_ref[j]
        acc[e] = acc[e] + slots_v[16 + j].astype(F32)
        return 0

    def close(e, _):
        v = acc[e].astype(BF)
        gg_ref[e] = v[:, 0:128]
        gu_ref[e] = v[:, 128:256]
        gd_ref[e] = v[:, 256:384]
        return 0

    rows_in.wait()
    for kind, ref in enumerate((out_ref, gtok_ref)):
        for h in range(2):
            part = rows_v[kind * 8 : (kind + 1) * 8, h].reshape(128, 128).astype(F32)
            v = jnp.transpose(part)[0:112]
            if kind == 0:
                v = v * rw_ref[...]
            ref[h * 112 : (h + 1) * 112, :] = v.astype(BF)
    low.wait()
    lax.fori_loop(0, 16, base, 0)
    high.wait()
    lax.fori_loop(0, 16, more, 0)
    lax.fori_loop(0, 16, close, 0)


def layer(tokens, routes, route_weights, hot_experts, w_gate, w_up, w_down, cotangent):
    v = pltpu.VMEM
    dma = pltpu.SemaphoreType.DMA
    vm = pl.BlockSpec(memory_space=pltpu.VMEM)
    anym = pl.BlockSpec(memory_space=pl.ANY)
    sems = [
        (3,), (5,), (16,), (16,), (32,), (32,), (32,), (32,), (2, 15), (2, 15),
        (16,), (16,), (2, 8, 2), (2, 8, 2), (2, 8, 2), (2, 8, 2), None, None,
        None, None, (2, 8), (2, 8), (2, 8), (2, 8), (16,), (16,),
        (2, 8), (2, 8), (2, 2), (2, 2), (2, 2, 2), (2, 2, 2), (2,), (2,), (32,), (32,),
    ]
    rw = route_weights.reshape(1, 128)
    rows, slots = pl.pallas_call(
        body,
        out_shape=(
            jax.ShapeDtypeStruct((16, 2, 16, 128), BF),
            jax.ShapeDtypeStruct((32, 112, 384), BF),
        ),
        in_specs=[vm, vm, vm, pl.BlockSpec(memory_space=pltpu.SMEM), anym, anym, anym, vm],
        out_specs=(anym, anym),
        scratch_shapes=[
            v((16, 2, 16, 128), BF),
            v((32, 16, 128), BF),
            v((16, 2, 16, 128), BF),
            v((16, 2, 2, 8, 16, 128), BF),
            v((16, 512, 256), BF),
            v((16, 256, 512), BF),
            v((16, 128, 384), BF),
            v((16, 512, 256), BF),
            v((16, 512, 384), BF),
            v((32, 128, 256), BF),
            v((16, 2, 128, 128), BF),
            v((16, 128, 256), BF),
            v((2, 8, 128, 256), BF),
            v((2, 8, 2, 128, 128), BF),
            v((128, 128), BF),
            v((32, 128, 256), BF),
            v((16, 2, 128, 128), BF),
            v((16, 512, 384), BF),
            v((16, 2, 2, 8, 16, 128), BF),
            v((2, 8, 2, 8, 16, 128), BF),
            v((2, 2, 2, 8, 16, 128), BF),
            v((2, 2, 2, 2, 8, 16, 128), BF),
            v((2, 2, 8, 16, 128), BF),
            v((2, 2, 8, 16, 128), BF),
            v((16, 2, 16, 128), BF),
            v((32, 112, 384), BF),
        ]
        + [dma if s is None else dma(s) for s in sems],
        compiler_params=pltpu.CompilerParams(
            collective_id=0, has_side_effects=True, vmem_limit_bytes=60 * 1024 * 1024
        ),
        cost_estimate=pl.CostEstimate(flops=8 * 10**9, bytes_accessed=3 * 10**6, transcendentals=0),
    )(
        tokens.T,
        routes.reshape(1, 128),
        rw,
        hot_experts,
        w_gate,
        w_up,
        jnp.swapaxes(w_down, 1, 2),
        cotangent.T,
    )
    grad = jax.ShapeDtypeStruct((16, 112, 128), BF)
    out_t, gtok_t, gg, gu, gd = pl.pallas_call(
        finish,
        out_shape=(
            jax.ShapeDtypeStruct((224, 128), BF),
            jax.ShapeDtypeStruct((224, 128), BF),
            grad,
            grad,
            grad,
        ),
        in_specs=[anym, anym, vm, pl.BlockSpec(memory_space=pltpu.SMEM)],
        out_specs=(vm, vm, vm, vm, vm),
        scratch_shapes=[
            v((16, 2, 16, 128), BF),
            v((32, 112, 384), BF),
            v((16, 112, 384), F32),
            dma((3,)),
        ],
        compiler_params=pltpu.CompilerParams(vmem_limit_bytes=60 * 1024 * 1024),
    )(rows, slots, rw, hot_experts)
    return out_t.T, gtok_t.T, gg, gu, jnp.swapaxes(gd, 1, 2)


def solution(mesh):
    placed = (
        P("ep", "grp"),
        P("ep", None),
        P("ep", None),
        P(),
        P(None, "ep", "grp"),
        P(None, "ep", "grp"),
        P(None, "grp", "ep"),
        P("ep", "grp"),
    )
    return jax.shard_map(
        layer,
        mesh=mesh,
        in_specs=placed,
        out_specs=(
            P("ep", "grp"),
            P("ep", "grp"),
            P(None, "ep", "grp"),
            P(None, "ep", "grp"),
            P(None, "grp", "ep"),
        ),
        check_vma=False,
    )
```

```python
import functools

import jax
import jax.numpy as jnp
from jax import lax
from jax.experimental import pallas as pl
from jax.experimental.pallas import tpu as pltpu
from jax.sharding import PartitionSpec as P

MESH = pl.DeviceIdType.MESH
BF = jnp.bfloat16
F32 = jnp.float32
NX, NY, NZ, NEP, NGRP = 4, 2, 16, 32, 16
LAST = (((1,), (1,)), ((), ()))
FIRST = (((0,), (0,)), ((), ()))


def mm(a, b, dims=(((1,), (0,)), ((), ()))):
    return lax.dot_general(a, b, dims, preferred_element_type=F32)


def body(
    tok_ref, routes_ref, rw_ref, hot_ref, wg_ref, wu_ref, wd_ref, cot_ref,
    rows_ref, slots_ref,
    src, meta, a1r, xb, er, et, wall, xe, se, pa, pb, ya, ra, rb, yb,
    ha, hb, he, qq, rc, rfar, rx, ry, fin, b2r, tot,
    w_sem, o_sem, a1_s, a1_q, m_s, m_q, a2_s, a2_q, g3_s, g3_q,
    ya_s, ya_q, ra_s, ra_q, rb_s, rb_q, yb_s, yb_q,
    hy_s, hy_q, ga_s, ga_q, gb_s, gb_q, gy_s, gy_q,
    c5_s, c5_q, f5_s, f5_q, x5_s, x5_q, y5_s, y5_q, b1_s, b1_q,
):
    g = lax.axis_index("grp")
    p = lax.axis_index("ep")
    x, yh, c = g // 4, (g // 2) % 2, g % 2
    y, z = p // NZ, p % NZ
    zr, zl = y * NZ + (z + 1) % NZ, y * NZ + (z + NZ - 1) % NZ
    py = (1 - y) * NZ + z
    gi = lambda xx, hh, cc: xx * 4 + hh * 2 + cc
    xr, xl = (x + 1) % NX, (x + 3) % NX
    gr, gl = gi(xr, yh, c), gi(xl, yh, c)
    gy, gc = gi(x, 1 - yh, c), gi(x, yh, 1 - c)

    def put(s, d, ss, rs, **dev):
        return pltpu.make_async_remote_copy(
            src_ref=s, dst_ref=d, send_sem=ss, recv_sem=rs, device_id=dev, device_id_type=MESH
        )

    w_in = [
        pltpu.make_async_copy(r, wall.at[:, pl.ds(0, 112), pl.ds(128 * i, 128)], w_sem.at[i])
        for i, r in enumerate((wg_ref, wu_ref, wd_ref))
    ]
    for cp in w_in:
        cp.start()

    tail = []

    barrier = pltpu.get_barrier_semaphore()

    def hello_g(i, _):
        pl.semaphore_signal(barrier, inc=1, device_id={"grp": (g + i) % NGRP}, device_id_type=MESH)
        return 0

    def hello_e(i, _):
        pl.semaphore_signal(barrier, inc=1, device_id={"ep": (p + i) % NEP}, device_id_type=MESH)
        return 0

    lax.fori_loop(1, NGRP, hello_g, 0)
    lax.fori_loop(1, NEP, hello_e, 0)

    def hello_b(i, _):
        t, h = i // 2, i % 2

        @pl.when(jnp.logical_not((t == g) & (2 * g + h == p)))
        def _():
            pl.semaphore_signal(barrier, inc=1, device_id={"grp": t, "ep": 2 * g + h}, device_id_type=MESH)

        return 0

    lax.fori_loop(0, NEP, hello_b, 0)

    slot_row = routes_ref[...]
    dz = (cot_ref[...].astype(F32) * rw_ref[...]).astype(BF)
    for h in range(2):
        src[0:7, h] = tok_ref[h * 112 : (h + 1) * 112, :].reshape(7, 16, 128)
        src[8:15, h] = dz[h * 112 : (h + 1) * 112, :].reshape(7, 16, 128)
    src[7] = jnp.zeros((2, 16, 128), BF)
    src[15] = jnp.zeros((2, 16, 128), BF)
    wall[:, 112:128, :] = jnp.zeros((16, 16, 384), BF)

    oh = jnp.where(lax.broadcasted_iota(jnp.int32, (NEP, 128), 0) == slot_row, 1.0, 0.0).astype(F32)
    upper = jnp.where(
        lax.broadcasted_iota(jnp.int32, (128, 128), 0) < lax.broadcasted_iota(jnp.int32, (128, 128), 1), 1.0, 0.0
    ).astype(BF)
    before = mm(oh.astype(BF), upper)
    pos_row = jnp.sum(oh * before, axis=0, keepdims=True)
    row_id = lax.broadcasted_iota(jnp.int32, (16, 128), 0)
    mrows = jnp.where(row_id == 0, slot_row.astype(F32), jnp.where(row_id == 1, pos_row, 0.0))
    meta[p] = mrows.astype(BF)

    pl.semaphore_wait(barrier, NGRP + NEP - 2 + NEP - jnp.where(p // 2 == g, 1, 0))

    a1 = lambda i, t: put(src.at[t], a1r.at[g], a1_s.at[i], a1_q.at[i], grp=t)
    mt = lambda i, t: put(meta.at[p], meta.at[p], m_s.at[i], m_q.at[i], ep=t)

    def place(at, yy, zz):
        r = (zz + 2 * NZ - 2 * (at // 2 + 3)) % NZ
        return r // 8, yy, r % 8

    def a2(t):
        return put(
            a1r.at[t // 2, t % 2], xb.at[(g,) + place(t % NZ, y, z)], a2_s.at[t], a2_q.at[p], ep=t
        )

    def a2_start(n):
        m = n // 2
        off = jnp.where(m % 2 == 0, 8 - m // 2, 8 + (m + 1) // 2)
        a2(((y + n) % 2) * NZ + (z + off) % NZ).start()

    def zpair(half, j):
        return (z // 2 + 3 + 4 * half + j) % 8

    def pair_block(q):
        return ((q // 4) % 2) * NZ + 2 * zpair(q // 8, q % 4)

    def loop(lo, hi, f):
        def step(i, _):
            f(i)
            return 0

        lax.fori_loop(lo, hi, step, 0)

    def dots(lo, hi, f, unroll=1):
        def step(i, _):
            f(i)
            return 0

        lax.fori_loop(lo, hi, step, 0, unroll=unroll)

    loop(1, NGRP, lambda i: a1(i, (g + i) % NGRP).start())
    loop(1, NEP, lambda i: mt(i, (p + i) % NEP).start())
    a1r[g] = src[g]

    def a1_wait(i):
        f = (g + NGRP - i) % NGRP
        put(src.at[f], a1r.at[f], a1_s.at[i], a1_q.at[i], grp=f).wait_recv()

    loop(1, NGRP, a1_wait)
    loop(0, 30, a2_start)
    a2(py).start()
    tail.append(lambda: loop(1, NGRP, lambda i: a1(i, (g + i) % NGRP).wait_send()))
    tail.append(lambda: loop(1, NEP, lambda i: mt(i, (p + i) % NEP).wait_send()))
    tail.append(lambda: loop(1, NEP, lambda i: a2((p + i) % NEP).wait_send()))
    xb[(g,) + place(z, y, z)] = a1r[p // 2, p % 2]

    def m_wait(i):
        f = (p + NEP - i) % NEP
        put(meta.at[p], meta.at[f], m_s.at[i], m_q.at[i], ep=f).wait_recv()

    loop(1, NEP, m_wait)

    def build(q):
        m0 = meta[pair_block(q)].astype(F32)
        m1 = meta[pair_block(q) + 1].astype(F32)
        d0 = m0[0:1, :] * 16.0 + m0[1:2, :]
        d1 = m1[0:1, :] * 16.0 + m1[1:2, :] + 8.0
        row = jnp.concatenate([d0, d1], axis=1)
        irow = row.astype(jnp.int32)
        er[q] = jnp.where(
            lax.broadcasted_iota(jnp.int32, (512, 256), 0) == irow, 1.0, 0.0
        ).astype(BF)
        col = jnp.transpose(jnp.broadcast_to(row, (128, 256))).astype(jnp.int32)
        for b in range(4):
            et[q, :, 128 * b : 128 * (b + 1)] = jnp.where(
                lax.broadcasted_iota(jnp.int32, (256, 128), 1) + 128 * b == col, 1.0, 0.0
            ).astype(BF)

    def a2_wait(i):
        f = (p + NEP - i) % NEP
        put(a1r.at[0, 0], xb.at[(g,) + place(z, f // NZ, f % NZ)], a2_s.at[f], a2_q.at[f], ep=f).wait_recv()

    dots(0, 4, build)
    loop(1, NEP, a2_wait)

    def g3(chunk, i, t, k):
        return put(xb.at[chunk, k], xb.at[chunk, k], g3_s.at[k, i], g3_q.at[k, i], grp=t)

    xf = (x + 2) % NX

    def g_own(k):
        g3(g, 1 + yh, gr, k).start()
        g3(g, 3 + yh, gl, k).start()
        g3(g, 7 + yh, gc, k).start()

    def g_pair(k):
        g3(gy, 0, gy, k).wait_recv()
        g3(gy, 1 + (1 - yh), gr, k).start()
        g3(gy, 3 + (1 - yh), gl, k).start()
        g3(gy, 7 + (1 - yh), gc, k).start()

    def g_relay(k):
        g3(gi(xl, 0, c), 1, gr, k).wait_recv()
        g3(gi(xl, 0, c), 5, gr, k).start()
        g3(gi(xl, 0, c), 7 + 6, gc, k).start()
        g3(gi(xr, 1, c), 4, gl, k).wait_recv()
        g3(gi(xr, 1, c), 6, gl, k).start()
        g3(gi(xr, 1, c), 7 + 3, gc, k).start()
        g3(gi(xl, 1, c), 2, gr, k).wait_recv()
        g3(gi(xl, 1, c), 7 + 7, gc, k).start()
        g3(gi(xr, 0, c), 3, gl, k).wait_recv()
        g3(gi(xr, 0, c), 7 + 2, gc, k).start()

    def g_far(k):
        for h in range(2):
            g3(gi(xf, h, c), 5 + h, gr, k).wait_recv()
            g3(gi(xf, h, c), 7 + 4 + h, gc, k).start()

    def g_core(k):
        for dx in range(4):
            for h in range(2):
                g3(gi((x + dx) % NX, h, 1 - c), 7 + 2 * dx + h, gc, k).wait_recv()

    def spread(i):
        e = er[pl.ds(2 * i, 2)]
        k, yy, m = i // 4, (i // 2) % 2, i % 2
        tb = xb[:, k, yy, pl.ds(4 * m, 4)]
        rows = []
        for j in range(2):
            t0, t1 = tb[:, 2 * j].reshape(256, 128), tb[:, 2 * j + 1].reshape(256, 128)
            rows.append(mm(e[j], jnp.concatenate([t0, t1], axis=1), LAST).astype(BF))
        xe[pl.ds(2 * i, 2)] = jnp.stack(rows)

    def host(s):
        return jnp.where(s < 16, s, hot_ref[jnp.maximum(s - 16, 0)])

    def first_dots(k):
        part = pl.ds(8 * k, 8)

        def four(i):
            rows = pl.ds(pl.multiple_of(i * 64, 64), 64)
            xd = xe[part, rows, :]
            gu, dn = [], []
            for j in range(4):
                w = wall[host(4 * i + j)]
                xj = xd[:, 16 * j : 16 * j + 16].reshape(128, 256)
                gu.append(mm(xj[:, 0:128], w[:, 0:256]).astype(BF).reshape(8, 16, 256))
                dn.append(mm(xj[:, 128:256], w[:, 256:384]).astype(BF).reshape(8, 16, 128))
            se[part, rows, 0:256] = jnp.concatenate(gu, axis=1)
            se[part, rows, 256:384] = jnp.concatenate(dn, axis=1)

        dots(0, 8, four, 1)

    def squeeze(k, yy, i):
        js = (1 - i, 2 + i) if k == 0 else (3 - i, i)
        both = [mm(et[8 * k + 4 * yy + j], se[8 * k + 4 * yy + j]).astype(BF) for j in js]
        for j, cc in zip(js, both):
            zp = zpair(k, j)
            pa[pl.ds(yy * NZ + 2 * zp, 2)] = cc[:, 0:256].reshape(2, 128, 256)
            pb[pl.ds(2 * zp, 2), yy] = cc[:, 256:384].reshape(2, 128, 128)
        return js

    def squeezes(k):
        def far(i):
            for j in squeeze(k, 1 - y, i):
                ya_put(2 * zpair(k, j)).start()
                ya_put(2 * zpair(k, j) + 1).start()

        loop(0, 2, far)
        loop(0, 2, lambda i: squeeze(k, y, i))

    def ya_put(t):
        return put(pa.at[(1 - y) * NZ + t], ya.at[t], ya_s.at[t], ya_q.at[t], ep=py)

    tail.append(lambda: loop(0, 16, lambda t: ya_put(t).wait_send()))

    def target(d, n, k):
        return (z + NZ + (n - k if d == 0 else k - n)) % NZ

    def a_put(d, k, t, j):
        r = pl.ds(64 * j, 64)
        return put(
            pa.at[y * NZ + t, r], ra.at[d, k, r], ra_s.at[d, k, j], ra_q.at[d, k, j], ep=zr if d == 0 else zl
        )

    def b_put(d, k, t, j):
        return put(
            pb.at[t, j], rb.at[d, k, j], rb_s.at[d, k, j], rb_q.at[d, k, j], ep=zr if d == 0 else zl
        )

    def a_step(d, n, k, j):
        t = target(d, n, k)
        r = pl.ds(64 * j, 64)
        if j == 0:
            ya_put(t).wait_recv()
        v = pa[y * NZ + t, r].astype(F32) + ya[t, r].astype(F32)
        if not (isinstance(k, int) and k == 0):
            a_put(d, k - 1, t, j).wait_recv()
            v = v + ra[d, k - 1, r].astype(F32)
        pa[y * NZ + t, r] = v.astype(BF)
        a_put(d, k, t, j).start()

    def b_step(d, n, k, j):
        t = target(d, n, k)
        if not (isinstance(k, int) and k == 0):
            b_put(d, k - 1, t, j).wait_recv()
            pb[t, j] = (pb[t, j].astype(F32) + rb[d, k - 1, j].astype(F32)).astype(BF)
        b_put(d, k, t, j).start()

    def all_steps(k):
        for j in range(2):
            b_step(0, 7, k, j)
            b_step(1, 8, k, j)
        for j in range(2):
            a_step(0, 8, k, j)
            a_step(1, 7, k, j)

    g3(g, 0, gy, 0).start()
    g3(g, 0, gy, 1).start()
    g_own(0)
    dots(4, 10, build)
    g_pair(0)
    g_own(1)
    dots(10, 16, build)
    g_relay(0)
    for cp in w_in:
        cp.wait()
    g_pair(1)
    g_far(0)
    for k in range(2):
        tail.append(lambda k=k: loop(0, 15, lambda i: g3(g, i, gy, k).wait_send()))
    g_core(0)
    dots(0, 4, spread)
    g_relay(1)
    first_dots(0)
    squeezes(0)
    all_steps(0)
    g_far(1)
    g_core(1)
    dots(4, 8, spread)

    def ring_and_rest(k):
        all_steps(k)

        @pl.when(k == 1)
        def _():
            first_dots(1)
            squeezes(1)

        for at, waits in ((3, tail[0:3]), (4, tail[3:])):

            @pl.when(k == at)
            def _(waits=waits):
                for wait in waits:
                    wait()

    loop(1, 7, ring_and_rest)
    tail.clear()
    for j in range(2):
        b_step(1, 8, 7, j)
    for j in range(2):
        a_step(0, 8, 7, j)
    for j in range(2):
        b_put(0, 6, z, j).wait_recv()
        b_put(1, 7, z, j).wait_recv()
    ag_own = (
        pb[z, y].astype(F32) + rb[0, 6, y].astype(F32) + rb[1, 7, y].astype(F32)
    )
    pb[z, 1 - y] = (
        pb[z, 1 - y].astype(F32) + rb[0, 6, 1 - y].astype(F32) + rb[1, 7, 1 - y].astype(F32)
    ).astype(BF)
    yb_put = put(pb.at[z, 1 - y], yb, yb_s, yb_q, ep=py)
    yb_put.start()

    def ring_sends():
        for d in range(2):
            na, nb = (8, 7) if d == 0 else (7, 8)
            for j in range(2):
                loop(0, na, lambda k: a_put(d, k, z, j).wait_send())
                loop(0, nb, lambda k: b_put(d, k, z, j).wait_send())
        yb_put.wait_send()

    tail.append(ring_sends)
    ya_put(z).wait_recv()
    for j in range(2):
        a_put(1, 6, z, j).wait_recv()
        a_put(0, 7, z, j).wait_recv()
    pre = (
        pa[p].astype(F32) + ya[z].astype(F32) + ra[0, 7].astype(F32) + ra[1, 6].astype(F32)
    )
    gate, up = pre[:, 0:128], pre[:, 128:256]
    sg = jax.nn.sigmoid(gate)
    hb[z, y] = (gate * sg * up).astype(BF)
    hy_put = put(hb.at[z, y], hb.at[z, y], hy_s, hy_q, ep=py)
    hy_put.start()
    yb_put.wait_recv()
    ag = ag_own + yb[...].astype(F32)
    ha[p, :, 0:128] = (ag * up * sg * (1.0 + gate * (1.0 - sg))).astype(BF)
    ha[p, :, 128:256] = (ag * gate * sg).astype(BF)

    tail.append(hy_put.wait_send)
    def origin(d, k):
        return (z + NZ + (-k if d == 0 else k)) % NZ

    def ga_put(d, k, o):
        return put(
            ha.at[y * NZ + o], ha.at[y * NZ + o], ga_s.at[d, k], ga_q.at[d, k], ep=zr if d == 0 else zl
        )

    def gb_put(d, k, o):
        return put(hb.at[o], hb.at[o], gb_s.at[d, k], gb_q.at[d, k], ep=zr if d == 0 else zl)

    def gy_put(yy, o):
        return put(ha.at[yy * NZ + o], ha.at[yy * NZ + o], gy_s.at[o], gy_q.at[o], ep=py)

    ga_put(0, 0, z).start()
    ga_put(1, 0, z).start()
    gy_put(y, z).start()
    put(hb.at[z, 1 - y], hb.at[z, 1 - y], hy_s, hy_q, ep=py).wait_recv()
    gb_put(0, 0, z).start()
    gb_put(1, 0, z).start()

    def ga_step(d, k, more=True):
        o = origin(d, k)
        ga_put(d, k - 1, o).wait_recv()
        if more:
            ga_put(d, k, o).start()
        gy_put(y, o).start()

    def gb_step(d, k, more=True):
        o = origin(d, k)
        gb_put(d, k - 1, o).wait_recv()
        if more:
            gb_put(d, k, o).start()

    def gather_steps(k):
        ga_step(0, k)
        ga_step(1, k)
        gb_step(0, k)
        gb_step(1, k)

    def gather_sends():
        for d in range(2):
            na, nb = (8, 7) if d == 0 else (7, 8)
            loop(0, na, lambda k: ga_put(d, k, z).wait_send())
            loop(0, nb, lambda k: gb_put(d, k, z).wait_send())
        loop(0, 16, lambda o: gy_put(y, o).wait_send())

    def spread_back(k):
        def two(n):
            yy, m = n // 2, n % 2
            i = 8 * k + 2 * n
            e = er[pl.ds(i, 2)]
            rows = []
            for j in range(2):
                zp = zpair(k, 2 * m + j)
                hq = jnp.concatenate(
                    [
                        ha[pl.ds(yy * NZ + 2 * zp, 2)].reshape(256, 256),
                        hb[pl.ds(2 * zp, 2), yy].reshape(256, 128),
                    ],
                    axis=1,
                )
                rows.append(mm(e[j], hq).astype(BF))
            he[pl.ds(i, 2)] = jnp.stack(rows)

        loop(0, 4, two)

    def gy_wait(k):
        for j in range(4):
            gy_put(1 - y, 2 * zpair(k, j)).wait_recv()
            gy_put(1 - y, 2 * zpair(k, j) + 1).wait_recv()

    def back_dots(k):
        part = pl.ds(8 * k, 8)

        def four(i):
            rows = pl.ds(pl.multiple_of(i * 64, 64), 64)
            hs = he[part, rows, :]
            dn, gu = [], []
            for j in range(4):
                w = wall[host(4 * i + j)]
                hj = hs[:, 16 * j : 16 * j + 16].reshape(128, 384)
                dn.append(mm(hj[:, 256:384], w[:, 256:384], LAST).astype(BF).reshape(8, 16, 128))
                gu.append(mm(hj[:, 0:256], w[:, 0:256], LAST).astype(BF).reshape(8, 16, 128))
            se[part, rows, 0:128] = jnp.concatenate(dn, axis=1)
            se[part, rows, 128:256] = jnp.concatenate(gu, axis=1)

        dots(0, 8, four, 1)

    def squeeze_out(k):
        def two(i):
            r = 8 * k + 2 * i
            t = et[pl.ds(r, 2)]
            parts = se[pl.ds(r, 2), :, 0:256]
            sums = jnp.stack([mm(t[j], parts[j]).astype(BF) for j in range(2)])
            sums = sums.reshape(4, 8, 16, 256)
            m = pl.ds(4 * (i % 2), 4)
            for b in range(8):
                qq[b, k, i // 2, m] = sums[:, b, :, 0:128]
                qq[8 + b, k, i // 2, m] = sums[:, b, :, 128:256]

        dots(0, 4, two, 1)

    def c5(dx, h, k):
        i = 2 * dx + h
        return put(
            qq.at[gi((x + dx) % NX, h, 1 - c), k], rc.at[k, i], c5_s.at[k, i], c5_q.at[k, i], grp=gc
        )

    def core_sends(k):
        for dx in (2, 1, 3, 0):
            for h in range(2):
                c5(dx, h, k).start()

    def weight_dots(i):
        rows = pl.ds(pl.multiple_of(i * 64, 64), 64)
        xd = xe[:, rows, :]
        hs = he[:, rows, :]
        for j in range(4):
            xj = xd[:, 16 * j : 16 * j + 16].reshape(256, 256)
            hj = hs[:, 16 * j : 16 * j + 16].reshape(256, 384)
            tot[4 * i + j, :, 0:256] = mm(xj[:, 0:128], hj[:, 0:256], FIRST)[0:112].astype(BF)
            tot[4 * i + j, :, 256:384] = mm(xj[:, 128:256], hj[:, 256:384], FIRST)[0:112].astype(BF)

    w_out = []

    def weight_group(i):
        dots(2 * i, 2 * i + 2, weight_dots, 1)
        part = pl.ds(8 * i, 8)
        w_out.append(pltpu.make_async_copy(tot.at[part], slots_ref.at[part], o_sem.at[i]))
        w_out[-1].start()

    def addto(t, k, r):
        qq[t, k] = (qq[t, k].astype(F32) + r.astype(F32)).astype(BF)

    def with_core(dx, h, k):
        c5(dx, h, k).wait_recv()
        addto(gi((x + dx) % NX, h, c), k, rc[k, 2 * dx + h])

    def f5(h, k):
        return put(
            qq.at[gi(xf, h, c), k], rfar.at[k, h], f5_s.at[k, h], f5_q.at[k, h], grp=gr if h == 0 else gl
        )

    def x5(d, h, k):
        t = xr if d == 0 else xl
        return put(
            qq.at[gi(t, h, c), k],
            rx.at[k, d, h],
            x5_s.at[k, d, h],
            x5_q.at[k, d, h],
            grp=gr if d == 0 else gl,
        )

    def x_first(k):
        for h in range(2):
            with_core(2, h, k)
            f5(h, k).start()
        with_core(1, 1, k)
        x5(0, 1, k).start()
        with_core(3, 0, k)
        x5(1, 0, k).start()
        with_core(1, 0, k)
        with_core(3, 1, k)

    def x_second(k):
        f5(0, k).wait_recv()
        addto(gi(xr, 0, c), k, rfar[k, 0])
        x5(0, 0, k).start()
        f5(1, k).wait_recv()
        addto(gi(xl, 1, c), k, rfar[k, 1])
        x5(1, 1, k).start()

    def own_sum(h, k):
        return (
            qq[gi(x, h, c), k].astype(F32)
            + rc[k, h].astype(F32)
            + rx[k, 0, h].astype(F32)
            + rx[k, 1, h].astype(F32)
        )

    def y5(k):
        return put(qq.at[gy, k], ry.at[k], y5_s.at[k], y5_q.at[k], grp=gy)

    def y_sends(k):
        for h in range(2):
            c5(0, h, k).wait_recv()
            for d in range(2):
                x5(d, h, k).wait_recv()
        qq[gy, k] = own_sum(1 - yh, k).astype(BF)
        y5(k).start()

    def y_close(k):
        y5(k).wait_recv()
        fin[k] = (own_sum(yh, k) + ry[k].astype(F32)).astype(BF)

    def grp_sends():
        for k in range(2):
            for h in range(2):
                for dx in range(4):
                    c5(dx, h, k).wait_send()
                f5(h, k).wait_send()
                for d in range(2):
                    x5(d, h, k).wait_send()
            y5(k).wait_send()

    def b1(f):
        return put(
            fin.at[place(z, f // NZ, f % NZ)],
            b2r.at[g, p % 2],
            b1_s.at[f],
            b1_q.at[2 * g + p % 2],
            grp=p // 2,
            ep=f,
        )

    def b1_here(f):
        return (p // 2 == g) & (f == p)

    def b1_start(i):
        f = ((i // 8) % 2) * NZ + (2 * zpair(i // 16, 0) + i % 8) % NZ

        @pl.when(jnp.logical_not(b1_here(f)))
        def _():
            b1(f).start()

    early, tail[:] = tail[:], []

    def gather_and_rest(k):
        gather_steps(k)

        @pl.when(k == 2)
        def _():
            for wait in early:
                wait()

    loop(1, 6, gather_and_rest)
    gy_wait(1)
    spread_back(1)
    gather_steps(6)
    back_dots(1)
    ga_step(0, 7)
    ga_step(1, 7, False)
    gb_step(0, 7, False)
    gb_step(1, 7)
    squeeze_out(1)
    core_sends(1)
    ga_step(0, 8, False)
    gb_step(1, 8, False)
    x_first(1)
    gy_wait(0)
    spread_back(0)
    x_second(1)
    back_dots(0)
    squeeze_out(0)
    core_sends(0)
    gather_sends()
    y_sends(1)
    weight_group(0)
    x_first(0)
    y_close(1)
    loop(16, 32, b1_start)

    @pl.when(p // 2 == g)
    def _():
        b2r[g, p % 2] = fin[place(z, y, z)]

    weight_group(1)
    x_second(0)
    weight_group(2)
    y_sends(0)
    weight_group(3)
    y_close(0)
    loop(0, 16, b1_start)

    def b1_wait(i):
        t, h = i // 2, i % 2

        @pl.when(jnp.logical_not((t == g) & (2 * g + h == p)))
        def _():
            put(fin.at[0, 0, 0], b2r.at[t, h], b1_s.at[0], b1_q.at[i], grp=t, ep=2 * g + h).wait_recv()

    def b1_left(f):
        @pl.when(jnp.logical_not(b1_here(f)))
        def _():
            b1(f).wait_send()

    grp_sends()
    loop(0, NEP, b1_left)
    loop(0, NEP, b1_wait)
    rows_out = pltpu.make_async_copy(b2r, rows_ref, o_sem.at[4])
    rows_out.start()
    tail.append(rows_out.wait)
    for grp4 in w_out:
        tail.append(grp4.wait)

    for wait in tail:
        wait()


def finish(
    rows_ref, slots_ref, rw_ref, hot_ref, out_ref, gtok_ref, gg_ref, gu_ref, gd_ref, rows_v, slots_v, acc, sem
):
    rows_in = pltpu.make_async_copy(rows_ref, rows_v, sem.at[0])
    low = pltpu.make_async_copy(slots_ref.at[pl.ds(0, 16)], slots_v.at[pl.ds(0, 16)], sem.at[1])
    high = pltpu.make_async_copy(slots_ref.at[pl.ds(16, 16)], slots_v.at[pl.ds(16, 16)], sem.at[2])
    rows_in.start()
    low.start()
    high.start()

    def base(e, _):
        acc[e] = slots_v[e].astype(F32)
        return 0

    def more(j, _):
        e = hot_ref[j]
        acc[e] = acc[e] + slots_v[16 + j].astype(F32)
        return 0

    def close(e, _):
        v = acc[e].astype(BF)
        gg_ref[e] = v[:, 0:128]
        gu_ref[e] = v[:, 128:256]
        gd_ref[e] = v[:, 256:384]
        return 0

    rows_in.wait()
    for kind, ref in enumerate((out_ref, gtok_ref)):
        for h in range(2):
            part = rows_v[kind * 8 : (kind + 1) * 8, h].reshape(128, 128).astype(F32)
            v = jnp.transpose(part)[0:112]
            if kind == 0:
                v = v * rw_ref[...]
            ref[h * 112 : (h + 1) * 112, :] = v.astype(BF)
    low.wait()
    lax.fori_loop(0, 16, base, 0, unroll=4)
    high.wait()
    lax.fori_loop(0, 16, more, 0, unroll=2)
    lax.fori_loop(0, 16, close, 0, unroll=4)


def layer(tokens, routes, route_weights, hot_experts, w_gate, w_up, w_down, cotangent):
    v = pltpu.VMEM
    dma = pltpu.SemaphoreType.DMA
    vm = pl.BlockSpec(memory_space=pltpu.VMEM)
    anym = pl.BlockSpec(memory_space=pl.ANY)
    sems = [
        (3,), (5,), (16,), (16,), (32,), (32,), (32,), (32,), (2, 15), (2, 15),
        (16,), (16,), (2, 8, 2), (2, 8, 2), (2, 8, 2), (2, 8, 2), None, None,
        None, None, (2, 8), (2, 8), (2, 8), (2, 8), (16,), (16,),
        (2, 8), (2, 8), (2, 2), (2, 2), (2, 2, 2), (2, 2, 2), (2,), (2,), (32,), (32,),
    ]
    rw = route_weights.reshape(1, 128)
    rows, slots = pl.pallas_call(
        body,
        out_shape=(
            jax.ShapeDtypeStruct((16, 2, 16, 128), BF),
            jax.ShapeDtypeStruct((32, 112, 384), BF),
        ),
        in_specs=[vm, vm, vm, pl.BlockSpec(memory_space=pltpu.SMEM), anym, anym, anym, vm],
        out_specs=(anym, anym),
        scratch_shapes=[
            v((16, 2, 16, 128), BF),
            v((32, 16, 128), BF),
            v((16, 2, 16, 128), BF),
            v((16, 2, 2, 8, 16, 128), BF),
            v((16, 512, 256), BF),
            v((16, 256, 512), BF),
            v((16, 128, 384), BF),
            v((16, 512, 256), BF),
            v((16, 512, 384), BF),
            v((32, 128, 256), BF),
            v((16, 2, 128, 128), BF),
            v((16, 128, 256), BF),
            v((2, 8, 128, 256), BF),
            v((2, 8, 2, 128, 128), BF),
            v((128, 128), BF),
            v((32, 128, 256), BF),
            v((16, 2, 128, 128), BF),
            v((16, 512, 384), BF),
            v((16, 2, 2, 8, 16, 128), BF),
            v((2, 8, 2, 8, 16, 128), BF),
            v((2, 2, 2, 8, 16, 128), BF),
            v((2, 2, 2, 2, 8, 16, 128), BF),
            v((2, 2, 8, 16, 128), BF),
            v((2, 2, 8, 16, 128), BF),
            v((16, 2, 16, 128), BF),
            v((32, 112, 384), BF),
        ]
        + [dma if s is None else dma(s) for s in sems],
        compiler_params=pltpu.CompilerParams(
            collective_id=0, has_side_effects=True, vmem_limit_bytes=60 * 1024 * 1024
        ),
        cost_estimate=pl.CostEstimate(flops=8 * 10**9, bytes_accessed=3 * 10**6, transcendentals=0),
    )(
        tokens.T,
        routes.reshape(1, 128),
        rw,
        hot_experts,
        w_gate,
        w_up,
        jnp.swapaxes(w_down, 1, 2),
        cotangent.T,
    )
    grad = jax.ShapeDtypeStruct((16, 112, 128), BF)
    out_t, gtok_t, gg, gu, gd = pl.pallas_call(
        finish,
        out_shape=(
            jax.ShapeDtypeStruct((224, 128), BF),
            jax.ShapeDtypeStruct((224, 128), BF),
            grad,
            grad,
            grad,
        ),
        in_specs=[anym, anym, vm, pl.BlockSpec(memory_space=pltpu.SMEM)],
        out_specs=(vm, vm, vm, vm, vm),
        scratch_shapes=[
            v((16, 2, 16, 128), BF),
            v((32, 112, 384), BF),
            v((16, 112, 384), F32),
            dma((3,)),
        ],
        compiler_params=pltpu.CompilerParams(vmem_limit_bytes=60 * 1024 * 1024),
    )(rows, slots, rw, hot_experts)
    return out_t.T, gtok_t.T, gg, gu, jnp.swapaxes(gd, 1, 2)


def solution(mesh):
    placed = (
        P("ep", "grp"),
        P("ep", None),
        P("ep", None),
        P(),
        P(None, "ep", "grp"),
        P(None, "ep", "grp"),
        P(None, "grp", "ep"),
        P("ep", "grp"),
    )
    return jax.shard_map(
        layer,
        mesh=mesh,
        in_specs=placed,
        out_specs=(
            P("ep", "grp"),
            P("ep", "grp"),
            P(None, "ep", "grp"),
            P(None, "ep", "grp"),
            P(None, "grp", "ep"),
        ),
        check_vma=False,
    )
```
